512 devices in a mesh: row: 32 (over z, x_lo), col: 16 (over y, x_hi, core).
Axes of the slice: x: 4 (x_hi: 2, x_lo: 2; x = x_hi * 2 + x_lo), y: 4, z: 16, core: 2. Of those that a mesh axis runs over, the one named last changes fastest.
Arguments:
- image: bfloat16 [256, 196608], P('row', 'col'), may hold values from -6 to 6
- cotangent: bfloat16 [256, 196608], P('row', 'col'), may hold values from -6 to 6
- qkv_weight: bfloat16 [192, 576], replicated, may hold values from -0.4375 to 0.4375
- qkv_bias: float32 [576], replicated, may hold values from -3 to 3
- proj_weight: bfloat16 [192, 192], replicated, may hold values from -0.4375 to 0.4375
- proj_bias: float32 [192], replicated, may hold values from -3 to 3
- norm_gain: float32 [192], replicated, may hold values from 0.1 to 1.9
- norm_bias: float32 [192], replicated, may hold values from -3 to 3
- bias_table: float32 [6, 225], replicated, may hold values from -4 to 304
Outputs:
- result: bfloat16 [256, 196608], P('row', 'col')
- grad_input: bfloat16 [256, 196608], P('row', 'col')
- grad_qkv_weight: float32 [192, 576], replicated
- grad_qkv_bias: float32 [576], replicated
- grad_proj_weight: float32 [192, 192], replicated
- grad_proj_bias: float32 [192], replicated
- grad_norm_gain: float32 [192], replicated
- grad_norm_bias: float32 [192], replicated
- grad_bias_table: float32 [6, 225], replicated
The draws below stay inside these ranges and needn't reach their ends.
All inputs are finite; a program needn't handle non-finite values.
Results may differ from the reference program's by a relative error of at most 0.019.
Values may be sent and summed in bfloat16 or wider, within the bound.
A program may use at most 64 MiB of HBM per device.

```python
import jax
import jax.numpy as jnp
import numpy as np
from jax import lax

WIDTH = 192
HEADS = 6
HEAD_DIM = 32
WIN = 8
SHIFT = 4
RELS = 225
ROWS = 256
COLS = 1024
TOKENS = 262144


def draw_bias_table(key, part):
    base_key = jax.random.fold_in(key, 0)
    base = jnp.clip(jax.random.normal(base_key, (HEADS, RELS), jnp.float32), -4.0, 4.0)
    return base


def block_scale(rng, shape, cuts, least, high):
    gain = 1.0
    for dim, shards_of in cuts:
        draws = jax.random.uniform(jax.random.fold_in(jax.random.fold_in(rng, 6), dim), (shards_of,), jnp.float32, least / len(cuts), high / len(cuts))
        gain = gain * jnp.repeat(jnp.exp(draws), shape[dim] // shards_of).reshape((-1,) + (1,) * (len(shape) - 1 - dim))
    return gain


def noise(own_key, shape, width, limit, pieces=(), kind=jnp.bfloat16):
    factor_of = block_scale(own_key, shape, pieces, -0.22, 0.18) if pieces else 1.0
    array = jax.random.normal(own_key, shape, jnp.float32) * width * factor_of
    return jnp.minimum(jnp.maximum(array, -limit), limit).astype(kind)


def setup_inputs(seed: int = 0) -> dict:
    key_list = jax.random.split(jax.random.key(seed), 10)
    return {
        "image": noise(key_list[0], (ROWS, COLS * WIDTH), 1.0, 6.0, ((0, 32), (1, 16))),
        "cotangent": noise(key_list[1], (ROWS, COLS * WIDTH), 1.0, 6.0, ((0, 32), (1, 16))),
        "qkv_weight": noise(key_list[2], (WIDTH, 3 * WIDTH), WIDTH ** -0.5, 0.4375),
        "qkv_bias": noise(key_list[3], (3 * WIDTH,), 0.5, 3.0, (), jnp.float32),
        "proj_weight": noise(key_list[4], (WIDTH, WIDTH), WIDTH ** -0.5, 0.4375),
        "proj_bias": noise(key_list[5], (WIDTH,), 0.5, 3.0, (), jnp.float32),
        "norm_gain": jnp.clip(1.0 + 0.18 * jax.random.normal(key_list[6], (WIDTH,), jnp.float32), 0.1, 1.9),
        "norm_bias": noise(key_list[7], (WIDTH,), 0.5, 3.0, (), jnp.float32),
        "bias_table": draw_bias_table(jax.random.fold_in(key_list[9], 71), 0),
    }


EPS = 1e-05
NEG = -1e+30

def product(spec, left, right):
    return jnp.einsum(spec, left.astype(jnp.float32), right.astype(jnp.float32))

def offset_onehot():
    cells = np.arange(WIN * WIN)
    down = cells // WIN
    across = cells % WIN
    offset = (down[:, None] - down[None, :] + WIN - 1) * (2 * WIN - 1) + (across[:, None] - across[None, :] + WIN - 1)
    table = offset.reshape(-1)[:, None] == np.arange(RELS)[None, :]
    return jnp.asarray(table.astype(np.float32))

def to_windows(field, tile_rows, tile_cols):
    feats = field.shape[-1]
    field = field.reshape(tile_rows // WIN, WIN, tile_cols // WIN, WIN, feats)
    return field.transpose(0, 2, 1, 3, 4).reshape(-1, WIN * WIN, feats)

def from_windows(field, tile_rows, tile_cols):
    feats = field.shape[-1]
    field = field.reshape(tile_rows // WIN, tile_cols // WIN, WIN, WIN, feats)
    return field.transpose(0, 2, 1, 3, 4).reshape(tile_rows, tile_cols * feats)

def region(index, total):
    return (index >= total - WIN).astype(jnp.int32) + (index >= total - SHIFT).astype(jnp.int32)

def mask_for(row_start, col_start, tile_rows, tile_cols, total_rows, total_cols):
    grid_rows = row_start + jnp.arange(tile_rows, dtype=jnp.int32)
    grid_cols = col_start + jnp.arange(tile_cols, dtype=jnp.int32)
    label = region(grid_rows, total_rows)[:, None] * 3 + region(grid_cols, total_cols)[None, :]
    label = to_windows(label[:, :, None], tile_rows, tile_cols)[:, :, 0]
    return label[:, :, None] == label[:, None, :]

def forward(tile, params, allowed, tile_rows, tile_cols):
    qkv_weight, qkv_bias, proj_weight, proj_bias, norm_gain, norm_bias, bias_table = params
    tokens = to_windows(tile.reshape(tile_rows, tile_cols, WIDTH), tile_rows, tile_cols).astype(jnp.float32)
    win_count = tokens.shape[0]
    center = tokens - lax.optimization_barrier(jnp.mean(tokens, -1, keepdims=True))
    inv_std = lax.rsqrt(lax.optimization_barrier(jnp.mean(center * center, -1, keepdims=True)) + EPS)
    normed = center * inv_std
    hidden = (normed * norm_gain + norm_bias).astype(jnp.bfloat16)
    packed = (product('wtc,cf->wtf', hidden, qkv_weight) + qkv_bias).astype(jnp.bfloat16)
    query_h = packed[..., :WIDTH].reshape(win_count, WIN * WIN, HEADS, HEAD_DIM)
    key_h = packed[..., WIDTH:2 * WIDTH].reshape(win_count, WIN * WIN, HEADS, HEAD_DIM)
    value_h = packed[..., 2 * WIDTH:].reshape(win_count, WIN * WIN, HEADS, HEAD_DIM)
    rel = jnp.einsum('pr,hr->hp', offset_onehot(), bias_table, precision=lax.Precision.HIGHEST)
    rel = rel.reshape(HEADS, WIN * WIN, WIN * WIN)
    scores = product('wqhd,wkhd->whqk', query_h, key_h) * HEAD_DIM ** (-0.5) + rel[None]
    scores = jnp.where(allowed[:, None], scores, NEG)
    row_max = lax.optimization_barrier(jnp.max(scores, -1, keepdims=True))
    expo = jnp.exp(scores - row_max)
    probs = expo / lax.optimization_barrier(jnp.sum(expo, -1, keepdims=True))
    probs_b = probs.astype(jnp.bfloat16)
    attended = product('whqk,wkhd->wqhd', probs_b, value_h).astype(jnp.bfloat16)
    attended = attended.reshape(win_count, WIN * WIN, WIDTH)
    mixed = product('wtc,cf->wtf', attended, proj_weight) + proj_bias
    out = (tokens + mixed).astype(jnp.bfloat16)
    saved = (normed, inv_std, hidden, query_h, key_h, value_h, probs, probs_b, attended)
    return (from_windows(out, tile_rows, tile_cols), saved)

def backward(cot_tile, saved, params, tile_rows, tile_cols):
    qkv_weight, qkv_bias, proj_weight, proj_bias, norm_gain, norm_bias, bias_table = params
    normed, inv_std, hidden, query_h, key_h, value_h, probs, probs_b, attended = saved
    win_count = normed.shape[0]
    cot_win = to_windows(cot_tile.reshape(tile_rows, tile_cols, WIDTH), tile_rows, tile_cols)
    cot_float = cot_win.astype(jnp.float32)
    grad_proj_w = product('wtc,wtf->cf', attended, cot_win)
    grad_proj_b = lax.optimization_barrier(jnp.sum(cot_float, (0, 1)))
    d_attended = product('wtf,cf->wtc', cot_win, proj_weight).astype(jnp.bfloat16)
    d_attended = d_attended.reshape(win_count, WIN * WIN, HEADS, HEAD_DIM)
    d_probs = product('wqhd,wkhd->whqk', d_attended, value_h)
    d_value = product('whqk,wqhd->wkhd', probs_b, d_attended)
    d_scores = probs * (d_probs - lax.optimization_barrier(jnp.sum(probs * d_probs, -1, keepdims=True)))
    grad_table = jnp.einsum('hp,pr->hr', lax.optimization_barrier(jnp.sum(d_scores, 0)).reshape(HEADS, WIN * WIN * WIN * WIN), offset_onehot(), precision=lax.Precision.HIGHEST)
    d_scores_b = d_scores.astype(jnp.bfloat16)
    scale = HEAD_DIM ** (-0.5)
    d_query = product('whqk,wkhd->wqhd', d_scores_b, key_h) * scale
    d_key = product('whqk,wqhd->wkhd', d_scores_b, query_h) * scale
    shape_out = (win_count, WIN * WIN, WIDTH)
    d_packed = jnp.concatenate([d_query.reshape(shape_out), d_key.reshape(shape_out), d_value.reshape(shape_out)], 2)
    d_packed_b = d_packed.astype(jnp.bfloat16)
    grad_qkv_w = product('wtc,wtf->cf', hidden, d_packed_b)
    grad_qkv_b = lax.optimization_barrier(jnp.sum(d_packed, (0, 1)))
    d_hidden = product('wtf,cf->wtc', d_packed_b, qkv_weight)
    grad_gain = lax.optimization_barrier(jnp.sum(d_hidden * normed, (0, 1)))
    grad_shift = lax.optimization_barrier(jnp.sum(d_hidden, (0, 1)))
    d_normed = d_hidden * norm_gain
    d_tokens = cot_float + inv_std * (d_normed - lax.optimization_barrier(jnp.mean(d_normed, -1, keepdims=True)) - normed * lax.optimization_barrier(jnp.mean(d_normed * normed, -1, keepdims=True)))
    back = from_windows(d_tokens.astype(jnp.bfloat16), tile_rows, tile_cols)
    return (back, (grad_qkv_w, grad_qkv_b, grad_proj_w, grad_proj_b, grad_gain, grad_shift, grad_table))

def reference(image, cotangent, qkv_weight, qkv_bias, proj_weight, proj_bias, norm_gain, norm_bias, bias_table):
    params = (qkv_weight, qkv_bias, proj_weight, proj_bias, norm_gain, norm_bias, bias_table)
    rolled = jnp.roll(image.reshape(ROWS, COLS, WIDTH), (-SHIFT, -SHIFT), (0, 1))
    rolled_cot = jnp.roll(cotangent.reshape(ROWS, COLS, WIDTH), (-SHIFT, -SHIFT), (0, 1))
    strips = rolled.reshape(ROWS // WIN, WIN, COLS * WIDTH)
    strips_cot = rolled_cot.reshape(ROWS // WIN, WIN, COLS * WIDTH)

    def one_strip(items):
        strip, strip_cot, index = items
        allowed = mask_for(index * WIN, jnp.int32(0), WIN, COLS, ROWS, COLS)
        out, saved = forward(strip, params, allowed, WIN, COLS)
        back, grads = backward(strip_cot, saved, params, WIN, COLS)
        return (out, back, grads)
    outs, backs, grads = lax.map(one_strip, (strips, strips_cot, jnp.arange(ROWS // WIN, dtype=jnp.int32)))
    factor = float(TOKENS) ** (-0.5)
    grads = [lax.optimization_barrier(jnp.sum(piece, 0)) * factor for piece in grads]
    result = jnp.roll(outs.reshape(ROWS, COLS, WIDTH), (SHIFT, SHIFT), (0, 1)).reshape(ROWS, COLS * WIDTH)
    grad_input = jnp.roll(backs.reshape(ROWS, COLS, WIDTH), (SHIFT, SHIFT), (0, 1)).reshape(ROWS, COLS * WIDTH)
    return (result, grad_input, grads[0], grads[1], grads[2], grads[3], grads[4], grads[5], grads[6])
```

```python
import functools

import jax
import jax.numpy as jnp
import numpy as np
from jax import lax
from jax.experimental import pallas as pl
from jax.experimental.pallas import tpu as pltpu
from jax.sharding import PartitionSpec as P

WIDTH = 192
HEADS = 6
HEAD_DIM = 32
WIN = 8
SHIFT = 4
RELS = 225

MESH = pl.DeviceIdType.MESH
ROW_AXIS, COL_AXIS = "row", "col"
EPS = 1e-05
NEG = -1e30


def passed_along(value, axis, steps):
    count = lax.axis_size(axis)
    pairs = [(source, (source + steps) % count) for source in range(count)]
    return lax.ppermute(value, axis, pairs)


def product(spec, left, right):
    return jnp.einsum(spec, left, right, preferred_element_type=jnp.float32)


def offset_onehot():
    cells = np.arange(WIN * WIN)
    down = cells // WIN
    across = cells % WIN
    offset = (down[:, None] - down[None, :] + WIN - 1) * (2 * WIN - 1) + (
        across[:, None] - across[None, :] + WIN - 1
    )
    table = offset.reshape(-1)[:, None] == np.arange(RELS)[None, :]
    return jnp.asarray(table.astype(np.float32))


def to_windows(field, tile_rows, tile_cols):
    feats = field.shape[-1]
    field = field.reshape(tile_rows // WIN, WIN, tile_cols // WIN, WIN, feats)
    return field.transpose(0, 2, 1, 3, 4).reshape(-1, WIN * WIN, feats)


def from_windows(field, tile_rows, tile_cols):
    feats = field.shape[-1]
    field = field.reshape(tile_rows // WIN, tile_cols // WIN, WIN, WIN, feats)
    return field.transpose(0, 2, 1, 3, 4).reshape(tile_rows, tile_cols * feats)


def region(index, total):
    return (index >= total - WIN).astype(jnp.int32) + (index >= total - SHIFT).astype(jnp.int32)


def mask_for(row_start, col_start, tile_rows, tile_cols, total_rows, total_cols):
    grid_rows = row_start + jnp.arange(tile_rows, dtype=jnp.int32)
    grid_cols = col_start + jnp.arange(tile_cols, dtype=jnp.int32)
    label = region(grid_rows, total_rows)[:, None] * 3 + region(grid_cols, total_cols)[None, :]
    label = to_windows(label[:, :, None], tile_rows, tile_cols)[:, :, 0]
    return label[:, :, None] == label[:, None, :]


def roll_lead(stacked):
    arrived = passed_along(stacked[:, :SHIFT], "row", -1)
    stacked = jnp.concatenate([stacked[:, SHIFT:], arrived], 1)
    edge = SHIFT * WIDTH
    arrived = passed_along(stacked[:, :, :edge], "col", -1)
    return jnp.concatenate([stacked[:, :, edge:], arrived], 2)


def roll_trail(stacked):
    arrived = passed_along(stacked[:, -SHIFT:], "row", 1)
    stacked = jnp.concatenate([arrived, stacked[:, :-SHIFT]], 1)
    edge = SHIFT * WIDTH
    arrived = passed_along(stacked[:, :, -edge:], "col", 1)
    return jnp.concatenate([arrived, stacked[:, :, :-edge]], 2)


def forward(tile, params, allowed, tile_rows, tile_cols):
    qkv_weight, qkv_bias, proj_weight, proj_bias, norm_gain, norm_bias, bias_table = params
    tokens = to_windows(tile.reshape(tile_rows, tile_cols, WIDTH), tile_rows, tile_cols).astype(
        jnp.float32
    )
    win_count = tokens.shape[0]
    center = tokens - jnp.mean(tokens, -1, keepdims=True)
    inv_std = lax.rsqrt(jnp.mean(center * center, -1, keepdims=True) + EPS)
    normed = center * inv_std
    hidden = (normed * norm_gain + norm_bias).astype(jnp.bfloat16)
    packed = (product("wtc,cf->wtf", hidden, qkv_weight) + qkv_bias).astype(jnp.bfloat16)
    query_h = packed[..., :WIDTH].reshape(win_count, WIN * WIN, HEADS, HEAD_DIM)
    key_h = packed[..., WIDTH : 2 * WIDTH].reshape(win_count, WIN * WIN, HEADS, HEAD_DIM)
    value_h = packed[..., 2 * WIDTH :].reshape(win_count, WIN * WIN, HEADS, HEAD_DIM)
    rel = jnp.einsum("pr,hr->hp", offset_onehot(), bias_table, precision=lax.Precision.HIGHEST)
    rel = rel.reshape(HEADS, WIN * WIN, WIN * WIN)
    scores = product("wqhd,wkhd->whqk", query_h, key_h) * HEAD_DIM ** (-0.5) + rel[None]
    scores = jnp.where(allowed[:, None], scores, NEG)
    row_max = jnp.max(scores, -1, keepdims=True)
    expo = jnp.exp(scores - row_max)
    probs = expo / jnp.sum(expo, -1, keepdims=True)
    probs_b = probs.astype(jnp.bfloat16)
    attended = product("whqk,wkhd->wqhd", probs_b, value_h).astype(jnp.bfloat16)
    attended = attended.reshape(win_count, WIN * WIN, WIDTH)
    mixed = product("wtc,cf->wtf", attended, proj_weight) + proj_bias
    out = (tokens + mixed).astype(jnp.bfloat16)
    saved = (normed, inv_std, hidden, query_h, key_h, value_h, probs, probs_b, attended)
    return (from_windows(out, tile_rows, tile_cols), saved)


def backward(cot_tile, saved, params, tile_rows, tile_cols):
    qkv_weight, qkv_bias, proj_weight, proj_bias, norm_gain, norm_bias, bias_table = params
    normed, inv_std, hidden, query_h, key_h, value_h, probs, probs_b, attended = saved
    win_count = normed.shape[0]
    cot_win = to_windows(cot_tile.reshape(tile_rows, tile_cols, WIDTH), tile_rows, tile_cols)
    cot_float = cot_win.astype(jnp.float32)
    grad_proj_w = product("wtc,wtf->cf", attended, cot_win)
    grad_proj_b = jnp.sum(cot_float, (0, 1))
    d_attended = product("wtf,cf->wtc", cot_win, proj_weight).astype(jnp.bfloat16)
    d_attended = d_attended.reshape(win_count, WIN * WIN, HEADS, HEAD_DIM)
    d_probs = product("wqhd,wkhd->whqk", d_attended, value_h)
    d_value = product("whqk,wqhd->wkhd", probs_b, d_attended)
    d_scores = probs * (d_probs - jnp.sum(probs * d_probs, -1, keepdims=True))
    grad_table = jnp.einsum(
        "hp,pr->hr",
        jnp.sum(d_scores, 0).reshape(HEADS, WIN * WIN * WIN * WIN),
        offset_onehot(),
        precision=lax.Precision.HIGHEST,
    )
    d_scores_b = d_scores.astype(jnp.bfloat16)
    scale = HEAD_DIM ** (-0.5)
    d_query = product("whqk,wkhd->wqhd", d_scores_b, key_h) * scale
    d_key = product("whqk,wqhd->wkhd", d_scores_b, query_h) * scale
    shape_out = (win_count, WIN * WIN, WIDTH)
    d_packed = jnp.concatenate(
        [d_query.reshape(shape_out), d_key.reshape(shape_out), d_value.reshape(shape_out)], 2
    )
    d_packed_b = d_packed.astype(jnp.bfloat16)
    grad_qkv_w = product("wtc,wtf->cf", hidden, d_packed_b)
    grad_qkv_b = jnp.sum(d_packed, (0, 1))
    d_hidden = product("wtf,cf->wtc", d_packed_b, qkv_weight)
    grad_gain = jnp.sum(d_hidden * normed, (0, 1))
    grad_shift = jnp.sum(d_hidden, (0, 1))
    d_normed = d_hidden * norm_gain
    d_tokens = cot_float + inv_std * (
        d_normed
        - jnp.mean(d_normed, -1, keepdims=True)
        - normed * jnp.mean(d_normed * normed, -1, keepdims=True)
    )
    back = from_windows(d_tokens.astype(jnp.bfloat16), tile_rows, tile_cols)
    return (
        back,
        (grad_qkv_w, grad_qkv_b, grad_proj_w, grad_proj_b, grad_gain, grad_shift, grad_table),
    )


def reduce_kernel(n_row, n_col, tiles, per, scale, g_ref, o_ref, sbuf, rbuf, s2, r2, g2, fbuf,
                  ss1, rs1, ss2, rs2, ss3, rs3, ss4, rs4):
    my_r, my_c = lax.axis_index(ROW_AXIS), lax.axis_index(COL_AXIS)
    lane_tiles = g_ref.shape[1] // 128
    barrier = pltpu.get_barrier_semaphore()

    def greet_col(k, _):
        peer = lax.rem(my_c + k, n_col)
        pl.semaphore_signal(barrier, inc=1, device_id=(my_r, peer), device_id_type=MESH)
        return 0

    def greet_row(k, _):
        peer = lax.rem(my_r + k, n_row)
        pl.semaphore_signal(barrier, inc=1, device_id=(peer, my_c), device_id_type=MESH)
        return 0

    lax.fori_loop(1, n_col, greet_col, 0)
    lax.fori_loop(1, n_row, greet_row, 0)

    for t in range(n_col * per):
        if t < tiles:
            rt, lt = t // lane_tiles, t % lane_tiles
            tile = g_ref[rt * 16 : rt * 16 + 16, lt * 128 : lt * 128 + 128].astype(jnp.bfloat16)
        else:
            tile = jnp.zeros((16, 128), jnp.bfloat16)
        sbuf[t // per, (t % per) * 16 : (t % per) * 16 + 16, :] = tile
    pl.semaphore_wait(barrier, n_col - 1 + n_row - 1)

    def scatter(peer, slot):
        return pltpu.make_async_remote_copy(
            src_ref=sbuf.at[peer], dst_ref=rbuf.at[slot], send_sem=ss1.at[peer],
            recv_sem=rs1.at[slot], device_id=(my_r, peer), device_id_type=MESH)

    def send1(k, _):
        peer = lax.rem(my_c + k, n_col)
        scatter(peer, my_c).start()
        return 0

    lax.fori_loop(1, n_col, send1, 0)
    rbuf[my_c] = sbuf[my_c]

    def recv1(k, _):
        peer = lax.rem(my_c + k, n_col)
        scatter(peer, peer).wait_recv()
        return 0

    lax.fori_loop(1, n_col, recv1, 0)
    acc = rbuf[0].astype(jnp.float32)
    for j in range(1, n_col):
        acc = acc + rbuf[j].astype(jnp.float32)
    acc = acc.astype(jnp.bfloat16)
    for i in range(per):
        s2[i] = acc[i * 16 : i * 16 + 16]

    gap = n_row // per

    def owner(i):
        return lax.rem(i * gap + 2 * my_c, n_row)

    def up(i):
        return pltpu.make_async_remote_copy(
            src_ref=s2.at[i], dst_ref=r2.at[my_r], send_sem=ss2.at[i],
            recv_sem=rs2.at[my_r], device_id=(owner(i), my_c), device_id_type=MESH)

    def up_from(peer):
        return pltpu.make_async_remote_copy(
            src_ref=s2.at[0], dst_ref=r2.at[peer], send_sem=ss2.at[0],
            recv_sem=rs2.at[peer], device_id=(peer, my_c), device_id_type=MESH)

    def down(i, peer):
        return pltpu.make_async_remote_copy(
            src_ref=g2.at[i], dst_ref=g2.at[i], send_sem=ss3.at[peer],
            recv_sem=rs3.at[i], device_id=(peer, my_c), device_id_type=MESH)

    for i in range(per):
        @pl.when(owner(i) != my_r)
        def _():
            up(i).start()

    for i in range(per):
        @pl.when(owner(i) == my_r)
        def _():
            r2[my_r] = s2[i]

            def recv2(k, _):
                up_from(lax.rem(my_r + k, n_row)).wait_recv()
                return 0

            lax.fori_loop(1, n_row, recv2, 0)
            total = r2[0].astype(jnp.float32)
            for j in range(1, n_row):
                total = total + r2[j].astype(jnp.float32)
            g2[i] = total.astype(jnp.bfloat16)

            def send3(k, _):
                down(i, lax.rem(my_r + k, n_row)).start()
                return 0

            lax.fori_loop(1, n_row, send3, 0)

    for i in range(per):
        @pl.when(owner(i) != my_r)
        def _():
            down(i, my_r).wait_recv()

    def gather(peer, slot):
        return pltpu.make_async_remote_copy(
            src_ref=g2, dst_ref=fbuf.at[slot], send_sem=ss4.at[peer],
            recv_sem=rs4.at[slot], device_id=(my_r, peer), device_id_type=MESH)

    def send4(k, _):
        gather(lax.rem(my_c + k, n_col), my_c).start()
        return 0

    lax.fori_loop(1, n_col, send4, 0)
    fbuf[my_c] = g2[...]

    def recv4(k, _):
        peer = lax.rem(my_c + k, n_col)
        gather(peer, peer).wait_recv()
        return 0

    lax.fori_loop(1, n_col, recv4, 0)
    for t in range(tiles):
        rt, lt = t // lane_tiles, t % lane_tiles
        o_ref[rt * 16 : rt * 16 + 16, lt * 128 : lt * 128 + 128] = (
            fbuf[t // per, t % per].astype(jnp.float32) * scale)

    def drain1(k, _):
        peer = lax.rem(my_c + k, n_col)
        scatter(peer, peer).wait_send()
        gather(peer, peer).wait_send()
        return 0

    lax.fori_loop(1, n_col, drain1, 0)
    for i in range(per):
        @pl.when(owner(i) != my_r)
        def _():
            up(i).wait_send()

        @pl.when(owner(i) == my_r)
        def _():
            def drain3(k, _):
                down(i, lax.rem(my_r + k, n_row)).wait_send()
                return 0

            lax.fori_loop(1, n_row, drain3, 0)


def all_reduce(g, n_row, n_col, scale):
    tiles = (g.shape[0] // 16) * (g.shape[1] // 128)
    per = -(-tiles // n_col)
    return pl.pallas_call(
        functools.partial(reduce_kernel, n_row, n_col, tiles, per, scale),
        out_shape=jax.ShapeDtypeStruct(g.shape, jnp.float32),
        in_specs=[pl.BlockSpec(memory_space=pltpu.VMEM)],
        out_specs=pl.BlockSpec(memory_space=pltpu.VMEM),
        scratch_shapes=[
            pltpu.VMEM((n_col, per * 16, 128), jnp.bfloat16),
            pltpu.VMEM((n_col, per * 16, 128), jnp.bfloat16),
            pltpu.VMEM((per, 16, 128), jnp.bfloat16),
            pltpu.VMEM((n_row, 16, 128), jnp.bfloat16),
            pltpu.VMEM((per, 16, 128), jnp.bfloat16),
            pltpu.VMEM((n_col, per, 16, 128), jnp.bfloat16),
            pltpu.SemaphoreType.DMA((n_col,)),
            pltpu.SemaphoreType.DMA((n_col,)),
            pltpu.SemaphoreType.DMA((per,)),
            pltpu.SemaphoreType.DMA((n_row,)),
            pltpu.SemaphoreType.DMA((n_row,)),
            pltpu.SemaphoreType.DMA((per,)),
            pltpu.SemaphoreType.DMA((n_col,)),
            pltpu.SemaphoreType.DMA((n_col,)),
        ],
        compiler_params=pltpu.CompilerParams(collective_id=1, has_side_effects=True,
                                             vmem_limit_bytes=16 * 1024 * 1024),
    )(g)


def shards(
    image, cotangent, qkv_weight, qkv_bias, proj_weight, proj_bias, norm_gain, norm_bias, bias_table
):
    params = (qkv_weight, qkv_bias, proj_weight, proj_bias, norm_gain, norm_bias, bias_table)
    tile_rows = image.shape[0]
    tile_cols = image.shape[1] // WIDTH
    total_rows = tile_rows * lax.axis_size("row")
    total_cols = tile_cols * lax.axis_size("col")
    allowed = mask_for(
        lax.axis_index("row") * tile_rows,
        lax.axis_index("col") * tile_cols,
        tile_rows,
        tile_cols,
        total_rows,
        total_cols,
    )
    moved_image = roll_lead(image[None])[0]
    out_tile, saved = forward(moved_image, params, allowed, tile_rows, tile_cols)
    result = roll_trail(out_tile[None])[0]
    moved_cot = roll_lead(cotangent[None])[0]
    back_tile, grads = backward(moved_cot, saved, params, tile_rows, tile_cols)
    grad_input = roll_trail(back_tile[None])[0]
    grad_qkv_w, grad_qkv_b, grad_proj_w, grad_proj_b, grad_gain, grad_shift, grad_table = grads
    wide = jnp.concatenate([grad_qkv_w, grad_proj_w], 1)
    first = jnp.concatenate([grad_qkv_b, grad_proj_b])[None]
    second = jnp.pad(jnp.concatenate([grad_gain, grad_shift])[None], ((0, 0), (0, 384)))
    table = jnp.pad(grad_table, ((0, 8), (0, 768 - RELS)))
    packed = jnp.concatenate([wide, first, second, table], 0)
    total = all_reduce(
        packed,
        lax.axis_size("row"),
        lax.axis_size("col"),
        float(total_rows * total_cols) ** (-0.5),
    )
    pieces = [
        total[:WIDTH, : 3 * WIDTH],
        total[WIDTH, : 3 * WIDTH],
        total[:WIDTH, 3 * WIDTH :],
        total[WIDTH, 3 * WIDTH :],
        total[WIDTH + 1, :WIDTH],
        total[WIDTH + 1, WIDTH : 2 * WIDTH],
        total[WIDTH + 2 : WIDTH + 2 + HEADS, :RELS],
    ]
    return (
        result,
        grad_input,
        pieces[0],
        pieces[1],
        pieces[2],
        pieces[3],
        pieces[4],
        pieces[5],
        pieces[6],
    )


def solution(mesh):
    in_specs = (P("row", "col"), P("row", "col"), P(), P(), P(), P(), P(), P(), P())
    out_specs = (P("row", "col"), P("row", "col"), P(), P(), P(), P(), P(), P(), P())
    return jax.shard_map(shards, mesh=mesh, in_specs=in_specs, out_specs=out_specs, check_vma=False)
```

```python
import functools

import jax
import jax.numpy as jnp
from jax import lax
from jax.experimental import pallas as pl
from jax.experimental.pallas import tpu as pltpu
from jax.sharding import PartitionSpec as P

WIDTH = 192
HEADS = 6
HEAD_DIM = 32
WIN = 8
CELLS = WIN * WIN
SHIFT = 4
RELS = 225
EPS = 1e-05
NEG = -1e30
TILE_COLS = 64
LANES = TILE_COLS * WIDTH
HALF = LANES // 2
EDGE = SHIFT * WIDTH
WINDOWS = TILE_COLS // WIN
SPAN = WIN * WIDTH
TOKENS_HERE = WINDOWS * CELLS
SCALE = HEAD_DIM**-0.5
GROUPS = ((0, 4), (4, 2))
TILES = 78
UNROLL = 2

MESH = pl.DeviceIdType.MESH
F32 = jnp.float32
BF16 = jnp.bfloat16


def dot(a, b, ca=1, cb=0):
    return lax.dot_general(a, b, (((ca,), (cb,)), ((), ())), preferred_element_type=F32)


def iota(shape, dim):
    return lax.broadcasted_iota(jnp.int32, shape, dim)


def upper(shape):
    return iota(shape, 0) < SHIFT


def pack_rows(field):
    back = pltpu.roll(field[:, HALF:], SHIFT, 0)
    return jnp.where(upper((WIN, HALF)), field[:, :HALF], back)


def merge_rows(packed, field):
    low = jnp.where(upper((WIN, HALF)), packed, field[:, :HALF])
    high = jnp.where(upper((WIN, HALF)), pltpu.roll(packed, SHIFT, 0), field[:, HALF:])
    return low, high


def split_tokens(strip):
    left = iota((WIN, 128), 1) < 64
    first, second = [], []
    for j in range(WIN // 2):
        v = [strip[:, (3 * j + i) * 128 : (3 * j + i + 1) * 128] for i in range(3)]
        r1, r2 = pltpu.roll(v[1], 64, 1), pltpu.roll(v[2], 64, 1)
        first += [v[0], jnp.where(left, r1, r2)]
        second += [v[1], r2]
    return jnp.concatenate(first, 0), jnp.concatenate(second, 0)


def join_tokens(first, second):
    left = iota((WIN, 128), 1) < 64
    out = []
    for j in range(WIN // 2):
        e = slice(16 * j, 16 * j + 8)
        o = slice(16 * j + 8, 16 * j + 16)
        swapped = pltpu.roll(first[o], 64, 1)
        out.append(first[e])
        out.append(jnp.where(left, second[e], swapped))
        out.append(jnp.where(left, swapped, pltpu.roll(second[o], 64, 1)))
    return jnp.concatenate(out, 1)


def build_bias(table_ref, onehot, padded, diag, bias, last_row, last_col):
    padded[...] = jnp.zeros((8, 256), F32)
    padded[0:HEADS, 0:RELS] = table_ref[...]
    table = padded[...]
    hi = table.astype(BF16)
    rest = table - hi.astype(F32)
    mid = rest.astype(BF16)
    low = (rest - mid.astype(F32)).astype(BF16)
    lane = iota((1, 128), 1)
    a_q = (lane + SHIFT) % WIN
    for a in range(WIN):
        target = (a_q - (a + SHIFT) % WIN + WIN - 1) * (2 * WIN - 1) + lane // WIN
        target = jnp.where(lane < 120, target, -1)
        hot = jnp.where(iota((256, 128), 0) == target, 1.0, 0.0).astype(BF16)
        onehot[a] = hot
        rows = dot(hi, hot) + dot(mid, hot) + dot(low, hot)
        for h in range(HEADS):
            diag[h, a : a + 1, :] = rows[h : h + 1, :]
    sub = iota((WIN, 128), 0)
    lanes = iota((WIN, 128), 1)
    row_cut = jnp.where((sub < SHIFT) != (lanes % WIN < SHIFT), NEG, 0.0) * last_row
    right = lanes % 64 // WIN >= SHIFT
    for b in range(WIN):
        col_cut = jnp.where(right != (b >= SHIFT), NEG, 0.0) * last_col
        for pair in range(HEADS // 2):
            shift = (WIN - 1 - b) * WIN
            even = pltpu.roll(diag[2 * pair], (128 - shift) % 128, 1)
            odd = pltpu.roll(diag[2 * pair + 1], (192 - shift) % 128, 1)
            block = jnp.where(lanes < 64, even, odd) + row_cut
            where = (slice(b * WIN, b * WIN + WIN), slice(pair * 128, pair * 128 + 128))
            bias[(0,) + where] = block
            bias[(1,) + where] = block + col_cut


def table_grad(total, onehot, diag):
    lanes = iota((WIN, 128), 1)
    for h in range(HEADS):
        mine = (lanes < 64) == (h % 2 == 0)
        acc = jnp.zeros((WIN, 128), F32)
        for b in range(WIN):
            block = total[b * WIN : b * WIN + WIN, h // 2 * 128 : h // 2 * 128 + 128]
            block = jnp.where(mine, block, 0.0)
            acc = acc + pltpu.roll(block, ((WIN - 1 - b) * WIN + h % 2 * 64) % 128, 1)
        diag[h] = acc
    flat = jnp.concatenate([diag[h] for h in range(HEADS)], 0)
    hi = flat.astype(BF16)
    low = (flat - hi.astype(F32)).astype(BF16)
    sub = iota((HEADS * WIN, 256), 0) % WIN
    acc = jnp.zeros((HEADS * WIN, 256), F32)
    for a in range(WIN):
        part = dot(hi, onehot[a], 1, 1) + dot(low, onehot[a], 1, 1)
        acc = acc + jnp.where(sub == a, part, 0.0)
    return [
        jnp.sum(acc[h * WIN : h * WIN + WIN], 0, keepdims=True) for h in range(HEADS)
    ]


def masked_heads(x, group):
    start, count = group
    lane = iota((CELLS, count * HEAD_DIM), 1) // HEAD_DIM
    wide = x[:, start * HEAD_DIM : (start + count) * HEAD_DIM]
    zero = jnp.zeros_like(wide)
    return jnp.concatenate([jnp.where(lane == h, wide, zero) for h in range(count)], 0)


def own_heads(x, count):
    lane = iota((CELLS, count * HEAD_DIM), 1) // HEAD_DIM
    out = x[(count - 1) * CELLS : count * CELLS]
    for h in range(count - 1):
        out = jnp.where(lane == h, x[h * CELLS : (h + 1) * CELLS], out)
    return out


def window_step(w, qs, ks, vs, das, bias, att, dq, dk, dv, gsum, last):
    rows = pl.ds(pl.multiple_of(w * CELLS, CELLS), CELLS)
    q, k, v, da = qs[rows, :], ks[rows, :], vs[rows, :], das[rows, :]
    for start, count in GROUPS:
        ch = slice(start * HEAD_DIM, (start + count) * HEAD_DIM)
        lanes = slice(start * CELLS, (start + count) * CELLS)
        qm = masked_heads(q, (start, count))
        dam = masked_heads(da, (start, count))
        s = dot(k[:, ch], qm, 1, 1) * SCALE + bias[last, :, lanes]
        e = jnp.exp(s - jnp.max(s, 0, keepdims=True))
        p = e * (1.0 / jnp.sum(e, 0, keepdims=True))
        dp = dot(v[:, ch], dam, 1, 1)
        ds = p * (dp - jnp.sum(p * dp, 0, keepdims=True))
        gsum[:, lanes] += ds
        pb, dsb = p.astype(BF16), ds.astype(BF16)
        dv[rows, ch] = dot(pb, dam)
        dk[rows, ch] = dot(dsb, qm) * SCALE
        att[rows, ch] = own_heads(dot(pb, v[:, ch], 0, 0), count).astype(BF16)
        dq[rows, ch] = own_heads(dot(dsb, k[:, ch], 0, 0), count) * SCALE


def block_kernel(n_row, n_col, per, grad_scale, *refs):
    (img, cot, wqkv, bqkv, wproj, bproj, gain_ref, shift_ref, table_ref,
     res, gin, g_qkv_w, g_qkv_b, g_proj_w, g_proj_b, g_gain, g_shift, g_table,
     irow, icol, hrow, hcol, hdiag, orow, ocol, rrow, rcol, rdiag,
     field, cfield, xs, cs, norm, hid, qs, ks, vs, das, att, dq, dk, dv, gsum,
     bias, onehot, padded, diag, gs, sbuf, rbuf, s2, r2, g2, fbuf,
     hs, hr, ss1, rs1, ss2, rs2, ss3, rs3, ss4, rs4) = refs
    my_r, my_c = lax.axis_index("row"), lax.axis_index("col")
    above, below = lax.rem(my_r + n_row - 1, n_row), lax.rem(my_r + 1, n_row)
    left, right = lax.rem(my_c + n_col - 1, n_col), lax.rem(my_c + 1, n_col)
    barrier = pltpu.get_barrier_semaphore()

    def greet(r, c):
        pl.semaphore_signal(barrier, inc=1, device_id=(r, c), device_id_type=MESH)

    greet(above, left)
    greet(below, right)

    def greet_col(k, _):
        greet(my_r, lax.rem(my_c + k, n_col))
        return 0

    def greet_row(k, _):
        greet(lax.rem(my_r + k, n_row), my_c)
        return 0

    lax.fori_loop(1, n_row, greet_row, 0)
    lax.fori_loop(1, n_col, greet_col, 0)

    def remote(src, dst, i, r, c):
        return pltpu.make_async_remote_copy(
            src_ref=src, dst_ref=dst, send_sem=hs.at[i], recv_sem=hr.at[i],
            device_id=(r, c), device_id_type=MESH)

    lead = (remote(irow, hrow, 0, above, my_c), remote(icol, hcol, 1, my_r, left),
            remote(icol, hdiag, 2, above, left))
    trail = (remote(orow, rrow, 3, below, my_c), remote(ocol, rcol, 4, my_r, right),
             remote(ocol, rdiag, 5, below, right))

    for i, src in enumerate((img, cot)):
        half = slice(i * WIN, i * WIN + WIN)
        tile = src[...].astype(F32)
        irow[half, :] = pack_rows(tile).astype(BF16)
        icol[half, :] = tile[:, :EDGE].astype(BF16)
    pl.semaphore_wait(barrier, n_row - 1 + n_col - 1 + 2)
    for copy in lead:
        copy.start()

    last_row = (my_r == n_row - 1).astype(F32)
    last_col = (my_c == n_col - 1).astype(F32)
    build_bias(table_ref, onehot, padded, diag, bias, last_row, last_col)
    gsum[...] = jnp.zeros_like(gsum)
    gs[WIDTH:, :] = jnp.zeros((16, 4 * WIDTH), F32)
    weights = [wqkv[:, i * WIDTH : (i + 1) * WIDTH] for i in range(3)]
    biases = [bqkv[:, i * WIDTH : (i + 1) * WIDTH] for i in range(3)]

    for copy in lead:
        copy.wait_recv()
    for i, (src, dst) in enumerate(((img, field), (cot, cfield))):
        half = slice(i * WIN, i * WIN + WIN)
        low, high = merge_rows(hrow[half, :].astype(F32), src[...].astype(F32))
        dst[:, :HALF] = low
        dst[:, HALF:LANES] = high
        dst[:, LANES:] = jnp.where(
            upper((WIN, EDGE)), hdiag[half, :].astype(F32), hcol[half, :].astype(F32))

    def tokens_of(w, _):
        lanes = pl.ds(pl.multiple_of(EDGE + w * SPAN, 128), SPAN)
        rows = pl.ds(pl.multiple_of(w * CELLS, CELLS), CELLS)
        for src, dst in ((field, xs), (cfield, cs)):
            first, second = split_tokens(src[:, lanes])
            dst[rows, 0:128] = first
            dst[rows, 128:WIDTH] = second[:, : WIDTH - 128]
        return 0

    lax.fori_loop(0, WINDOWS, tokens_of, 0)
    x = xs[...]
    center = x - jnp.mean(x, 1, keepdims=True)
    inv_std = lax.rsqrt(jnp.mean(center * center, 1, keepdims=True) + EPS)
    normed = center * inv_std
    norm[...] = normed
    gain = gain_ref[...]
    hidden = (normed * gain + shift_ref[...]).astype(BF16)
    hid[...] = hidden
    for dst, weight, add in zip((qs, ks, vs), weights, biases):
        dst[...] = (dot(hidden, weight) + add).astype(BF16)
    cot_b = cs[...].astype(BF16)
    das[...] = dot(cot_b, wproj[...], 1, 1).astype(BF16)

    def windows(i, _):
        for u in range(UNROLL):
            w = i * UNROLL + u
            last = (w == WINDOWS - 1).astype(jnp.int32)
            window_step(w, qs, ks, vs, das, bias, att, dq, dk, dv, gsum, last)
        return 0

    lax.fori_loop(0, WINDOWS // UNROLL, windows, 0)

    d_hidden = jnp.zeros((TOKENS_HERE, WIDTH), F32)
    hidden_t = hid[...].T
    for i, (part, weight) in enumerate(zip((dq, dk, dv), weights)):
        part_f = part[...]
        part_b = part_f.astype(BF16)
        lanes = slice(i * WIDTH, (i + 1) * WIDTH)
        gs[WIDTH : WIDTH + 1, lanes] = jnp.sum(part_f, 0, keepdims=True)
        gs[0:WIDTH, lanes] = dot(hidden_t, part_b)
        d_hidden = d_hidden + dot(part_b, weight, 1, 1)
    cot_b = cs[...].astype(BF16)
    gs[0:WIDTH, 3 * WIDTH :] = dot(att[...], cot_b, 0, 0)
    gs[WIDTH : WIDTH + 1, 3 * WIDTH :] = jnp.sum(cs[...], 0, keepdims=True)
    normed = norm[...]
    gs[WIDTH + 1 : WIDTH + 2, 0:WIDTH] = jnp.sum(d_hidden * normed, 0, keepdims=True)
    gs[WIDTH + 1 : WIDTH + 2, WIDTH : 2 * WIDTH] = jnp.sum(d_hidden, 0, keepdims=True)
    for h, line in enumerate(table_grad(gsum[...], onehot, diag)):
        gs[WIDTH + 2 + h : WIDTH + 3 + h, 0:256] = line

    for t in range(n_col * per):
        if t < TILES:
            rt, lt = t // 6, t % 6
            tile = gs[rt * 16 : rt * 16 + 16, lt * 128 : lt * 128 + 128].astype(BF16)
        else:
            tile = jnp.zeros((16, 128), BF16)
        sbuf[t // per, t % per * 16 : t % per * 16 + 16, :] = tile

    def scatter(peer, slot):
        return pltpu.make_async_remote_copy(
            src_ref=sbuf.at[peer], dst_ref=rbuf.at[slot], send_sem=ss1.at[peer],
            recv_sem=rs1.at[slot], device_id=(my_r, peer), device_id_type=MESH)

    def send1(k, _):
        scatter(lax.rem(my_c + k, n_col), my_c).start()
        return 0

    lax.fori_loop(1, n_col, send1, 0)
    rbuf[my_c] = sbuf[my_c]

    def to_lanes(value, stage, dst):
        stage[...] = value

        def one(w, _):
            lanes = pl.ds(pl.multiple_of(EDGE + w * SPAN, 128), SPAN)
            rows = pl.ds(pl.multiple_of(w * CELLS, CELLS), CELLS)
            first = stage[rows, 0:128]
            second = jnp.concatenate(
                [stage[rows, 128:WIDTH], jnp.zeros((CELLS, 256 - WIDTH), F32)], 1)
            dst[:, lanes] = join_tokens(first, second)
            return 0

        lax.fori_loop(0, WINDOWS, one, 0)

    d_normed = d_hidden * gain
    x = xs[...]
    center = x - jnp.mean(x, 1, keepdims=True)
    inv_std = lax.rsqrt(jnp.mean(center * center, 1, keepdims=True) + EPS)
    d_tokens = cs[...] + inv_std * (
        d_normed
        - jnp.mean(d_normed, 1, keepdims=True)
        - normed * jnp.mean(d_normed * normed, 1, keepdims=True))
    to_lanes(x + dot(att[...], wproj[...]) + bproj[...], xs, field)
    to_lanes(d_tokens, cs, cfield)
    for i, src in enumerate((field, cfield)):
        half = slice(i * WIN, i * WIN + WIN)
        orow[half, :] = pack_rows(src[:, :LANES]).astype(BF16)
        ocol[half, :] = src[:, LANES:].astype(BF16)
    for copy in lead:
        copy.wait_send()
    for copy in trail:
        copy.start()

    def recv1(k, _):
        peer = lax.rem(my_c + k, n_col)
        scatter(peer, peer).wait_recv()
        return 0

    lax.fori_loop(1, n_col, recv1, 0)
    acc = rbuf[0].astype(F32)
    for j in range(1, n_col):
        acc = acc + rbuf[j].astype(F32)
    acc = acc.astype(BF16)
    for i in range(per):
        s2[i] = acc[i * 16 : i * 16 + 16]

    gap = max(n_row // per, 1)
    slots = r2.shape[0]

    def owner(i):
        return lax.rem(i * gap + 2 * my_c, n_row)

    def up(i, device, slot):
        return pltpu.make_async_remote_copy(
            src_ref=s2.at[i], dst_ref=r2.at[i % slots, slot], send_sem=ss2.at[i],
            recv_sem=rs2.at[i % slots, slot], device_id=(device, my_c), device_id_type=MESH)

    def down(i, peer):
        return pltpu.make_async_remote_copy(
            src_ref=g2.at[i], dst_ref=g2.at[i], send_sem=ss3.at[peer],
            recv_sem=rs3.at[i], device_id=(peer, my_c), device_id_type=MESH)

    for i in range(per):
        @pl.when(owner(i) != my_r)
        def _():
            up(i, owner(i), my_r).start()

    for copy in trail:
        copy.wait_recv()
    for i, (src, dst) in enumerate(((field, res), (cfield, gin))):
        half = slice(i * WIN, i * WIN + WIN)
        low, high = merge_rows(rrow[half, :].astype(F32), src[:, :LANES])
        corner = jnp.where(
            upper((WIN, EDGE)), rdiag[half, :].astype(F32), rcol[half, :].astype(F32))
        dst[:, :EDGE] = corner.astype(BF16)
        dst[:, EDGE:HALF] = low[:, EDGE:].astype(BF16)
        dst[:, HALF:] = high.astype(BF16)

    for i in range(per):
        @pl.when(owner(i) == my_r)
        def _():
            slot = i % slots
            r2[slot, my_r] = s2[i]

            def recv2(k, _):
                peer = lax.rem(my_r + k, n_row)
                up(i, peer, peer).wait_recv()
                return 0

            lax.fori_loop(1, n_row, recv2, 0)
            total = r2[slot, 0].astype(F32)
            for j in range(1, n_row):
                total = total + r2[slot, j].astype(F32)
            g2[i] = total.astype(BF16)

            def send3(k, _):
                down(i, lax.rem(my_r + k, n_row)).start()
                return 0

            lax.fori_loop(1, n_row, send3, 0)

    for i in range(per):
        @pl.when(owner(i) != my_r)
        def _():
            down(i, my_r).wait_recv()

    def gather(peer, slot):
        return pltpu.make_async_remote_copy(
            src_ref=g2, dst_ref=fbuf.at[slot], send_sem=ss4.at[peer],
            recv_sem=rs4.at[slot], device_id=(my_r, peer), device_id_type=MESH)

    def send4(k, _):
        gather(lax.rem(my_c + k, n_col), my_c).start()
        return 0

    lax.fori_loop(1, n_col, send4, 0)
    fbuf[my_c] = g2[...]

    def recv4(k, _):
        peer = lax.rem(my_c + k, n_col)
        gather(peer, peer).wait_recv()
        return 0

    lax.fori_loop(1, n_col, recv4, 0)
    for t in range(TILES):
        rt, lt = t // 6, t % 6
        gs[rt * 16 : rt * 16 + 16, lt * 128 : lt * 128 + 128] = (
            fbuf[t // per, t % per].astype(F32) * grad_scale)
    g_qkv_w[...] = gs[0:WIDTH, : 3 * WIDTH]
    g_proj_w[...] = gs[0:WIDTH, 3 * WIDTH :]
    g_qkv_b[...] = gs[WIDTH : WIDTH + 1, : 3 * WIDTH]
    g_proj_b[...] = gs[WIDTH : WIDTH + 1, 3 * WIDTH :]
    g_gain[...] = gs[WIDTH + 1 : WIDTH + 2, :WIDTH]
    g_shift[...] = gs[WIDTH + 1 : WIDTH + 2, WIDTH : 2 * WIDTH]
    g_table[...] = gs[WIDTH + 2 : WIDTH + 2 + HEADS, :RELS]

    for copy in trail:
        copy.wait_send()

    def drain1(k, _):
        peer = lax.rem(my_c + k, n_col)
        scatter(peer, peer).wait_send()
        gather(peer, peer).wait_send()
        return 0

    lax.fori_loop(1, n_col, drain1, 0)
    for i in range(per):
        @pl.when(owner(i) != my_r)
        def _():
            up(i, owner(i), my_r).wait_send()

        @pl.when(owner(i) == my_r)
        def _():
            def drain3(k, _):
                down(i, lax.rem(my_r + k, n_row)).wait_send()
                return 0

            lax.fori_loop(1, n_row, drain3, 0)


def shards(image, cotangent, qkv_weight, qkv_bias, proj_weight, proj_bias, norm_gain, norm_bias,
           bias_table):
    n_row, n_col = lax.axis_size("row"), lax.axis_size("col")
    per = -(-TILES // n_col)
    slots = 1 if n_row >= per else per
    factor = float(n_row * n_col * TOKENS_HERE) ** (-0.5)
    tile = jax.ShapeDtypeStruct(image.shape, BF16)

    def line(width):
        return jax.ShapeDtypeStruct((1, width), F32)

    vmem = pl.BlockSpec(memory_space=pltpu.VMEM)
    dma = pltpu.SemaphoreType.DMA
    tokens = (TOKENS_HERE, WIDTH)
    halo = [pltpu.VMEM((16, HALF), BF16), pltpu.VMEM((16, EDGE), BF16)]
    arrived = [pltpu.VMEM((16, HALF), BF16)] + [pltpu.VMEM((16, EDGE), BF16)] * 2
    outs = pl.pallas_call(
        functools.partial(block_kernel, n_row, n_col, per, factor),
        out_shape=(
            tile, tile,
            jax.ShapeDtypeStruct((WIDTH, 3 * WIDTH), F32), line(3 * WIDTH),
            jax.ShapeDtypeStruct((WIDTH, WIDTH), F32), line(WIDTH),
            line(WIDTH), line(WIDTH), jax.ShapeDtypeStruct((HEADS, RELS), F32)),
        in_specs=[vmem] * 9,
        out_specs=(vmem,) * 9,
        scratch_shapes=halo + arrived + halo + arrived + [
            pltpu.VMEM((WIN, LANES + EDGE), F32), pltpu.VMEM((WIN, LANES + EDGE), F32),
            pltpu.VMEM(tokens, F32), pltpu.VMEM(tokens, F32), pltpu.VMEM(tokens, F32),
            pltpu.VMEM(tokens, BF16),
            pltpu.VMEM(tokens, BF16), pltpu.VMEM(tokens, BF16), pltpu.VMEM(tokens, BF16),
            pltpu.VMEM(tokens, BF16), pltpu.VMEM(tokens, BF16),
            pltpu.VMEM(tokens, F32), pltpu.VMEM(tokens, F32), pltpu.VMEM(tokens, F32),
            pltpu.VMEM((CELLS, HEADS * CELLS), F32),
            pltpu.VMEM((2, CELLS, HEADS * CELLS), F32),
            pltpu.VMEM((WIN, 256, 128), BF16),
            pltpu.VMEM((8, 256), F32),
            pltpu.VMEM((HEADS, WIN, 128), F32),
            pltpu.VMEM((WIDTH + 16, 4 * WIDTH), F32),
            pltpu.VMEM((n_col, per * 16, 128), BF16),
            pltpu.VMEM((n_col, per * 16, 128), BF16),
            pltpu.VMEM((per, 16, 128), BF16),
            pltpu.VMEM((slots, n_row, 16, 128), BF16),
            pltpu.VMEM((per, 16, 128), BF16),
            pltpu.VMEM((n_col, per, 16, 128), BF16),
            dma((6,)), dma((6,)), dma((n_col,)), dma((n_col,)), dma((per,)),
            dma((slots, n_row)), dma((n_row,)), dma((per,)), dma((n_col,)), dma((n_col,)),
        ],
        compiler_params=pltpu.CompilerParams(
            collective_id=1, has_side_effects=True, vmem_limit_bytes=48 * 1024 * 1024),
    )(image, cotangent, qkv_weight, qkv_bias[None], proj_weight, proj_bias[None], norm_gain[None],
      norm_bias[None], bias_table)
    return tuple(o[0] if o.shape[0] == 1 else o for o in outs)


def solution(mesh):
    in_specs = (P("row", "col"), P("row", "col"), P(), P(), P(), P(), P(), P(), P())
    out_specs = (P("row", "col"), P("row", "col"), P(), P(), P(), P(), P(), P(), P())
    return jax.shard_map(shards, mesh=mesh, in_specs=in_specs, out_specs=out_specs, check_vma=False)
```

```python
import functools

import jax
import jax.numpy as jnp
from jax import lax
from jax.experimental import pallas as pl
from jax.experimental.pallas import tpu as pltpu
from jax.sharding import PartitionSpec as P

WIDTH = 192
HEADS = 6
HEAD_DIM = 32
WIN = 8
CELLS = WIN * WIN
SHIFT = 4
RELS = 225
EPS = 1e-05
NEG = -1e30
TILE_COLS = 64
LANES = TILE_COLS * WIDTH
EDGE = SHIFT * WIDTH
WINDOWS = TILE_COLS // WIN
SPAN = WIN * WIDTH
TOKENS_HERE = WINDOWS * CELLS
CHUNKS = 4
PER_CHUNK = WINDOWS // CHUNKS
CHUNK_TOKENS = PER_CHUNK * CELLS
CHUNK = PER_CHUNK * SPAN
HALF = CHUNK // 2
SCALE = HEAD_DIM**-0.5
GROUPS = ((0, 4), (4, 2))
STRIPES = 13
WIDE = 4 * WIDTH
MID = WIDE // 2

MESH = pl.DeviceIdType.MESH
F32 = jnp.float32
BF16 = jnp.bfloat16


def dot(a, b, ca=1, cb=0):
    return lax.dot_general(a, b, (((ca,), (cb,)), ((), ())), preferred_element_type=F32)


def iota(shape, dim):
    return lax.broadcasted_iota(jnp.int32, shape, dim)


def upper(shape):
    return iota(shape, 0) < SHIFT


def pack_rows(field):
    back = pltpu.roll(field[:, HALF:], SHIFT, 0)
    return jnp.where(upper((WIN, HALF)), field[:, :HALF], back)


def merge_rows(packed, field):
    low = jnp.where(upper((WIN, HALF)), packed, field[:, :HALF])
    high = jnp.where(upper((WIN, HALF)), pltpu.roll(packed, SHIFT, 0), field[:, HALF:])
    return jnp.concatenate([low, high], 1)


def split_tokens(strip):
    left = iota((WIN, 128), 1) < 64
    first, second = [], []
    for j in range(WIN // 2):
        v = [strip[:, (3 * j + i) * 128 : (3 * j + i + 1) * 128] for i in range(3)]
        r1, r2 = pltpu.roll(v[1], 64, 1), pltpu.roll(v[2], 64, 1)
        first += [v[0], jnp.where(left, r1, r2)]
        second += [v[1], r2]
    return jnp.concatenate(first, 0), jnp.concatenate(second, 0)


def join_tokens(first, second):
    left = iota((WIN, 128), 1) < 64
    out = []
    for j in range(WIN // 2):
        e = slice(16 * j, 16 * j + 8)
        o = slice(16 * j + 8, 16 * j + 16)
        swapped = pltpu.roll(first[o], 64, 1)
        out.append(first[e])
        out.append(jnp.where(left, second[e], swapped))
        out.append(jnp.where(left, swapped, pltpu.roll(second[o], 64, 1)))
    return jnp.concatenate(out, 1)


def build_bias(table_ref, onehot, padded, diag, bias, last_row, last_col):
    padded[...] = jnp.zeros((8, 256), F32)
    padded[0:HEADS, 0:RELS] = table_ref[...]
    table = padded[...]
    hi = table.astype(BF16)
    rest = table - hi.astype(F32)
    mid = rest.astype(BF16)
    low = (rest - mid.astype(F32)).astype(BF16)
    lane = iota((1, 128), 1)
    a_q = (lane + SHIFT) % WIN
    for a in range(WIN):
        target = (a_q - (a + SHIFT) % WIN + WIN - 1) * (2 * WIN - 1) + lane // WIN
        target = jnp.where(lane < 120, target, -1)
        hot = jnp.where(iota((256, 128), 0) == target, 1.0, 0.0).astype(BF16)
        onehot[a] = hot
        rows = dot(hi, hot) + dot(mid, hot) + dot(low, hot)
        for h in range(HEADS):
            diag[h, a : a + 1, :] = rows[h : h + 1, :]
    sub = iota((WIN, 128), 0)
    lanes = iota((WIN, 128), 1)
    row_cut = jnp.where((sub < SHIFT) != (lanes % WIN < SHIFT), NEG, 0.0) * last_row
    right = lanes % 64 // WIN >= SHIFT
    for b in range(WIN):
        col_cut = jnp.where(right != (b >= SHIFT), NEG, 0.0) * last_col
        for pair in range(HEADS // 2):
            shift = (WIN - 1 - b) * WIN
            even = pltpu.roll(diag[2 * pair], (128 - shift) % 128, 1)
            odd = pltpu.roll(diag[2 * pair + 1], (192 - shift) % 128, 1)
            block = jnp.where(lanes < 64, even, odd) + row_cut
            where = (slice(b * WIN, b * WIN + WIN), slice(pair * 128, pair * 128 + 128))
            bias[(0,) + where] = block
            bias[(1,) + where] = block + col_cut


def table_grad(total, onehot, diag):
    lanes = iota((WIN, 128), 1)
    for h in range(HEADS):
        mine = (lanes < 64) == (h % 2 == 0)
        acc = jnp.zeros((WIN, 128), F32)
        for b in range(WIN):
            block = total[b * WIN : b * WIN + WIN, h // 2 * 128 : h // 2 * 128 + 128]
            block = jnp.where(mine, block, 0.0)
            acc = acc + pltpu.roll(block, ((WIN - 1 - b) * WIN + h % 2 * 64) % 128, 1)
        diag[h] = acc
    flat = jnp.concatenate([diag[h] for h in range(HEADS)], 0)
    hi = flat.astype(BF16)
    low = (flat - hi.astype(F32)).astype(BF16)
    sub = iota((HEADS * WIN, 256), 0) % WIN
    acc = jnp.zeros((HEADS * WIN, 256), F32)
    for a in range(WIN):
        part = dot(hi, onehot[a], 1, 1) + dot(low, onehot[a], 1, 1)
        acc = acc + jnp.where(sub == a, part, 0.0)
    return [
        jnp.sum(acc[h * WIN : h * WIN + WIN], 0, keepdims=True) for h in range(HEADS)
    ]


def masked_heads(x, group):
    start, count = group
    lane = iota((CELLS, count * HEAD_DIM), 1) // HEAD_DIM
    wide = x[:, start * HEAD_DIM : (start + count) * HEAD_DIM]
    zero = jnp.zeros_like(wide)
    return jnp.concatenate([jnp.where(lane == h, wide, zero) for h in range(count)], 0)


def own_heads(x, count):
    lane = iota((CELLS, count * HEAD_DIM), 1) // HEAD_DIM
    out = x[(count - 1) * CELLS : count * CELLS]
    for h in range(count - 1):
        out = jnp.where(lane == h, x[h * CELLS : (h + 1) * CELLS], out)
    return out


def fold(x):
    return jnp.sum(x.reshape(-1, WIN, x.shape[1]), 0)


def window_step(q, k, v, da, bias, gsum):
    att, dq, dk, dv = [], [], [], []
    for start, count in GROUPS:
        ch = slice(start * HEAD_DIM, (start + count) * HEAD_DIM)
        lanes = slice(start * CELLS, (start + count) * CELLS)
        qm = masked_heads(q, (start, count))
        dam = masked_heads(da, (start, count))
        s = dot(k[:, ch], qm, 1, 1) * SCALE + bias[:, lanes]
        e = jnp.exp(s - jnp.max(s, 0, keepdims=True))
        p = e * (1.0 / jnp.sum(e, 0, keepdims=True))
        dp = dot(v[:, ch], dam, 1, 1)
        ds = p * (dp - jnp.sum(p * dp, 0, keepdims=True))
        gsum[:, lanes] += ds
        pb, dsb = p.astype(BF16), ds.astype(BF16)
        dv.append(dot(pb, dam))
        dk.append(dot(dsb, qm) * SCALE)
        att.append(own_heads(dot(pb, v[:, ch], 0, 0), count).astype(BF16))
        dq.append(own_heads(dot(dsb, k[:, ch], 0, 0), count) * SCALE)
    return [jnp.concatenate(parts, 1) for parts in (att, dq, dk, dv)]


def block_kernel(n_row, n_col, spp, grad_scale, *refs):
    (img_h, cot_h, wqkv_h, bqkv_h, wproj_h, bproj_h, gain_h, shift_h, table_h,
     res, gin, total_out,
     img, cot, wqkv, bqkv, wproj, bproj, gain_ref, shift_ref, table_ref,
     irow, icol, hrow, hcol, hdiag, orow, ocol, rrow, rcol, rdiag,
     field, cfield, corner, weights, xd, xhid, xatt, sums, gsum,
     bias, onehot, padded, diag, gs, c_out, c_in, plane_buf, p_in, z_out, z_in, half_buf, last_in,
     ls, hs, hr, cs_sem, cr_sem, ps, pr, zs, zr, as_sem, ar_sem) = refs
    my_r, my_c = lax.axis_index("row"), lax.axis_index("col")
    above, below = lax.rem(my_r + n_row - 1, n_row), lax.rem(my_r + 1, n_row)
    left, right = lax.rem(my_c + n_col - 1, n_col), lax.rem(my_c + 1, n_col)
    n_plane, n_z = n_col, n_row // 2
    core = lax.rem(my_c, 2)
    my_p = my_c // 2 * 2 + lax.rem(my_r, 2)
    my_z = my_r // 2
    owners = -(-STRIPES // spp)
    rows_each = spp * 16

    def plane_peer(p):
        return (my_z * 2 + lax.rem(p, 2), p // 2 * 2 + core)

    def z_peer(z):
        return (z * 2 + lax.rem(my_r, 2), my_c)

    local = [
        pltpu.make_async_copy(src, dst, ls.at[i])
        for i, (src, dst) in enumerate((
            (img_h, img), (cot_h, cot), (wqkv_h, wqkv), (bqkv_h, bqkv), (wproj_h, wproj),
            (bproj_h, bproj), (gain_h, gain_ref), (shift_h, shift_ref), (table_h, table_ref)))
    ]
    for copy in local:
        copy.start()
    barrier = pltpu.get_barrier_semaphore()

    def greet(device):
        pl.semaphore_signal(barrier, inc=1, device_id=device, device_id_type=MESH)

    def greet_z(k, _):
        greet(z_peer(lax.rem(my_z + k, n_z)))
        return 0

    def greet_plane(k, _):
        greet(plane_peer(lax.rem(my_p + k, n_plane)))
        return 0

    lax.fori_loop(1, n_z, greet_z, 0)
    lax.fori_loop(1, n_plane, greet_plane, 0)
    for device in ((above, my_c), (below, my_c), (my_r, left), (my_r, right), (above, left),
                   (below, right)):
        greet(device)

    def remote(src, dst, send, recv, device):
        return pltpu.make_async_remote_copy(
            src_ref=src, dst_ref=dst, send_sem=send, recv_sem=recv, device_id=device,
            device_id_type=MESH)

    def halo(src, dst, i, device):
        return remote(src, dst, hs.at[i], hr.at[i], device)

    def lead_row(g):
        return halo(irow.at[g], hrow.at[g], g, (above, my_c))

    def trail_row(g):
        return halo(orow.at[g], rrow.at[g], CHUNKS + g, (below, my_c))

    n = 2 * CHUNKS
    lead = (halo(icol, hcol, n, (my_r, left)), halo(icol, hdiag, n + 1, (above, left)))
    trail = (halo(ocol, rcol, n + 2, (my_r, right)), halo(ocol, rdiag, n + 3, (below, right)))

    local[0].wait()
    local[1].wait()
    for i, (src, dst) in enumerate(((img, field), (cot, cfield))):
        half = slice(i * WIN, i * WIN + WIN)
        tile = src[...].astype(F32)
        icol[half, :] = tile[:, :EDGE].astype(BF16)
        dst[:, :LANES] = tile
        dst[:, LANES:] = tile[:, :EDGE]
        for g in range(CHUNKS):
            lanes = slice(EDGE + g * CHUNK, EDGE + (g + 1) * CHUNK)
            irow[g, half, :] = pack_rows(dst[:, lanes]).astype(BF16)
    pl.semaphore_wait(barrier, n_z - 1 + n_plane - 1 + 6)
    for g in range(CHUNKS):
        lead_row(g).start()
    for copy in lead:
        copy.start()

    for copy in local[2:]:
        copy.wait()
    last_row = (my_r == n_row - 1).astype(F32)
    last_col = (my_c == n_col - 1).astype(F32)
    build_bias(table_ref, onehot, padded, diag, bias, last_row, last_col)
    gsum[...] = jnp.zeros_like(gsum)
    sums[...] = jnp.zeros_like(sums)
    gs[WIDTH:, :] = jnp.zeros((owners * rows_each - WIDTH, WIDE), F32)
    for i in range(3):
        weights[i] = wqkv[:, i * WIDTH : (i + 1) * WIDTH]
    qkv_bias = bqkv[...].reshape(1, 3 * WIDTH)
    biases = [qkv_bias[:, i * WIDTH : (i + 1) * WIDTH] for i in range(3)]
    proj_bias = bproj[...].reshape(1, WIDTH)
    gain = gain_ref[...].reshape(1, WIDTH)
    shift = shift_ref[...].reshape(1, WIDTH)

    for copy in lead:
        copy.wait_recv()
    for i in range(2):
        half = slice(i * WIN, i * WIN + WIN)
        corner[i] = jnp.where(
            upper((WIN, EDGE)), hdiag[half, :].astype(F32), hcol[half, :].astype(F32))

    def chunk_step(g, _):
        final = g == CHUNKS - 1
        lanes = pl.ds(pl.multiple_of(EDGE + g * CHUNK, 128), CHUNK)
        rows = pl.ds(pl.multiple_of(g * CHUNK_TOKENS, CHUNK_TOKENS), CHUNK_TOKENS)
        lead_row(g).wait_recv()
        tokens = []
        for i, src in enumerate((field, cfield)):
            half = slice(i * WIN, i * WIN + WIN)
            whole = merge_rows(hrow[g, half, :].astype(F32), src[:, lanes])
            end = jnp.where(final, corner[i], whole[:, CHUNK - EDGE :])
            whole = jnp.concatenate([whole[:, : CHUNK - EDGE], end], 1)
            parts = [split_tokens(whole[:, j * SPAN : (j + 1) * SPAN]) for j in range(PER_CHUNK)]
            first = jnp.concatenate([part[0] for part in parts], 0)
            second = jnp.concatenate([part[1] for part in parts], 0)
            tokens.append(jnp.concatenate([first, second[:, : WIDTH - 128]], 1))
        x, cot_f = tokens
        center = x - jnp.mean(x, 1, keepdims=True)
        inv_std = lax.rsqrt(jnp.mean(center * center, 1, keepdims=True) + EPS)
        normed = center * inv_std
        hidden = (normed * gain + shift).astype(BF16)
        xhid[rows, :] = hidden
        q, k, v = [(dot(hidden, weights[i]) + biases[i]).astype(BF16) for i in range(3)]
        cot_b = cot_f.astype(BF16)
        da = dot(cot_b, wproj[...], 1, 1).astype(BF16)
        found = []
        for j in range(PER_CHUNK):
            r = slice(j * CELLS, (j + 1) * CELLS)
            if j == PER_CHUNK - 1:
                add = bias.at[final.astype(jnp.int32)]
            else:
                add = bias.at[0]
            found.append(window_step(q[r], k[r], v[r], da[r], add, gsum))
        att, dq, dk, dv = [jnp.concatenate([part[i] for part in found], 0) for i in range(4)]
        xatt[rows, :] = att
        out = x + dot(att, wproj[...]) + proj_bias
        d_hidden = jnp.zeros((CHUNK_TOKENS, WIDTH), F32)
        for i, part in enumerate((dq, dk, dv)):
            part_b = part.astype(BF16)
            xd[i, rows, :] = part_b
            sums[i] += fold(part)
            d_hidden = d_hidden + dot(part_b, weights[i], 1, 1)
        xd[3, rows, :] = cot_b
        sums[3] += fold(cot_f)
        sums[4] += fold(d_hidden * normed)
        sums[5] += fold(d_hidden)
        d_normed = d_hidden * gain
        d_tokens = cot_f + inv_std * (
            d_normed
            - jnp.mean(d_normed, 1, keepdims=True)
            - normed * jnp.mean(d_normed * normed, 1, keepdims=True))
        for i, (value, dst) in enumerate(((out, field), (d_tokens, cfield))):
            half = slice(i * WIN, i * WIN + WIN)
            first = value[:, :128]
            second = jnp.concatenate(
                [value[:, 128:], jnp.zeros((CHUNK_TOKENS, 256 - WIDTH), F32)], 1)
            strips = []
            for j in range(PER_CHUNK):
                r = slice(j * CELLS, (j + 1) * CELLS)
                strips.append(join_tokens(first[r], second[r]))
            whole = jnp.concatenate(strips, 1)
            dst[:, lanes] = whole
            orow[g, half, :] = pack_rows(whole).astype(BF16)
            ocol[half, :] = whole[:, CHUNK - EDGE :].astype(BF16)
        trail_row(g).start()
        return 0

    lax.fori_loop(0, CHUNKS, chunk_step, 0)
    for copy in trail:
        copy.start()

    hidden_t = xhid[...].T
    for i in range(3):
        gs[0:WIDTH, i * WIDTH : (i + 1) * WIDTH] = dot(hidden_t, xd[i])
    gs[0:WIDTH, 3 * WIDTH :] = dot(xatt[...], xd[3], 0, 0)
    for i in range(4):
        gs[WIDTH : WIDTH + 1, i * WIDTH : (i + 1) * WIDTH] = jnp.sum(sums[i], 0, keepdims=True)
    for i in range(2):
        gs[WIDTH + 1 : WIDTH + 2, i * WIDTH : (i + 1) * WIDTH] = jnp.sum(
            sums[4 + i], 0, keepdims=True)
    for h, line in enumerate(table_grad(gsum[...], onehot, diag)):
        gs[WIDTH + 2 + h : WIDTH + 3 + h, 0:256] = line

    mine = pl.ds(pl.multiple_of(core * MID, 128), MID)
    other = pl.ds(pl.multiple_of((1 - core) * MID, 128), MID)
    partner = (my_r, my_c + 1 - 2 * core)
    c_out[...] = gs[:, other].astype(BF16)
    swap = remote(c_out, c_in, cs_sem.at[0], cr_sem.at[0], partner)
    swap.start()
    swap.wait_recv()
    plane_buf[...] = (gs[:, mine] + c_in[...].astype(F32)).astype(BF16).reshape(
        owners, rows_each, MID)

    def scatter(p, slot):
        return remote(plane_buf.at[p], p_in.at[slot], ps.at[p], pr.at[slot], plane_peer(p))

    def from_plane(p):
        return remote(plane_buf.at[0], p_in.at[p], ps.at[0], pr.at[p], plane_peer(p))

    def send_scatter(k, _):
        p = lax.rem(my_p + k, n_plane)

        @pl.when(p < owners)
        def _():
            scatter(p, my_p).start()

        return 0

    lax.fori_loop(1, n_plane, send_scatter, 0)

    for g in range(CHUNKS):
        trail_row(g).wait_recv()
    for copy in trail:
        copy.wait_recv()
    for i, (src, dst) in enumerate(((field, res), (cfield, gin))):
        half = slice(i * WIN, i * WIN + WIN)
        ends = jnp.where(
            upper((WIN, EDGE)), rdiag[half, :].astype(F32), rcol[half, :].astype(F32))
        dst[:, :EDGE] = ends.astype(BF16)
        for g in range(CHUNKS):
            start = EDGE + g * CHUNK
            size = min(CHUNK, LANES - start)
            whole = merge_rows(rrow[g, half, :].astype(F32), src[:, start : start + CHUNK])
            dst[:, start : start + size] = whole[:, :size].astype(BF16)

    def along_z(z, slot):
        return remote(z_out, z_in.at[slot], zs.at[z], zr.at[slot], z_peer(z))

    def spread(p, owner):
        return remote(half_buf.at[owner], half_buf.at[owner], as_sem.at[p], ar_sem.at[owner],
                      plane_peer(p))

    def loop_plane(step):
        def one(k, _):
            step(lax.rem(my_p + k, n_plane))
            return 0

        lax.fori_loop(1, n_plane, one, 0)

    def loop_z(step):
        def one(k, _):
            step(lax.rem(my_z + k, n_z))
            return 0

        lax.fori_loop(1, n_z, one, 0)

    @pl.when(my_p < owners)
    def _():
        p_in[my_p] = plane_buf[my_p]
        loop_plane(lambda p: from_plane(p).wait_recv())
        acc = p_in[0].astype(F32)
        for j in range(1, n_plane):
            acc = acc + p_in[j].astype(F32)
        z_out[...] = acc.astype(BF16)
        loop_z(lambda z: along_z(z, my_z).start())
        z_in[my_z] = z_out[...]
        loop_z(lambda z: along_z(z, z).wait_recv())
        acc = z_in[0].astype(F32)
        for j in range(1, n_z):
            acc = acc + z_in[j].astype(F32)
        half_buf[my_p] = acc.astype(BF16)
        loop_plane(lambda p: spread(p, my_p).start())

    def arrive(p):
        @pl.when(p < owners)
        def _():
            spread(p, p).wait_recv()

    loop_plane(arrive)
    back = remote(half_buf, last_in, cs_sem.at[1], cr_sem.at[1], partner)
    back.start()
    flat = (owners * rows_each, MID)
    total_out[:, mine] = half_buf[...].astype(F32).reshape(flat) * grad_scale
    back.wait_recv()
    total_out[:, other] = last_in[...].astype(F32).reshape(flat) * grad_scale

    for g in range(CHUNKS):
        lead_row(g).wait_send()
        trail_row(g).wait_send()
    for copy in lead + trail + (swap, back):
        copy.wait_send()

    def sent(p):
        @pl.when(p < owners)
        def _():
            scatter(p, my_p).wait_send()

    loop_plane(sent)

    @pl.when(my_p < owners)
    def _():
        loop_z(lambda z: along_z(z, my_z).wait_send())
        loop_plane(lambda p: spread(p, my_p).wait_send())


def finish_kernel(res, gin, total, *refs):
    outs, (b0, b1, w0, w1, v0, v1, v2, t0, sems) = refs[:9], refs[9:]
    w0[...] = total[0:WIDTH, : 3 * WIDTH]
    w1[...] = total[0:WIDTH, 3 * WIDTH :]
    b0[...] = total[WIDTH : WIDTH + 1, : 3 * WIDTH].reshape(3 * WIDTH)
    v0[...] = total[WIDTH : WIDTH + 1, 3 * WIDTH :].reshape(WIDTH)
    v1[...] = total[WIDTH + 1 : WIDTH + 2, :WIDTH].reshape(WIDTH)
    v2[...] = total[WIDTH + 1 : WIDTH + 2, WIDTH : 2 * WIDTH].reshape(WIDTH)
    t0[...] = total[WIDTH + 2 : WIDTH + 2 + HEADS, :RELS]
    copies = [
        pltpu.make_async_copy(src, dst, sems.at[i])
        for i, (src, dst) in enumerate(zip((res, gin, w0, b0, w1, v0, v1, v2, t0), outs))
    ]
    for copy in copies:
        copy.start()
    for copy in copies:
        copy.wait()


def shards(image, cotangent, qkv_weight, qkv_bias, proj_weight, proj_bias, norm_gain, norm_bias,
           bias_table):
    n_row, n_col = lax.axis_size("row"), lax.axis_size("col")
    spp = -(-STRIPES // n_col)
    owners = -(-STRIPES // spp)
    rows_each = spp * 16
    factor = float(n_row * n_col * TOKENS_HERE) ** (-0.5)
    args = (image, cotangent, qkv_weight, qkv_bias, proj_weight, proj_bias, norm_gain, norm_bias,
            bias_table)
    tile = jax.ShapeDtypeStruct(image.shape, BF16)
    vmem = pl.BlockSpec(memory_space=pltpu.VMEM)
    hbm = pl.BlockSpec(memory_space=pltpu.HBM)
    dma = pltpu.SemaphoreType.DMA
    row_halo = pltpu.VMEM((CHUNKS, 16, HALF), BF16)
    col_halo = pltpu.VMEM((16, EDGE), BF16)
    half = (owners * rows_each, MID)
    halves = (owners, rows_each, MID)
    stripe = (rows_each, MID)
    parts = pl.pallas_call(
        functools.partial(block_kernel, n_row, n_col, spp, factor),
        out_shape=(tile, tile, jax.ShapeDtypeStruct((owners * rows_each, WIDE), F32)),
        in_specs=[hbm] * 9,
        out_specs=(vmem,) * 3,
        scratch_shapes=[pltpu.VMEM(a.shape, a.dtype) for a in args]
        + [row_halo, col_halo, row_halo, col_halo, col_halo] * 2
        + [
            pltpu.VMEM((WIN, LANES + EDGE), F32), pltpu.VMEM((WIN, LANES + EDGE), F32),
            pltpu.VMEM((2, WIN, EDGE), F32),
            pltpu.VMEM((3, WIDTH, WIDTH), BF16),
            pltpu.VMEM((4, TOKENS_HERE, WIDTH), BF16),
            pltpu.VMEM((TOKENS_HERE, WIDTH), BF16),
            pltpu.VMEM((TOKENS_HERE, WIDTH), BF16),
            pltpu.VMEM((6, WIN, WIDTH), F32),
            pltpu.VMEM((CELLS, HEADS * CELLS), F32),
            pltpu.VMEM((2, CELLS, HEADS * CELLS), F32),
            pltpu.VMEM((WIN, 256, 128), BF16),
            pltpu.VMEM((8, 256), F32),
            pltpu.VMEM((HEADS, WIN, 128), F32),
            pltpu.VMEM((owners * rows_each, WIDE), F32),
            pltpu.VMEM(half, BF16), pltpu.VMEM(half, BF16),
            pltpu.VMEM(halves, BF16), pltpu.VMEM((n_col,) + stripe, BF16),
            pltpu.VMEM(stripe, BF16), pltpu.VMEM((n_row // 2,) + stripe, BF16),
            pltpu.VMEM(halves, BF16), pltpu.VMEM(halves, BF16),
            dma((9,)), dma((2 * CHUNKS + 4,)), dma((2 * CHUNKS + 4,)), dma((2,)), dma((2,)),
            dma((n_col,)), dma((n_col,)), dma((n_row // 2,)), dma((n_row // 2,)),
            dma((n_col,)), dma((n_col,)),
        ],
        compiler_params=pltpu.CompilerParams(
            collective_id=1, has_side_effects=True, vmem_limit_bytes=60 * 1024 * 1024),
    )(*args)
    shapes = (image, cotangent, (WIDTH, 3 * WIDTH), (3 * WIDTH,), (WIDTH, WIDTH), (WIDTH,),
              (WIDTH,), (WIDTH,), (HEADS, RELS))
    outs = (tile, tile) + tuple(jax.ShapeDtypeStruct(s, F32) for s in shapes[2:])
    stage = [shapes[3], (1,), shapes[2], shapes[4], shapes[5], shapes[6], shapes[7], shapes[8]]
    return pl.pallas_call(
        finish_kernel,
        out_shape=outs,
        in_specs=[vmem] * 3,
        out_specs=(hbm,) * 9,
        scratch_shapes=[pltpu.VMEM(s, F32) for s in stage] + [dma((9,))],
        compiler_params=pltpu.CompilerParams(vmem_limit_bytes=60 * 1024 * 1024),
    )(*parts)


def solution(mesh):
    in_specs = (P("row", "col"), P("row", "col"), P(), P(), P(), P(), P(), P(), P())
    out_specs = (P("row", "col"), P("row", "col"), P(), P(), P(), P(), P(), P(), P())
    return jax.shard_map(shards, mesh=mesh, in_specs=in_specs, out_specs=out_specs, check_vma=False)
```

```python
import functools

import jax
import jax.numpy as jnp
from jax import lax
from jax.experimental import pallas as pl
from jax.experimental.pallas import tpu as pltpu
from jax.sharding import PartitionSpec as P

WIDTH = 192
HEADS = 6
HEAD_DIM = 32
WIN = 8
CELLS = WIN * WIN
SHIFT = 4
RELS = 225
EPS = 1e-05
NEG = -1e30
TILE_COLS = 64
LANES = TILE_COLS * WIDTH
EDGE = SHIFT * WIDTH
WINDOWS = TILE_COLS // WIN
SPAN = WIN * WIDTH
TOKENS_HERE = WINDOWS * CELLS
CHUNKS = 4
PER_CHUNK = WINDOWS // CHUNKS
CHUNK_TOKENS = PER_CHUNK * CELLS
CHUNK = PER_CHUNK * SPAN
HALF = CHUNK // 2
SCALE = HEAD_DIM**-0.5
GROUPS = ((0, 4), (4, 2))
STRIPES = 13
WIDE = 4 * WIDTH
MID = WIDE // 2

MESH = pl.DeviceIdType.MESH
F32 = jnp.float32
BF16 = jnp.bfloat16


def dot(a, b, ca=1, cb=0):
    return lax.dot_general(a, b, (((ca,), (cb,)), ((), ())), preferred_element_type=F32)


def iota(shape, dim):
    return lax.broadcasted_iota(jnp.int32, shape, dim)


def upper(shape):
    return iota(shape, 0) < SHIFT


def pack_rows(field):
    back = pltpu.roll(field[:, HALF:], SHIFT, 0)
    return jnp.where(upper((WIN, HALF)), field[:, :HALF], back)


def merge_rows(packed, field):
    low = jnp.where(upper((WIN, HALF)), packed, field[:, :HALF])
    high = jnp.where(upper((WIN, HALF)), pltpu.roll(packed, SHIFT, 0), field[:, HALF:])
    return jnp.concatenate([low, high], 1)


def split_tokens(strip):
    left = iota((WIN, 128), 1) < 64
    first, second = [], []
    for j in range(WIN // 2):
        v = [strip[:, (3 * j + i) * 128 : (3 * j + i + 1) * 128] for i in range(3)]
        r1, r2 = pltpu.roll(v[1], 64, 1), pltpu.roll(v[2], 64, 1)
        first += [v[0], jnp.where(left, r1, r2)]
        second += [v[1], r2]
    return jnp.concatenate(first, 0), jnp.concatenate(second, 0)


def join_tokens(first, second):
    left = iota((WIN, 128), 1) < 64
    out = []
    for j in range(WIN // 2):
        e = slice(16 * j, 16 * j + 8)
        o = slice(16 * j + 8, 16 * j + 16)
        swapped = pltpu.roll(first[o], 64, 1)
        out.append(first[e])
        out.append(jnp.where(left, second[e], swapped))
        out.append(jnp.where(left, swapped, pltpu.roll(second[o], 64, 1)))
    return jnp.concatenate(out, 1)


def build_bias(table_ref, onehot, padded, diag, bias, last_row, last_col):
    padded[...] = jnp.zeros((8, 256), F32)
    padded[0:HEADS, 0:RELS] = table_ref[...]
    table = padded[...]
    hi = table.astype(BF16)
    rest = table - hi.astype(F32)
    mid = rest.astype(BF16)
    low = (rest - mid.astype(F32)).astype(BF16)
    lane = iota((1, 128), 1)
    a_q = (lane + SHIFT) % WIN
    for a in range(WIN):
        target = (a_q - (a + SHIFT) % WIN + WIN - 1) * (2 * WIN - 1) + lane // WIN
        target = jnp.where(lane < 120, target, -1)
        hot = jnp.where(iota((256, 128), 0) == target, 1.0, 0.0).astype(BF16)
        onehot[a] = hot
        rows = dot(hi, hot) + dot(mid, hot) + dot(low, hot)
        for h in range(HEADS):
            diag[h, a : a + 1, :] = rows[h : h + 1, :]
    sub = iota((WIN, 128), 0)
    lanes = iota((WIN, 128), 1)
    row_cut = jnp.where((sub < SHIFT) != (lanes % WIN < SHIFT), NEG, 0.0) * last_row
    right = lanes % 64 // WIN >= SHIFT
    for b in range(WIN):
        col_cut = jnp.where(right != (b >= SHIFT), NEG, 0.0) * last_col
        for pair in range(HEADS // 2):
            shift = (WIN - 1 - b) * WIN
            even = pltpu.roll(diag[2 * pair], (128 - shift) % 128, 1)
            odd = pltpu.roll(diag[2 * pair + 1], (192 - shift) % 128, 1)
            block = jnp.where(lanes < 64, even, odd) + row_cut
            where = (slice(b * WIN, b * WIN + WIN), slice(pair * 128, pair * 128 + 128))
            bias[(0,) + where] = block
            bias[(1,) + where] = block + col_cut


def table_grad(total, onehot, diag):
    lanes = iota((WIN, 128), 1)
    for h in range(HEADS):
        mine = (lanes < 64) == (h % 2 == 0)
        acc = jnp.zeros((WIN, 128), F32)
        for b in range(WIN):
            block = total[b * WIN : b * WIN + WIN, h // 2 * 128 : h // 2 * 128 + 128]
            block = jnp.where(mine, block, 0.0)
            acc = acc + pltpu.roll(block, ((WIN - 1 - b) * WIN + h % 2 * 64) % 128, 1)
        diag[h] = acc
    flat = jnp.concatenate([diag[h] for h in range(HEADS)], 0)
    hi = flat.astype(BF16)
    low = (flat - hi.astype(F32)).astype(BF16)
    sub = iota((HEADS * WIN, 256), 0) % WIN
    acc = jnp.zeros((HEADS * WIN, 256), F32)
    for a in range(WIN):
        part = dot(hi, onehot[a], 1, 1) + dot(low, onehot[a], 1, 1)
        acc = acc + jnp.where(sub == a, part, 0.0)
    return [
        jnp.sum(acc[h * WIN : h * WIN + WIN], 0, keepdims=True) for h in range(HEADS)
    ]


def masked_heads(x, group):
    start, count = group
    lane = iota((CELLS, count * HEAD_DIM), 1) // HEAD_DIM
    wide = x[:, start * HEAD_DIM : (start + count) * HEAD_DIM]
    zero = jnp.zeros_like(wide)
    return jnp.concatenate([jnp.where(lane == h, wide, zero) for h in range(count)], 0)


def own_heads(x, count):
    lane = iota((CELLS, count * HEAD_DIM), 1) // HEAD_DIM
    out = x[(count - 1) * CELLS : count * CELLS]
    for h in range(count - 1):
        out = jnp.where(lane == h, x[h * CELLS : (h + 1) * CELLS], out)
    return out


def fold(x):
    return jnp.sum(x.reshape(-1, WIN, x.shape[1]), 0)


def window_step(q, k, v, da, bias, gsum):
    att, dq, dk, dv = [], [], [], []
    for start, count in GROUPS:
        ch = slice(start * HEAD_DIM, (start + count) * HEAD_DIM)
        lanes = slice(start * CELLS, (start + count) * CELLS)
        qm = masked_heads(q, (start, count))
        dam = masked_heads(da, (start, count))
        s = dot(k[:, ch], qm, 1, 1) * SCALE + bias[:, lanes]
        e = jnp.exp(s - jnp.max(s, 0, keepdims=True))
        p = e * (1.0 / jnp.sum(e, 0, keepdims=True))
        dp = dot(v[:, ch], dam, 1, 1)
        ds = p * (dp - jnp.sum(p * dp, 0, keepdims=True))
        gsum[:, lanes] += ds
        pb, dsb = p.astype(BF16), ds.astype(BF16)
        dv.append(dot(pb, dam))
        dk.append(dot(dsb, qm) * SCALE)
        att.append(own_heads(dot(pb, v[:, ch], 0, 0), count).astype(BF16))
        dq.append(own_heads(dot(dsb, k[:, ch], 0, 0), count) * SCALE)
    return [jnp.concatenate(parts, 1) for parts in (att, dq, dk, dv)]


def block_kernel(n_row, n_col, spp, grad_scale, *refs):
    (img_h, cot_h, wqkv_h, bqkv_h, wproj_h, bproj_h, gain_h, shift_h, table_h,
     res, gin, total_out,
     img, cot, wqkv, bqkv, wproj, bproj, gain_ref, shift_ref, table_ref,
     irow, icol, hrow, hcol, hdiag, orow, ocol, rrow, rcol, rdiag,
     field, cfield, corner, weights, xd, xhid, xatt, sums, gsum,
     bias, onehot, padded, diag, gs, c_out, c_in, plane_buf, p_in, z_out, z_in, half_buf, last_in,
     ls, hs, hr, cs_sem, cr_sem, ps, pr, zs, zr, as_sem, ar_sem,
     row_known, col_known, pair_known) = refs
    my_r, my_c = lax.axis_index("row"), lax.axis_index("col")
    above, below = lax.rem(my_r + n_row - 1, n_row), lax.rem(my_r + 1, n_row)
    left, right = lax.rem(my_c + n_col - 1, n_col), lax.rem(my_c + 1, n_col)
    n_plane, n_z = n_col, n_row // 2
    core = lax.rem(my_c, 2)
    my_p = my_c // 2 * 2 + lax.rem(my_r, 2)
    my_z = my_r // 2
    owners = -(-STRIPES // spp)
    rows_each = spp * 16

    def plane_peer(p):
        return (my_z * 2 + lax.rem(p, 2), p // 2 * 2 + core)

    def z_peer(z):
        return (z * 2 + lax.rem(my_r, 2), my_c)

    local = [
        pltpu.make_async_copy(src, dst, ls.at[i])
        for i, (src, dst) in enumerate((
            (img_h, img), (cot_h, cot), (wqkv_h, wqkv), (bqkv_h, bqkv), (wproj_h, wproj),
            (bproj_h, bproj), (gain_h, gain_ref), (shift_h, shift_ref), (table_h, table_ref)))
    ]
    for copy in local:
        copy.start()
    barrier = pltpu.get_barrier_semaphore()

    def greet(device):
        pl.semaphore_signal(barrier, inc=1, device_id=device, device_id_type=MESH)

    for device in ((above, my_c), (below, my_c), (my_r, left), (my_r, right), (above, left),
                   (below, right)):
        greet(device)

    rounds = [(g, 2**g) for g in range(CHUNKS)]
    row_rounds = [(g, d) for g, d in rounds if 4 * d <= n_row]
    col_rounds = [(g, d) for g, d in rounds if 4 * d <= n_col]

    def tell(sem, device):
        pl.semaphore_signal(sem, inc=1, device_id=device, device_id_type=MESH)

    def start_round(g):
        for k, d in row_rounds:
            @pl.when(g == k)
            def _():
                tell(row_known.at[k], (lax.rem(my_r + d, n_row), my_c))
                tell(row_known.at[k], (lax.rem(my_r + n_row - d, n_row), my_c))

        for k, d in col_rounds:
            @pl.when(g == k)
            def _():
                tell(col_known.at[k], (my_r, lax.rem(my_c + d, n_col)))
                tell(col_known.at[k], (my_r, lax.rem(my_c + n_col - d, n_col)))

        @pl.when(g == CHUNKS - 1)
        def _():
            tell(pair_known, (my_r + 1 - 2 * lax.rem(my_r, 2), my_c))

    def end_round(g):
        for k, _ in row_rounds:
            @pl.when(g == k)
            def _():
                pl.semaphore_wait(row_known.at[k], 2)

        for k, _ in col_rounds:
            @pl.when(g == k)
            def _():
                pl.semaphore_wait(col_known.at[k], 2)

        @pl.when(g == CHUNKS - 1)
        def _():
            pl.semaphore_wait(pair_known, 1)

    def remote(src, dst, send, recv, device):
        return pltpu.make_async_remote_copy(
            src_ref=src, dst_ref=dst, send_sem=send, recv_sem=recv, device_id=device,
            device_id_type=MESH)

    def halo(src, dst, i, device):
        return remote(src, dst, hs.at[i], hr.at[i], device)

    def lead_row(g):
        return halo(irow.at[g], hrow.at[g], g, (above, my_c))

    def trail_row(g):
        return halo(orow.at[g], rrow.at[g], CHUNKS + g, (below, my_c))

    n = 2 * CHUNKS
    lead = (halo(icol, hcol, n, (my_r, left)), halo(icol, hdiag, n + 1, (above, left)))
    trail = (halo(ocol, rcol, n + 2, (my_r, right)), halo(ocol, rdiag, n + 3, (below, right)))

    local[0].wait()
    local[1].wait()
    for i, (src, dst) in enumerate(((img, field), (cot, cfield))):
        half = slice(i * WIN, i * WIN + WIN)
        tile = src[...].astype(F32)
        icol[half, :] = tile[:, :EDGE].astype(BF16)
        dst[:, :LANES] = tile
        dst[:, LANES:] = tile[:, :EDGE]
        for g in range(CHUNKS):
            lanes = slice(EDGE + g * CHUNK, EDGE + (g + 1) * CHUNK)
            irow[g, half, :] = pack_rows(dst[:, lanes]).astype(BF16)
    pl.semaphore_wait(barrier, 6)
    for g in range(CHUNKS):
        lead_row(g).start()
    for copy in lead:
        copy.start()

    for copy in local[2:]:
        copy.wait()
    last_row = (my_r == n_row - 1).astype(F32)
    last_col = (my_c == n_col - 1).astype(F32)
    build_bias(table_ref, onehot, padded, diag, bias, last_row, last_col)
    gsum[...] = jnp.zeros_like(gsum)
    sums[...] = jnp.zeros_like(sums)
    gs[WIDTH:, :] = jnp.zeros((owners * rows_each - WIDTH, WIDE), F32)
    for i in range(3):
        weights[i] = wqkv[:, i * WIDTH : (i + 1) * WIDTH]
    qkv_bias = bqkv[...].reshape(1, 3 * WIDTH)
    biases = [qkv_bias[:, i * WIDTH : (i + 1) * WIDTH] for i in range(3)]
    proj_bias = bproj[...].reshape(1, WIDTH)
    gain = gain_ref[...].reshape(1, WIDTH)
    shift = shift_ref[...].reshape(1, WIDTH)

    for copy in lead:
        copy.wait_recv()
    for i in range(2):
        half = slice(i * WIN, i * WIN + WIN)
        corner[i] = jnp.where(
            upper((WIN, EDGE)), hdiag[half, :].astype(F32), hcol[half, :].astype(F32))

    def chunk_step(g, _):
        final = g == CHUNKS - 1
        lanes = pl.ds(pl.multiple_of(EDGE + g * CHUNK, 128), CHUNK)
        rows = pl.ds(pl.multiple_of(g * CHUNK_TOKENS, CHUNK_TOKENS), CHUNK_TOKENS)
        start_round(g)
        lead_row(g).wait_recv()
        tokens = []
        for i, src in enumerate((field, cfield)):
            half = slice(i * WIN, i * WIN + WIN)
            whole = merge_rows(hrow[g, half, :].astype(F32), src[:, lanes])
            end = jnp.where(final, corner[i], whole[:, CHUNK - EDGE :])
            whole = jnp.concatenate([whole[:, : CHUNK - EDGE], end], 1)
            parts = [split_tokens(whole[:, j * SPAN : (j + 1) * SPAN]) for j in range(PER_CHUNK)]
            first = jnp.concatenate([part[0] for part in parts], 0)
            second = jnp.concatenate([part[1] for part in parts], 0)
            tokens.append(jnp.concatenate([first, second[:, : WIDTH - 128]], 1))
        x, cot_f = tokens
        center = x - jnp.mean(x, 1, keepdims=True)
        inv_std = lax.rsqrt(jnp.mean(center * center, 1, keepdims=True) + EPS)
        normed = center * inv_std
        hidden = (normed * gain + shift).astype(BF16)
        xhid[rows, :] = hidden
        q, k, v = [(dot(hidden, weights[i]) + biases[i]).astype(BF16) for i in range(3)]
        cot_b = cot_f.astype(BF16)
        da = dot(cot_b, wproj[...], 1, 1).astype(BF16)
        found = []
        for j in range(PER_CHUNK):
            r = slice(j * CELLS, (j + 1) * CELLS)
            if j == PER_CHUNK - 1:
                add = bias.at[final.astype(jnp.int32)]
            else:
                add = bias.at[0]
            found.append(window_step(q[r], k[r], v[r], da[r], add, gsum))
        att, dq, dk, dv = [jnp.concatenate([part[i] for part in found], 0) for i in range(4)]
        xatt[rows, :] = att
        out = x + dot(att, wproj[...]) + proj_bias
        d_hidden = jnp.zeros((CHUNK_TOKENS, WIDTH), F32)
        for i, part in enumerate((dq, dk, dv)):
            part_b = part.astype(BF16)
            xd[i, rows, :] = part_b
            sums[i] += fold(part)
            d_hidden = d_hidden + dot(part_b, weights[i], 1, 1)
        xd[3, rows, :] = cot_b
        sums[3] += fold(cot_f)
        sums[4] += fold(d_hidden * normed)
        sums[5] += fold(d_hidden)
        d_normed = d_hidden * gain
        d_tokens = cot_f + inv_std * (
            d_normed
            - jnp.mean(d_normed, 1, keepdims=True)
            - normed * jnp.mean(d_normed * normed, 1, keepdims=True))
        for i, (value, dst) in enumerate(((out, field), (d_tokens, cfield))):
            half = slice(i * WIN, i * WIN + WIN)
            first = value[:, :128]
            second = jnp.concatenate(
                [value[:, 128:], jnp.zeros((CHUNK_TOKENS, 256 - WIDTH), F32)], 1)
            strips = []
            for j in range(PER_CHUNK):
                r = slice(j * CELLS, (j + 1) * CELLS)
                strips.append(join_tokens(first[r], second[r]))
            whole = jnp.concatenate(strips, 1)
            dst[:, lanes] = whole
            orow[g, half, :] = pack_rows(whole).astype(BF16)
            ocol[half, :] = whole[:, CHUNK - EDGE :].astype(BF16)
        trail_row(g).start()
        end_round(g)
        return 0

    lax.fori_loop(0, CHUNKS, chunk_step, 0)
    for copy in trail:
        copy.start()

    hidden_t = xhid[...].T
    for i in range(3):
        gs[0:WIDTH, i * WIDTH : (i + 1) * WIDTH] = dot(hidden_t, xd[i])
    gs[0:WIDTH, 3 * WIDTH :] = dot(xatt[...], xd[3], 0, 0)
    for i in range(4):
        gs[WIDTH : WIDTH + 1, i * WIDTH : (i + 1) * WIDTH] = jnp.sum(sums[i], 0, keepdims=True)
    for i in range(2):
        gs[WIDTH + 1 : WIDTH + 2, i * WIDTH : (i + 1) * WIDTH] = jnp.sum(
            sums[4 + i], 0, keepdims=True)
    for h, line in enumerate(table_grad(gsum[...], onehot, diag)):
        gs[WIDTH + 2 + h : WIDTH + 3 + h, 0:256] = line

    mine = pl.ds(pl.multiple_of(core * MID, 128), MID)
    other = pl.ds(pl.multiple_of((1 - core) * MID, 128), MID)
    partner = (my_r, my_c + 1 - 2 * core)
    c_out[...] = gs[:, other].astype(BF16)
    swap = remote(c_out, c_in, cs_sem.at[0], cr_sem.at[0], partner)
    swap.start()
    swap.wait_recv()
    plane_buf[...] = (gs[:, mine] + c_in[...].astype(F32)).astype(BF16).reshape(
        owners, rows_each, MID)

    def scatter(p, slot):
        return remote(plane_buf.at[p], p_in.at[slot], ps.at[p], pr.at[slot], plane_peer(p))

    def from_plane(p):
        return remote(plane_buf.at[0], p_in.at[p], ps.at[0], pr.at[p], plane_peer(p))

    def send_scatter(k, _):
        p = lax.rem(my_p + k, n_plane)

        @pl.when(p < owners)
        def _():
            scatter(p, my_p).start()

        return 0

    lax.fori_loop(1, n_plane, send_scatter, 0)

    for g in range(CHUNKS):
        trail_row(g).wait_recv()
    for copy in trail:
        copy.wait_recv()
    for i, (src, dst) in enumerate(((field, res), (cfield, gin))):
        half = slice(i * WIN, i * WIN + WIN)
        ends = jnp.where(
            upper((WIN, EDGE)), rdiag[half, :].astype(F32), rcol[half, :].astype(F32))
        dst[:, :EDGE] = ends.astype(BF16)
        for g in range(CHUNKS):
            start = EDGE + g * CHUNK
            size = min(CHUNK, LANES - start)
            whole = merge_rows(rrow[g, half, :].astype(F32), src[:, start : start + CHUNK])
            dst[:, start : start + size] = whole[:, :size].astype(BF16)

    def along_z(z, slot):
        return remote(z_out, z_in.at[slot], zs.at[z], zr.at[slot], z_peer(z))

    def spread(p, owner):
        return remote(half_buf.at[owner], half_buf.at[owner], as_sem.at[p], ar_sem.at[owner],
                      plane_peer(p))

    def loop_plane(step):
        def one(k, _):
            step(lax.rem(my_p + k, n_plane))
            return 0

        lax.fori_loop(1, n_plane, one, 0)

    def loop_z(step):
        def one(k, _):
            step(lax.rem(my_z + k, n_z))
            return 0

        lax.fori_loop(1, n_z, one, 0)

    @pl.when(my_p < owners)
    def _():
        p_in[my_p] = plane_buf[my_p]
        loop_plane(lambda p: from_plane(p).wait_recv())
        acc = p_in[0].astype(F32)
        for j in range(1, n_plane):
            acc = acc + p_in[j].astype(F32)
        z_out[...] = acc.astype(BF16)
        loop_z(lambda z: along_z(z, my_z).start())
        z_in[my_z] = z_out[...]
        loop_z(lambda z: along_z(z, z).wait_recv())
        acc = z_in[0].astype(F32)
        for j in range(1, n_z):
            acc = acc + z_in[j].astype(F32)
        half_buf[my_p] = acc.astype(BF16)
        loop_plane(lambda p: spread(p, my_p).start())

    def arrive(p):
        @pl.when(p < owners)
        def _():
            spread(p, p).wait_recv()

    loop_plane(arrive)
    back = remote(half_buf, last_in, cs_sem.at[1], cr_sem.at[1], partner)
    back.start()
    flat = (owners * rows_each, MID)
    total_out[:, mine] = half_buf[...].astype(F32).reshape(flat) * grad_scale
    back.wait_recv()
    total_out[:, other] = last_in[...].astype(F32).reshape(flat) * grad_scale

    for g in range(CHUNKS):
        lead_row(g).wait_send()
        trail_row(g).wait_send()
    for copy in lead + trail + (swap, back):
        copy.wait_send()

    def sent(p):
        @pl.when(p < owners)
        def _():
            scatter(p, my_p).wait_send()

    loop_plane(sent)

    @pl.when(my_p < owners)
    def _():
        loop_z(lambda z: along_z(z, my_z).wait_send())
        loop_plane(lambda p: spread(p, my_p).wait_send())


def finish_kernel(res, gin, total, *refs):
    outs, (b0, b1, w0, w1, v0, v1, v2, t0, sems) = refs[:9], refs[9:]
    w0[...] = total[0:WIDTH, : 3 * WIDTH]
    w1[...] = total[0:WIDTH, 3 * WIDTH :]
    b0[...] = total[WIDTH : WIDTH + 1, : 3 * WIDTH].reshape(3 * WIDTH)
    v0[...] = total[WIDTH : WIDTH + 1, 3 * WIDTH :].reshape(WIDTH)
    v1[...] = total[WIDTH + 1 : WIDTH + 2, :WIDTH].reshape(WIDTH)
    v2[...] = total[WIDTH + 1 : WIDTH + 2, WIDTH : 2 * WIDTH].reshape(WIDTH)
    t0[...] = total[WIDTH + 2 : WIDTH + 2 + HEADS, :RELS]
    copies = [
        pltpu.make_async_copy(src, dst, sems.at[i])
        for i, (src, dst) in enumerate(zip((res, gin, w0, b0, w1, v0, v1, v2, t0), outs))
    ]
    for copy in copies:
        copy.start()
    for copy in copies:
        copy.wait()


def shards(image, cotangent, qkv_weight, qkv_bias, proj_weight, proj_bias, norm_gain, norm_bias,
           bias_table):
    n_row, n_col = lax.axis_size("row"), lax.axis_size("col")
    spp = -(-STRIPES // n_col)
    owners = -(-STRIPES // spp)
    rows_each = spp * 16
    factor = float(n_row * n_col * TOKENS_HERE) ** (-0.5)
    args = (image, cotangent, qkv_weight, qkv_bias, proj_weight, proj_bias, norm_gain, norm_bias,
            bias_table)
    tile = jax.ShapeDtypeStruct(image.shape, BF16)
    vmem = pl.BlockSpec(memory_space=pltpu.VMEM)
    hbm = pl.BlockSpec(memory_space=pltpu.HBM)
    dma = pltpu.SemaphoreType.DMA
    row_halo = pltpu.VMEM((CHUNKS, 16, HALF), BF16)
    col_halo = pltpu.VMEM((16, EDGE), BF16)
    half = (owners * rows_each, MID)
    halves = (owners, rows_each, MID)
    stripe = (rows_each, MID)
    parts = pl.pallas_call(
        functools.partial(block_kernel, n_row, n_col, spp, factor),
        out_shape=(tile, tile, jax.ShapeDtypeStruct((owners * rows_each, WIDE), F32)),
        in_specs=[hbm] * 9,
        out_specs=(vmem,) * 3,
        scratch_shapes=[pltpu.VMEM(a.shape, a.dtype) for a in args]
        + [row_halo, col_halo, row_halo, col_halo, col_halo] * 2
        + [
            pltpu.VMEM((WIN, LANES + EDGE), F32), pltpu.VMEM((WIN, LANES + EDGE), F32),
            pltpu.VMEM((2, WIN, EDGE), F32),
            pltpu.VMEM((3, WIDTH, WIDTH), BF16),
            pltpu.VMEM((4, TOKENS_HERE, WIDTH), BF16),
            pltpu.VMEM((TOKENS_HERE, WIDTH), BF16),
            pltpu.VMEM((TOKENS_HERE, WIDTH), BF16),
            pltpu.VMEM((6, WIN, WIDTH), F32),
            pltpu.VMEM((CELLS, HEADS * CELLS), F32),
            pltpu.VMEM((2, CELLS, HEADS * CELLS), F32),
            pltpu.VMEM((WIN, 256, 128), BF16),
            pltpu.VMEM((8, 256), F32),
            pltpu.VMEM((HEADS, WIN, 128), F32),
            pltpu.VMEM((owners * rows_each, WIDE), F32),
            pltpu.VMEM(half, BF16), pltpu.VMEM(half, BF16),
            pltpu.VMEM(halves, BF16), pltpu.VMEM((n_col,) + stripe, BF16),
            pltpu.VMEM(stripe, BF16), pltpu.VMEM((n_row // 2,) + stripe, BF16),
            pltpu.VMEM(halves, BF16), pltpu.VMEM(halves, BF16),
            dma((9,)), dma((2 * CHUNKS + 4,)), dma((2 * CHUNKS + 4,)), dma((2,)), dma((2,)),
            dma((n_col,)), dma((n_col,)), dma((n_row // 2,)), dma((n_row // 2,)),
            dma((n_col,)), dma((n_col,)),
            pltpu.SemaphoreType.REGULAR((CHUNKS,)), pltpu.SemaphoreType.REGULAR((CHUNKS,)),
            pltpu.SemaphoreType.REGULAR,
        ],
        compiler_params=pltpu.CompilerParams(
            collective_id=1, has_side_effects=True, vmem_limit_bytes=60 * 1024 * 1024),
    )(*args)
    shapes = (image, cotangent, (WIDTH, 3 * WIDTH), (3 * WIDTH,), (WIDTH, WIDTH), (WIDTH,),
              (WIDTH,), (WIDTH,), (HEADS, RELS))
    outs = (tile, tile) + tuple(jax.ShapeDtypeStruct(s, F32) for s in shapes[2:])
    stage = [shapes[3], (1,), shapes[2], shapes[4], shapes[5], shapes[6], shapes[7], shapes[8]]
    return pl.pallas_call(
        finish_kernel,
        out_shape=outs,
        in_specs=[vmem] * 3,
        out_specs=(hbm,) * 9,
        scratch_shapes=[pltpu.VMEM(s, F32) for s in stage] + [dma((9,))],
        compiler_params=pltpu.CompilerParams(vmem_limit_bytes=60 * 1024 * 1024),
    )(*parts)


def solution(mesh):
    in_specs = (P("row", "col"), P("row", "col"), P(), P(), P(), P(), P(), P(), P())
    out_specs = (P("row", "col"), P("row", "col"), P(), P(), P(), P(), P(), P(), P())
    return jax.shard_map(shards, mesh=mesh, in_specs=in_specs, out_specs=out_specs, check_vma=False)
```

```python
import functools

import jax
import jax.numpy as jnp
from jax import lax
from jax.experimental import pallas as pl
from jax.experimental.pallas import tpu as pltpu
from jax.sharding import PartitionSpec as P

WIDTH = 192
HEADS = 6
HEAD_DIM = 32
WIN = 8
CELLS = WIN * WIN
SHIFT = 4
RELS = 225
EPS = 1e-05
NEG = -1e30
TILE_COLS = 64
LANES = TILE_COLS * WIDTH
EDGE = SHIFT * WIDTH
WINDOWS = TILE_COLS // WIN
SPAN = WIN * WIDTH
TOKENS_HERE = WINDOWS * CELLS
CHUNKS = 2
PER_CHUNK = WINDOWS // CHUNKS
CHUNK_TOKENS = PER_CHUNK * CELLS
CHUNK = PER_CHUNK * SPAN
HALF = CHUNK // 2
SCALE = HEAD_DIM**-0.5
GROUPS = ((0, 4), (4, 2))
STRIPES = 13
WIDE = 4 * WIDTH
MID = WIDE // 2

MESH = pl.DeviceIdType.MESH
F32 = jnp.float32
BF16 = jnp.bfloat16


def dot(a, b, ca=1, cb=0):
    return lax.dot_general(a, b, (((ca,), (cb,)), ((), ())), preferred_element_type=F32)


def iota(shape, dim):
    return lax.broadcasted_iota(jnp.int32, shape, dim)


def upper(shape):
    return iota(shape, 0) < SHIFT


def pack_rows(field):
    back = pltpu.roll(field[:, HALF:], SHIFT, 0)
    return jnp.where(upper((WIN, HALF)), field[:, :HALF], back)


def merge_rows(packed, field):
    low = jnp.where(upper((WIN, HALF)), packed, field[:, :HALF])
    high = jnp.where(upper((WIN, HALF)), pltpu.roll(packed, SHIFT, 0), field[:, HALF:])
    return jnp.concatenate([low, high], 1)


def split_tokens(strip):
    left = iota((WIN, 128), 1) < 64
    first, second = [], []
    for j in range(WIN // 2):
        v = [strip[:, (3 * j + i) * 128 : (3 * j + i + 1) * 128] for i in range(3)]
        r1, r2 = pltpu.roll(v[1], 64, 1), pltpu.roll(v[2], 64, 1)
        first += [v[0], jnp.where(left, r1, r2)]
        second += [v[1], r2]
    return jnp.concatenate(first, 0), jnp.concatenate(second, 0)


def join_tokens(first, second):
    left = iota((WIN, 128), 1) < 64
    out = []
    for j in range(WIN // 2):
        e = slice(16 * j, 16 * j + 8)
        o = slice(16 * j + 8, 16 * j + 16)
        swapped = pltpu.roll(first[o], 64, 1)
        out.append(first[e])
        out.append(jnp.where(left, second[e], swapped))
        out.append(jnp.where(left, swapped, pltpu.roll(second[o], 64, 1)))
    return jnp.concatenate(out, 1)


def build_bias(table_ref, onehot, padded, diag, bias, last_row, last_col):
    padded[...] = jnp.zeros((8, 256), F32)
    padded[0:HEADS, 0:RELS] = table_ref[...]
    table = padded[...]
    hi = table.astype(BF16)
    rest = table - hi.astype(F32)
    mid = rest.astype(BF16)
    low = (rest - mid.astype(F32)).astype(BF16)
    lane = iota((1, 128), 1)
    a_q = (lane + SHIFT) % WIN
    for a in range(WIN):
        target = (a_q - (a + SHIFT) % WIN + WIN - 1) * (2 * WIN - 1) + lane // WIN
        target = jnp.where(lane < 120, target, -1)
        hot = jnp.where(iota((256, 128), 0) == target, 1.0, 0.0).astype(BF16)
        onehot[a] = hot
        rows = dot(hi, hot) + dot(mid, hot) + dot(low, hot)
        for h in range(HEADS):
            diag[h, a : a + 1, :] = rows[h : h + 1, :]
    sub = iota((WIN, 128), 0)
    lanes = iota((WIN, 128), 1)
    row_cut = jnp.where((sub < SHIFT) != (lanes % WIN < SHIFT), NEG, 0.0) * last_row
    right = lanes % 64 // WIN >= SHIFT
    for b in range(WIN):
        col_cut = jnp.where(right != (b >= SHIFT), NEG, 0.0) * last_col
        for pair in range(HEADS // 2):
            shift = (WIN - 1 - b) * WIN
            even = pltpu.roll(diag[2 * pair], (128 - shift) % 128, 1)
            odd = pltpu.roll(diag[2 * pair + 1], (192 - shift) % 128, 1)
            block = jnp.where(lanes < 64, even, odd) + row_cut
            where = (slice(b * WIN, b * WIN + WIN), slice(pair * 128, pair * 128 + 128))
            bias[(0,) + where] = block
            bias[(1,) + where] = block + col_cut


def table_grad(total, onehot, diag):
    lanes = iota((WIN, 128), 1)
    for h in range(HEADS):
        mine = (lanes < 64) == (h % 2 == 0)
        acc = jnp.zeros((WIN, 128), F32)
        for b in range(WIN):
            block = total[b * WIN : b * WIN + WIN, h // 2 * 128 : h // 2 * 128 + 128]
            block = jnp.where(mine, block, 0.0)
            acc = acc + pltpu.roll(block, ((WIN - 1 - b) * WIN + h % 2 * 64) % 128, 1)
        diag[h] = acc
    flat = jnp.concatenate([diag[h] for h in range(HEADS)], 0)
    hi = flat.astype(BF16)
    low = (flat - hi.astype(F32)).astype(BF16)
    sub = iota((HEADS * WIN, 256), 0) % WIN
    acc = jnp.zeros((HEADS * WIN, 256), F32)
    for a in range(WIN):
        part = dot(hi, onehot[a], 1, 1) + dot(low, onehot[a], 1, 1)
        acc = acc + jnp.where(sub == a, part, 0.0)
    return [
        jnp.sum(acc[h * WIN : h * WIN + WIN], 0, keepdims=True) for h in range(HEADS)
    ]


def masked_heads(x, group):
    start, count = group
    lane = iota((CELLS, count * HEAD_DIM), 1) // HEAD_DIM
    wide = x[:, start * HEAD_DIM : (start + count) * HEAD_DIM]
    zero = jnp.zeros_like(wide)
    return jnp.concatenate([jnp.where(lane == h, wide, zero) for h in range(count)], 0)


def own_heads(x, count):
    lane = iota((CELLS, count * HEAD_DIM), 1) // HEAD_DIM
    out = x[(count - 1) * CELLS : count * CELLS]
    for h in range(count - 1):
        out = jnp.where(lane == h, x[h * CELLS : (h + 1) * CELLS], out)
    return out


def fold(x):
    return jnp.sum(x.reshape(-1, WIN, x.shape[1]), 0)


def window_step(q, k, v, da, bias, gsum):
    att, dq, dk, dv = [], [], [], []
    for start, count in GROUPS:
        ch = slice(start * HEAD_DIM, (start + count) * HEAD_DIM)
        lanes = slice(start * CELLS, (start + count) * CELLS)
        qm = masked_heads(q, (start, count))
        dam = masked_heads(da, (start, count))
        s = dot(k[:, ch], qm, 1, 1) * SCALE + bias[:, lanes]
        e = jnp.exp(s - jnp.max(s, 0, keepdims=True))
        p = e * (1.0 / jnp.sum(e, 0, keepdims=True))
        dp = dot(v[:, ch], dam, 1, 1)
        ds = p * (dp - jnp.sum(p * dp, 0, keepdims=True))
        gsum[:, lanes] += ds
        pb, dsb = p.astype(BF16), ds.astype(BF16)
        dv.append(dot(pb, dam))
        dk.append(dot(dsb, qm) * SCALE)
        att.append(own_heads(dot(pb, v[:, ch], 0, 0), count).astype(BF16))
        dq.append(own_heads(dot(dsb, k[:, ch], 0, 0), count) * SCALE)
    return [jnp.concatenate(parts, 1) for parts in (att, dq, dk, dv)]


def block_kernel(n_row, n_col, spp, grad_scale, *refs):
    (img_h, cot_h, wqkv_h, bqkv_h, wproj_h, bproj_h, gain_h, shift_h, table_h,
     res, gin, total_out,
     img, cot, wqkv, bqkv, wproj, bproj, gain_ref, shift_ref, table_ref,
     irow, icol, hrow, hcol, hdiag, orow, ocol, rrow, rcol, rdiag,
     field, cfield, corner, weights, xs, cs, dh, xd, xhid, xatt, sums, gsum,
     bias, onehot, padded, diag, gs, c_out, c_in, plane_buf, p_in, z_out, z_in, half_buf, last_in,
     ls, hs, hr, cs_sem, cr_sem, ps, pr, zs, zr, as_sem, ar_sem,
     row_known, col_known, pair_known) = refs
    my_r, my_c = lax.axis_index("row"), lax.axis_index("col")
    above, below = lax.rem(my_r + n_row - 1, n_row), lax.rem(my_r + 1, n_row)
    left, right = lax.rem(my_c + n_col - 1, n_col), lax.rem(my_c + 1, n_col)
    n_plane, n_z = n_col, n_row // 2
    core = lax.rem(my_c, 2)
    my_p = my_c // 2 * 2 + lax.rem(my_r, 2)
    my_z = my_r // 2
    owners = -(-STRIPES // spp)
    rows_each = spp * 16

    def plane_peer(p):
        return (my_z * 2 + lax.rem(p, 2), p // 2 * 2 + core)

    def z_peer(z):
        return (z * 2 + lax.rem(my_r, 2), my_c)

    local = [
        pltpu.make_async_copy(src, dst, ls.at[i])
        for i, (src, dst) in enumerate((
            (img_h, img), (cot_h, cot), (wqkv_h, wqkv), (bqkv_h, bqkv), (wproj_h, wproj),
            (bproj_h, bproj), (gain_h, gain_ref), (shift_h, shift_ref), (table_h, table_ref)))
    ]
    for copy in local:
        copy.start()
    barrier = pltpu.get_barrier_semaphore()

    def greet(device):
        pl.semaphore_signal(barrier, inc=1, device_id=device, device_id_type=MESH)

    for device in ((above, my_c), (below, my_c), (my_r, left), (my_r, right), (above, left),
                   (below, right)):
        greet(device)

    rounds = [(g, 2**g) for g in range(4)]
    row_rounds = [(g, d) for g, d in rounds if 4 * d <= n_row]
    col_rounds = [(g, d) for g, d in rounds if 4 * d <= n_col]

    def tell(sem, device):
        pl.semaphore_signal(sem, inc=1, device_id=device, device_id_type=MESH)

    def start_round(g):
        for k, d in row_rounds:
            @pl.when(g == k)
            def _():
                tell(row_known.at[k], (lax.rem(my_r + d, n_row), my_c))
                tell(row_known.at[k], (lax.rem(my_r + n_row - d, n_row), my_c))

        for k, d in col_rounds:
            @pl.when(g == k)
            def _():
                tell(col_known.at[k], (my_r, lax.rem(my_c + d, n_col)))
                tell(col_known.at[k], (my_r, lax.rem(my_c + n_col - d, n_col)))

        @pl.when(g == 3)
        def _():
            tell(pair_known, (my_r + 1 - 2 * lax.rem(my_r, 2), my_c))

    def end_round(g):
        for known, known_rounds in ((row_known, row_rounds), (col_known, col_rounds)):
            for k, _ in known_rounds:
                if k < 3:
                    @pl.when(g == k)
                    def _():
                        pl.semaphore_wait(known.at[k], 2)

    def remote(src, dst, send, recv, device):
        return pltpu.make_async_remote_copy(
            src_ref=src, dst_ref=dst, send_sem=send, recv_sem=recv, device_id=device,
            device_id_type=MESH)

    def halo(src, dst, i, device):
        return remote(src, dst, hs.at[i], hr.at[i], device)

    def lead_row(g):
        return halo(irow.at[g], hrow.at[g], g, (above, my_c))

    def trail_row(g):
        return halo(orow.at[g], rrow.at[g], CHUNKS + g, (below, my_c))

    n = 2 * CHUNKS
    lead = (halo(icol, hcol, n, (my_r, left)), halo(icol, hdiag, n + 1, (above, left)))
    trail = (halo(ocol, rcol, n + 2, (my_r, right)), halo(ocol, rdiag, n + 3, (below, right)))

    local[0].wait()
    local[1].wait()
    for i, (src, dst) in enumerate(((img, field), (cot, cfield))):
        half = slice(i * WIN, i * WIN + WIN)
        tile = src[...].astype(F32)
        icol[half, :] = tile[:, :EDGE].astype(BF16)
        dst[:, :LANES] = tile
        dst[:, LANES:] = tile[:, :EDGE]
        for g in range(CHUNKS):
            lanes = slice(EDGE + g * CHUNK, EDGE + (g + 1) * CHUNK)
            irow[g, half, :] = pack_rows(dst[:, lanes]).astype(BF16)
    pl.semaphore_wait(barrier, 6)
    for g in range(CHUNKS):
        lead_row(g).start()
    for copy in lead:
        copy.start()
    start_round(0)

    for copy in local[2:]:
        copy.wait()
    last_row = (my_r == n_row - 1).astype(F32)
    last_col = (my_c == n_col - 1).astype(F32)
    build_bias(table_ref, onehot, padded, diag, bias, last_row, last_col)
    gsum[...] = jnp.zeros_like(gsum)
    sums[...] = jnp.zeros_like(sums)
    gs[WIDTH:, :] = jnp.zeros((owners * rows_each - WIDTH, WIDE), F32)
    for i in range(3):
        weights[i] = wqkv[:, i * WIDTH : (i + 1) * WIDTH]
    qkv_bias = bqkv[...].reshape(1, 3 * WIDTH)
    biases = [qkv_bias[:, i * WIDTH : (i + 1) * WIDTH] for i in range(3)]
    proj_bias = bproj[...].reshape(1, WIDTH)
    gain = gain_ref[...].reshape(1, WIDTH)
    shift = shift_ref[...].reshape(1, WIDTH)

    for copy in lead:
        copy.wait_recv()
    for i in range(2):
        half = slice(i * WIN, i * WIN + WIN)
        corner[i] = jnp.where(
            upper((WIN, EDGE)), hdiag[half, :].astype(F32), hcol[half, :].astype(F32))

    def chunk_step(g, _):
        final = g == CHUNKS - 1
        lanes = pl.ds(pl.multiple_of(EDGE + g * CHUNK, 128), CHUNK)
        rows = pl.ds(pl.multiple_of(g * CHUNK_TOKENS, CHUNK_TOKENS), CHUNK_TOKENS)
        lead_row(g).wait_recv()
        tokens = []
        for i, src in enumerate((field, cfield)):
            half = slice(i * WIN, i * WIN + WIN)
            whole = merge_rows(hrow[g, half, :].astype(F32), src[:, lanes])
            end = jnp.where(final, corner[i], whole[:, CHUNK - EDGE :])
            whole = jnp.concatenate([whole[:, : CHUNK - EDGE], end], 1)
            parts = [split_tokens(whole[:, j * SPAN : (j + 1) * SPAN]) for j in range(PER_CHUNK)]
            first = jnp.concatenate([part[0] for part in parts], 0)
            second = jnp.concatenate([part[1] for part in parts], 0)
            tokens.append(jnp.concatenate([first, second[:, : WIDTH - 128]], 1))
        x, cot_f = tokens
        center = x - jnp.mean(x, 1, keepdims=True)
        inv_std = lax.rsqrt(jnp.mean(center * center, 1, keepdims=True) + EPS)
        normed = center * inv_std
        hidden = (normed * gain + shift).astype(BF16)
        xhid[rows, :] = hidden
        q, k, v = [(dot(hidden, weights[i]) + biases[i]).astype(BF16) for i in range(3)]
        cot_b = cot_f.astype(BF16)
        da = dot(cot_b, wproj[...], 1, 1).astype(BF16)
        found = []
        for j in range(PER_CHUNK):
            r = slice(j * CELLS, (j + 1) * CELLS)
            if j == PER_CHUNK - 1:
                add = bias.at[final.astype(jnp.int32)]
            else:
                add = bias.at[0]
            found.append(window_step(q[r], k[r], v[r], da[r], add, gsum))
        att, dq, dk, dv = [jnp.concatenate([part[i] for part in found], 0) for i in range(4)]
        xatt[rows, :] = att
        xs[rows, :] = x
        cs[rows, :] = cot_f
        d_hidden = jnp.zeros((CHUNK_TOKENS, WIDTH), F32)
        for i, part in enumerate((dq, dk, dv)):
            part_b = part.astype(BF16)
            xd[i, rows, :] = part_b
            sums[i] += fold(part)
            d_hidden = d_hidden + dot(part_b, weights[i], 1, 1)
        xd[3, rows, :] = cot_b
        sums[3] += fold(cot_f)
        sums[4] += fold(d_hidden * normed)
        sums[5] += fold(d_hidden)
        dh[rows, :] = d_hidden
        end_round(g + 1)
        start_round(g + 2)
        return 0

    end_round(0)
    start_round(1)
    lax.fori_loop(0, CHUNKS, chunk_step, 0)

    hidden_t = xhid[...].T
    for i in range(3):
        gs[0:WIDTH, i * WIDTH : (i + 1) * WIDTH] = dot(hidden_t, xd[i])
    gs[0:WIDTH, 3 * WIDTH :] = dot(xatt[...], xd[3], 0, 0)
    for i in range(4):
        gs[WIDTH : WIDTH + 1, i * WIDTH : (i + 1) * WIDTH] = jnp.sum(sums[i], 0, keepdims=True)
    for i in range(2):
        gs[WIDTH + 1 : WIDTH + 2, i * WIDTH : (i + 1) * WIDTH] = jnp.sum(
            sums[4 + i], 0, keepdims=True)
    for h, line in enumerate(table_grad(gsum[...], onehot, diag)):
        gs[WIDTH + 2 + h : WIDTH + 3 + h, 0:256] = line

    mine = pl.ds(pl.multiple_of(core * MID, 128), MID)
    other = pl.ds(pl.multiple_of((1 - core) * MID, 128), MID)
    partner = (my_r, my_c + 1 - 2 * core)
    c_out[...] = gs[:, other].astype(BF16)
    swap = remote(c_out, c_in, cs_sem.at[0], cr_sem.at[0], partner)
    swap.start()
    swap.wait_recv()
    plane_buf[...] = (gs[:, mine] + c_in[...].astype(F32)).astype(BF16).reshape(
        owners, rows_each, MID)

    def scatter(p, slot):
        return remote(plane_buf.at[p], p_in.at[slot], ps.at[p], pr.at[slot], plane_peer(p))

    def from_plane(p):
        return remote(plane_buf.at[0], p_in.at[p], ps.at[0], pr.at[p], plane_peer(p))

    def send_scatter(k, _):
        p = lax.rem(my_p + k, n_plane)

        @pl.when(p < owners)
        def _():
            scatter(p, my_p).start()

        return 0

    pl.semaphore_wait(pair_known, 1)
    lax.fori_loop(1, n_plane, send_scatter, 0)

    def output_step(g, _):
        lanes = pl.ds(pl.multiple_of(EDGE + g * CHUNK, 128), CHUNK)
        rows = pl.ds(pl.multiple_of(g * CHUNK_TOKENS, CHUNK_TOKENS), CHUNK_TOKENS)
        x, cot_f, d_hidden = xs[rows, :], cs[rows, :], dh[rows, :]
        center = x - jnp.mean(x, 1, keepdims=True)
        inv_std = lax.rsqrt(jnp.mean(center * center, 1, keepdims=True) + EPS)
        normed = center * inv_std
        out = x + dot(xatt[rows, :], wproj[...]) + proj_bias
        d_normed = d_hidden * gain
        d_tokens = cot_f + inv_std * (
            d_normed
            - jnp.mean(d_normed, 1, keepdims=True)
            - normed * jnp.mean(d_normed * normed, 1, keepdims=True))
        for i, (value, dst) in enumerate(((out, field), (d_tokens, cfield))):
            half = slice(i * WIN, i * WIN + WIN)
            first = value[:, :128]
            second = jnp.concatenate(
                [value[:, 128:], jnp.zeros((CHUNK_TOKENS, 256 - WIDTH), F32)], 1)
            strips = []
            for j in range(PER_CHUNK):
                r = slice(j * CELLS, (j + 1) * CELLS)
                strips.append(join_tokens(first[r], second[r]))
            whole = jnp.concatenate(strips, 1)
            dst[:, lanes] = whole
            orow[g, half, :] = pack_rows(whole).astype(BF16)
            ocol[half, :] = whole[:, CHUNK - EDGE :].astype(BF16)
        trail_row(g).start()
        return 0

    lax.fori_loop(0, CHUNKS, output_step, 0)
    for copy in trail:
        copy.start()

    def along_z(z, slot):
        return remote(z_out, z_in.at[slot], zs.at[z], zr.at[slot], z_peer(z))

    def spread(p, owner):
        return remote(half_buf.at[owner], half_buf.at[owner], as_sem.at[p], ar_sem.at[owner],
                      plane_peer(p))

    def loop_plane(step):
        def one(k, _):
            step(lax.rem(my_p + k, n_plane))
            return 0

        lax.fori_loop(1, n_plane, one, 0)

    def loop_z(step):
        def one(k, _):
            step(lax.rem(my_z + k, n_z))
            return 0

        lax.fori_loop(1, n_z, one, 0)

    @pl.when(my_p < owners)
    def _():
        p_in[my_p] = plane_buf[my_p]
        loop_plane(lambda p: from_plane(p).wait_recv())
        acc = p_in[0].astype(F32)
        for j in range(1, n_plane):
            acc = acc + p_in[j].astype(F32)
        z_out[...] = acc.astype(BF16)

    if len(row_rounds) > 3:
        pl.semaphore_wait(row_known.at[3], 2)

    @pl.when(my_p < owners)
    def _():
        loop_z(lambda z: along_z(z, my_z).start())
        z_in[my_z] = z_out[...]

    for g in range(CHUNKS):
        trail_row(g).wait_recv()
    for copy in trail:
        copy.wait_recv()
    for i, (src, dst) in enumerate(((field, res), (cfield, gin))):
        half = slice(i * WIN, i * WIN + WIN)
        ends = jnp.where(
            upper((WIN, EDGE)), rdiag[half, :].astype(F32), rcol[half, :].astype(F32))
        dst[:, :EDGE] = ends.astype(BF16)
        for g in range(CHUNKS):
            start = EDGE + g * CHUNK
            size = min(CHUNK, LANES - start)
            whole = merge_rows(rrow[g, half, :].astype(F32), src[:, start : start + CHUNK])
            dst[:, start : start + size] = whole[:, :size].astype(BF16)

    @pl.when(my_p < owners)
    def _():
        loop_z(lambda z: along_z(z, z).wait_recv())
        acc = z_in[0].astype(F32)
        for j in range(1, n_z):
            acc = acc + z_in[j].astype(F32)
        half_buf[my_p] = acc.astype(BF16)
        loop_plane(lambda p: spread(p, my_p).start())

    def arrive(p):
        @pl.when(p < owners)
        def _():
            spread(p, p).wait_recv()

    loop_plane(arrive)
    back = remote(half_buf, last_in, cs_sem.at[1], cr_sem.at[1], partner)
    back.start()
    flat = (owners * rows_each, MID)
    total_out[:, mine] = half_buf[...].astype(F32).reshape(flat) * grad_scale
    back.wait_recv()
    total_out[:, other] = last_in[...].astype(F32).reshape(flat) * grad_scale

    for g in range(CHUNKS):
        lead_row(g).wait_send()
        trail_row(g).wait_send()
    for copy in lead + trail + (swap, back):
        copy.wait_send()

    def sent(p):
        @pl.when(p < owners)
        def _():
            scatter(p, my_p).wait_send()

    loop_plane(sent)

    @pl.when(my_p < owners)
    def _():
        loop_z(lambda z: along_z(z, my_z).wait_send())
        loop_plane(lambda p: spread(p, my_p).wait_send())


def finish_kernel(res, gin, total, *refs):
    outs, (b0, b1, w0, w1, v0, v1, v2, t0, sems) = refs[:9], refs[9:]
    w0[...] = total[0:WIDTH, : 3 * WIDTH]
    w1[...] = total[0:WIDTH, 3 * WIDTH :]
    b0[...] = total[WIDTH : WIDTH + 1, : 3 * WIDTH].reshape(3 * WIDTH)
    v0[...] = total[WIDTH : WIDTH + 1, 3 * WIDTH :].reshape(WIDTH)
    v1[...] = total[WIDTH + 1 : WIDTH + 2, :WIDTH].reshape(WIDTH)
    v2[...] = total[WIDTH + 1 : WIDTH + 2, WIDTH : 2 * WIDTH].reshape(WIDTH)
    t0[...] = total[WIDTH + 2 : WIDTH + 2 + HEADS, :RELS]
    copies = [
        pltpu.make_async_copy(src, dst, sems.at[i])
        for i, (src, dst) in enumerate(zip((res, gin, w0, b0, w1, v0, v1, v2, t0), outs))
    ]
    for copy in copies:
        copy.start()
    for copy in copies:
        copy.wait()


def shards(image, cotangent, qkv_weight, qkv_bias, proj_weight, proj_bias, norm_gain, norm_bias,
           bias_table):
    n_row, n_col = lax.axis_size("row"), lax.axis_size("col")
    spp = -(-STRIPES // n_col)
    owners = -(-STRIPES // spp)
    rows_each = spp * 16
    factor = float(n_row * n_col * TOKENS_HERE) ** (-0.5)
    args = (image, cotangent, qkv_weight, qkv_bias, proj_weight, proj_bias, norm_gain, norm_bias,
            bias_table)
    tile = jax.ShapeDtypeStruct(image.shape, BF16)
    vmem = pl.BlockSpec(memory_space=pltpu.VMEM)
    hbm = pl.BlockSpec(memory_space=pltpu.HBM)
    dma = pltpu.SemaphoreType.DMA
    row_halo = pltpu.VMEM((CHUNKS, 16, HALF), BF16)
    col_halo = pltpu.VMEM((16, EDGE), BF16)
    half = (owners * rows_each, MID)
    halves = (owners, rows_each, MID)
    stripe = (rows_each, MID)
    parts = pl.pallas_call(
        functools.partial(block_kernel, n_row, n_col, spp, factor),
        out_shape=(tile, tile, jax.ShapeDtypeStruct((owners * rows_each, WIDE), F32)),
        in_specs=[hbm] * 9,
        out_specs=(vmem,) * 3,
        scratch_shapes=[pltpu.VMEM(a.shape, a.dtype) for a in args]
        + [row_halo, col_halo, row_halo, col_halo, col_halo] * 2
        + [
            pltpu.VMEM((WIN, LANES + EDGE), F32), pltpu.VMEM((WIN, LANES + EDGE), F32),
            pltpu.VMEM((2, WIN, EDGE), F32),
            pltpu.VMEM((3, WIDTH, WIDTH), BF16),
            pltpu.VMEM((TOKENS_HERE, WIDTH), F32),
            pltpu.VMEM((TOKENS_HERE, WIDTH), F32),
            pltpu.VMEM((TOKENS_HERE, WIDTH), F32),
            pltpu.VMEM((4, TOKENS_HERE, WIDTH), BF16),
            pltpu.VMEM((TOKENS_HERE, WIDTH), BF16),
            pltpu.VMEM((TOKENS_HERE, WIDTH), BF16),
            pltpu.VMEM((6, WIN, WIDTH), F32),
            pltpu.VMEM((CELLS, HEADS * CELLS), F32),
            pltpu.VMEM((2, CELLS, HEADS * CELLS), F32),
            pltpu.VMEM((WIN, 256, 128), BF16),
            pltpu.VMEM((8, 256), F32),
            pltpu.VMEM((HEADS, WIN, 128), F32),
            pltpu.VMEM((owners * rows_each, WIDE), F32),
            pltpu.VMEM(half, BF16), pltpu.VMEM(half, BF16),
            pltpu.VMEM(halves, BF16), pltpu.VMEM((n_col,) + stripe, BF16),
            pltpu.VMEM(stripe, BF16), pltpu.VMEM((n_row // 2,) + stripe, BF16),
            pltpu.VMEM(halves, BF16), pltpu.VMEM(halves, BF16),
            dma((9,)), dma((2 * CHUNKS + 4,)), dma((2 * CHUNKS + 4,)), dma((2,)), dma((2,)),
            dma((n_col,)), dma((n_col,)), dma((n_row // 2,)), dma((n_row // 2,)),
            dma((n_col,)), dma((n_col,)),
            pltpu.SemaphoreType.REGULAR((4,)), pltpu.SemaphoreType.REGULAR((4,)),
            pltpu.SemaphoreType.REGULAR,
        ],
        compiler_params=pltpu.CompilerParams(
            collective_id=1, has_side_effects=True, vmem_limit_bytes=60 * 1024 * 1024),
    )(*args)
    shapes = (image, cotangent, (WIDTH, 3 * WIDTH), (3 * WIDTH,), (WIDTH, WIDTH), (WIDTH,),
              (WIDTH,), (WIDTH,), (HEADS, RELS))
    outs = (tile, tile) + tuple(jax.ShapeDtypeStruct(s, F32) for s in shapes[2:])
    stage = [shapes[3], (1,), shapes[2], shapes[4], shapes[5], shapes[6], shapes[7], shapes[8]]
    return pl.pallas_call(
        finish_kernel,
        out_shape=outs,
        in_specs=[vmem] * 3,
        out_specs=(hbm,) * 9,
        scratch_shapes=[pltpu.VMEM(s, F32) for s in stage] + [dma((9,))],
        compiler_params=pltpu.CompilerParams(vmem_limit_bytes=60 * 1024 * 1024),
    )(*parts)


def solution(mesh):
    in_specs = (P("row", "col"), P("row", "col"), P(), P(), P(), P(), P(), P(), P())
    out_specs = (P("row", "col"), P("row", "col"), P(), P(), P(), P(), P(), P(), P())
    return jax.shard_map(shards, mesh=mesh, in_specs=in_specs, out_specs=out_specs, check_vma=False)
```

```python
import functools

import jax
import jax.numpy as jnp
from jax import lax
from jax.experimental import pallas as pl
from jax.experimental.pallas import tpu as pltpu
from jax.sharding import PartitionSpec as P

WIDTH = 192
HEADS = 6
HEAD_DIM = 32
WIN = 8
CELLS = WIN * WIN
SHIFT = 4
RELS = 225
EPS = 1e-05
NEG = -1e30
TILE_COLS = 64
LANES = TILE_COLS * WIDTH
EDGE = SHIFT * WIDTH
WINDOWS = TILE_COLS // WIN
SPAN = WIN * WIDTH
TOKENS_HERE = WINDOWS * CELLS
CHUNKS = 2
LOOSE = False
PER_CHUNK = WINDOWS // CHUNKS
CHUNK_TOKENS = PER_CHUNK * CELLS
CHUNK = PER_CHUNK * SPAN
HALF = CHUNK // 2
SCALE = HEAD_DIM**-0.5
GROUPS = ((0, 4), (4, 2))
STRIPES = 13
WIDE = 4 * WIDTH
MID = WIDE // 2

MESH = pl.DeviceIdType.MESH
F32 = jnp.float32
BF16 = jnp.bfloat16


def dot(a, b, ca=1, cb=0):
    return lax.dot_general(a, b, (((ca,), (cb,)), ((), ())), preferred_element_type=F32)


def iota(shape, dim):
    return lax.broadcasted_iota(jnp.int32, shape, dim)


def upper(shape):
    return iota(shape, 0) < SHIFT


def pack_rows(field):
    back = pltpu.roll(field[:, HALF:], SHIFT, 0)
    return jnp.where(upper((WIN, HALF)), field[:, :HALF], back)


def merge_rows(packed, field):
    low = jnp.where(upper((WIN, HALF)), packed, field[:, :HALF])
    high = jnp.where(upper((WIN, HALF)), pltpu.roll(packed, SHIFT, 0), field[:, HALF:])
    return jnp.concatenate([low, high], 1)


def split_tokens(strip):
    left = iota((WIN, 128), 1) < 64
    first, second = [], []
    for j in range(WIN // 2):
        v = [strip[:, (3 * j + i) * 128 : (3 * j + i + 1) * 128] for i in range(3)]
        r1, r2 = pltpu.roll(v[1], 64, 1), pltpu.roll(v[2], 64, 1)
        first += [v[0], jnp.where(left, r1, r2)]
        second += [v[1], r2]
    return jnp.concatenate(first, 0), jnp.concatenate(second, 0)


def join_tokens(first, second):
    left = iota((WIN, 128), 1) < 64
    out = []
    for j in range(WIN // 2):
        e = slice(16 * j, 16 * j + 8)
        o = slice(16 * j + 8, 16 * j + 16)
        swapped = pltpu.roll(first[o], 64, 1)
        out.append(first[e])
        out.append(jnp.where(left, second[e], swapped))
        out.append(jnp.where(left, swapped, pltpu.roll(second[o], 64, 1)))
    return jnp.concatenate(out, 1)


def build_bias(table_ref, onehot, padded, diag, bias, last_row, last_col):
    padded[...] = jnp.zeros((8, 256), F32)
    padded[0:HEADS, 0:RELS] = table_ref[...]
    table = padded[...]
    hi = table.astype(BF16)
    rest = table - hi.astype(F32)
    mid = rest.astype(BF16)
    low = (rest - mid.astype(F32)).astype(BF16)
    lane = iota((1, 128), 1)
    a_q = (lane + SHIFT) % WIN
    for a in range(WIN):
        target = (a_q - (a + SHIFT) % WIN + WIN - 1) * (2 * WIN - 1) + lane // WIN
        target = jnp.where(lane < 120, target, -1)
        hot = jnp.where(iota((256, 128), 0) == target, 1.0, 0.0).astype(BF16)
        onehot[a] = hot
        rows = dot(hi, hot) + dot(mid, hot) + dot(low, hot)
        for h in range(HEADS):
            diag[h, a : a + 1, :] = rows[h : h + 1, :]
    sub = iota((WIN, 128), 0)
    lanes = iota((WIN, 128), 1)
    row_cut = jnp.where((sub < SHIFT) != (lanes % WIN < SHIFT), NEG, 0.0) * last_row
    right = lanes % 64 // WIN >= SHIFT
    for b in range(WIN):
        col_cut = jnp.where(right != (b >= SHIFT), NEG, 0.0) * last_col
        for pair in range(HEADS // 2):
            shift = (WIN - 1 - b) * WIN
            even = pltpu.roll(diag[2 * pair], (128 - shift) % 128, 1)
            odd = pltpu.roll(diag[2 * pair + 1], (192 - shift) % 128, 1)
            block = jnp.where(lanes < 64, even, odd) + row_cut
            where = (slice(b * WIN, b * WIN + WIN), slice(pair * 128, pair * 128 + 128))
            bias[(0,) + where] = block
            bias[(1,) + where] = block + col_cut


def table_grad(total, onehot, diag):
    lanes = iota((WIN, 128), 1)
    for h in range(HEADS):
        mine = (lanes < 64) == (h % 2 == 0)
        acc = jnp.zeros((WIN, 128), F32)
        for b in range(WIN):
            block = total[b * WIN : b * WIN + WIN, h // 2 * 128 : h // 2 * 128 + 128]
            block = jnp.where(mine, block, 0.0)
            acc = acc + pltpu.roll(block, ((WIN - 1 - b) * WIN + h % 2 * 64) % 128, 1)
        diag[h] = acc
    flat = jnp.concatenate([diag[h] for h in range(HEADS)], 0)
    hi = flat.astype(BF16)
    low = (flat - hi.astype(F32)).astype(BF16)
    sub = iota((HEADS * WIN, 256), 0) % WIN
    acc = jnp.zeros((HEADS * WIN, 256), F32)
    for a in range(WIN):
        part = dot(hi, onehot[a], 1, 1) + dot(low, onehot[a], 1, 1)
        acc = acc + jnp.where(sub == a, part, 0.0)
    return [
        jnp.sum(acc[h * WIN : h * WIN + WIN], 0, keepdims=True) for h in range(HEADS)
    ]


def masked_heads(x, group):
    start, count = group
    lane = iota((CELLS, count * HEAD_DIM), 1) // HEAD_DIM
    wide = x[:, start * HEAD_DIM : (start + count) * HEAD_DIM]
    zero = jnp.zeros_like(wide)
    return jnp.concatenate([jnp.where(lane == h, wide, zero) for h in range(count)], 0)


def own_heads(x, count):
    lane = iota((CELLS, count * HEAD_DIM), 1) // HEAD_DIM
    out = x[(count - 1) * CELLS : count * CELLS]
    for h in range(count - 1):
        out = jnp.where(lane == h, x[h * CELLS : (h + 1) * CELLS], out)
    return out


def fold(x):
    return jnp.sum(x.reshape(-1, WIN, x.shape[1]), 0)


def window_step(q, k, v, da, bias, gsum):
    att, dq, dk, dv = [], [], [], []
    for start, count in GROUPS:
        ch = slice(start * HEAD_DIM, (start + count) * HEAD_DIM)
        lanes = slice(start * CELLS, (start + count) * CELLS)
        qm = masked_heads(q, (start, count))
        dam = masked_heads(da, (start, count))
        s = dot(k[:, ch], qm, 1, 1) * SCALE + bias[:, lanes]
        e = jnp.exp(s - jnp.max(s, 0, keepdims=True))
        p = e * (1.0 / jnp.sum(e, 0, keepdims=True))
        dp = dot(v[:, ch], dam, 1, 1)
        ds = p * (dp - jnp.sum(p * dp, 0, keepdims=True))
        gsum[:, lanes] += ds
        pb, dsb = p.astype(BF16), ds.astype(BF16)
        dv.append(dot(pb, dam))
        dk.append(dot(dsb, qm) * SCALE)
        att.append(own_heads(dot(pb, v[:, ch], 0, 0), count).astype(BF16))
        dq.append(own_heads(dot(dsb, k[:, ch], 0, 0), count) * SCALE)
    return [jnp.concatenate(parts, 1) for parts in (att, dq, dk, dv)]


def block_kernel(n_row, n_col, spp, grad_scale, *refs):
    (img_h, cot_h, wqkv_h, bqkv_h, wproj_h, bproj_h, gain_h, shift_h, table_h,
     res, gin, total_out,
     img, cot, wqkv, bqkv, wproj, bproj, gain_ref, shift_ref, table_ref,
     irow, icol, hrow, hcol, hdiag, orow, ocol, rrow, rcol, rdiag,
     field, cfield, corner, weights, xs, cs, dh, xd, xhid, xatt, sums, gsum,
     bias, onehot, padded, diag, gs, c_out, c_in, plane_buf, p_in, z_out, z_in, half_buf, last_in,
     ls, hs, hr, cs_sem, cr_sem, ps, pr, zs, zr, as_sem, ar_sem,
     row_known, col_known, pair_known) = refs
    my_r, my_c = lax.axis_index("row"), lax.axis_index("col")
    above, below = lax.rem(my_r + n_row - 1, n_row), lax.rem(my_r + 1, n_row)
    left, right = lax.rem(my_c + n_col - 1, n_col), lax.rem(my_c + 1, n_col)
    n_plane, n_z = n_col, n_row // 2
    core = lax.rem(my_c, 2)
    my_p = my_c // 2 * 2 + lax.rem(my_r, 2)
    my_z = my_r // 2
    owners = -(-STRIPES // spp)
    rows_each = spp * 16

    def plane_peer(p):
        return (my_z * 2 + lax.rem(p, 2), p // 2 * 2 + core)

    def z_peer(z):
        return (z * 2 + lax.rem(my_r, 2), my_c)

    local = [
        pltpu.make_async_copy(src, dst, ls.at[i])
        for i, (src, dst) in enumerate((
            (img_h, img), (cot_h, cot), (wqkv_h, wqkv), (bqkv_h, bqkv), (wproj_h, wproj),
            (bproj_h, bproj), (gain_h, gain_ref), (shift_h, shift_ref), (table_h, table_ref)))
    ]
    for copy in local:
        copy.start()
    barrier = pltpu.get_barrier_semaphore()

    def greet(device):
        pl.semaphore_signal(barrier, inc=1, device_id=device, device_id_type=MESH)

    for device in ((above, my_c), (below, my_c), (my_r, left), (my_r, right), (above, left),
                   (below, right)):
        greet(device)

    rounds = [(g, 2**g) for g in range(4)]
    row_rounds = [(g, d) for g, d in rounds if 4 * d <= n_row]
    col_rounds = [(g, d) for g, d in rounds if 4 * d <= n_col]

    def tell(sem, device):
        pl.semaphore_signal(sem, inc=1, device_id=device, device_id_type=MESH)

    def start_round(g):
        for k, d in row_rounds:
            @pl.when(g == k)
            def _():
                tell(row_known.at[k], (lax.rem(my_r + d, n_row), my_c))
                tell(row_known.at[k], (lax.rem(my_r + n_row - d, n_row), my_c))

        for k, d in col_rounds:
            @pl.when(g == k)
            def _():
                tell(col_known.at[k], (my_r, lax.rem(my_c + d, n_col)))
                tell(col_known.at[k], (my_r, lax.rem(my_c + n_col - d, n_col)))

        @pl.when(g == 3)
        def _():
            tell(pair_known, (my_r + 1 - 2 * lax.rem(my_r, 2), my_c))

    def end_round(g):
        for known, known_rounds in ((row_known, row_rounds), (col_known, col_rounds)):
            for k, _ in known_rounds:
                if k < 3:
                    @pl.when(g == k)
                    def _():
                        pl.semaphore_wait(known.at[k], 2)

    def remote(src, dst, send, recv, device):
        return pltpu.make_async_remote_copy(
            src_ref=src, dst_ref=dst, send_sem=send, recv_sem=recv, device_id=device,
            device_id_type=MESH)

    def halo(src, dst, i, device):
        return remote(src, dst, hs.at[i], hr.at[i], device)

    def lead_row(g):
        return halo(irow.at[g], hrow.at[g], g, (above, my_c))

    def trail_row(g):
        return halo(orow.at[g], rrow.at[g], CHUNKS + g, (below, my_c))

    n = 2 * CHUNKS
    lead = (halo(icol, hcol, n, (my_r, left)), halo(icol, hdiag, n + 1, (above, left)))
    trail = (halo(ocol, rcol, n + 2, (my_r, right)), halo(ocol, rdiag, n + 3, (below, right)))

    local[0].wait()
    local[1].wait()
    for i, (src, dst) in enumerate(((img, field), (cot, cfield))):
        half = slice(i * WIN, i * WIN + WIN)
        tile = src[...].astype(F32)
        icol[half, :] = tile[:, :EDGE].astype(BF16)
        dst[:, :LANES] = tile
        dst[:, LANES:] = tile[:, :EDGE]
        for g in range(CHUNKS):
            lanes = slice(EDGE + g * CHUNK, EDGE + (g + 1) * CHUNK)
            irow[g, half, :] = pack_rows(dst[:, lanes]).astype(BF16)
    pl.semaphore_wait(barrier, 6)
    for g in range(CHUNKS):
        lead_row(g).start()
    for copy in lead:
        copy.start()
    start_round(0)

    for copy in local[2:]:
        copy.wait()
    last_row = (my_r == n_row - 1).astype(F32)
    last_col = (my_c == n_col - 1).astype(F32)
    build_bias(table_ref, onehot, padded, diag, bias, last_row, last_col)
    gsum[...] = jnp.zeros_like(gsum)
    sums[...] = jnp.zeros_like(sums)
    gs[WIDTH:, :] = jnp.zeros((owners * rows_each - WIDTH, WIDE), F32)
    for i in range(3):
        weights[i] = wqkv[:, i * WIDTH : (i + 1) * WIDTH]
    qkv_bias = bqkv[...].reshape(1, 3 * WIDTH)
    biases = [qkv_bias[:, i * WIDTH : (i + 1) * WIDTH] for i in range(3)]
    proj_bias = bproj[...].reshape(1, WIDTH)
    gain = gain_ref[...].reshape(1, WIDTH)
    shift = shift_ref[...].reshape(1, WIDTH)

    for copy in lead:
        copy.wait_recv()
    for i in range(2):
        half = slice(i * WIN, i * WIN + WIN)
        corner[i] = jnp.where(
            upper((WIN, EDGE)), hdiag[half, :].astype(F32), hcol[half, :].astype(F32))

    def chunk_step(g, _):
        final = g == CHUNKS - 1
        lanes = pl.ds(pl.multiple_of(EDGE + g * CHUNK, 128), CHUNK)
        rows = pl.ds(pl.multiple_of(g * CHUNK_TOKENS, CHUNK_TOKENS), CHUNK_TOKENS)
        lead_row(g).wait_recv()
        tokens = []
        for i, src in enumerate((field, cfield)):
            half = slice(i * WIN, i * WIN + WIN)
            whole = merge_rows(hrow[g, half, :].astype(F32), src[:, lanes])
            end = jnp.where(final, corner[i], whole[:, CHUNK - EDGE :])
            whole = jnp.concatenate([whole[:, : CHUNK - EDGE], end], 1)
            parts = [split_tokens(whole[:, j * SPAN : (j + 1) * SPAN]) for j in range(PER_CHUNK)]
            first = jnp.concatenate([part[0] for part in parts], 0)
            second = jnp.concatenate([part[1] for part in parts], 0)
            tokens.append(jnp.concatenate([first, second[:, : WIDTH - 128]], 1))
        x, cot_f = tokens
        center = x - jnp.mean(x, 1, keepdims=True)
        inv_std = lax.rsqrt(jnp.mean(center * center, 1, keepdims=True) + EPS)
        normed = center * inv_std
        hidden = (normed * gain + shift).astype(BF16)
        xhid[rows, :] = hidden
        q, k, v = [(dot(hidden, weights[i]) + biases[i]).astype(BF16) for i in range(3)]
        cot_b = cot_f.astype(BF16)
        da = dot(cot_b, wproj[...], 1, 1).astype(BF16)
        found = []
        for j in range(PER_CHUNK):
            r = slice(j * CELLS, (j + 1) * CELLS)
            if j == PER_CHUNK - 1:
                add = bias.at[final.astype(jnp.int32)]
            else:
                add = bias.at[0]
            found.append(window_step(q[r], k[r], v[r], da[r], add, gsum))
        att, dq, dk, dv = [jnp.concatenate([part[i] for part in found], 0) for i in range(4)]
        xatt[rows, :] = att
        xs[rows, :] = x
        cs[rows, :] = cot_f
        d_hidden = jnp.zeros((CHUNK_TOKENS, WIDTH), F32)
        for i, part in enumerate((dq, dk, dv)):
            part_b = part.astype(BF16)
            xd[i, rows, :] = part_b
            sums[i] += fold(part)
            d_hidden = d_hidden + dot(part_b, weights[i], 1, 1)
        xd[3, rows, :] = cot_b
        sums[3] += fold(cot_f)
        sums[4] += fold(d_hidden * normed)
        sums[5] += fold(d_hidden)
        dh[rows, :] = d_hidden
        end_round(g + 1)
        start_round(g + 2)
        return 0

    end_round(0)
    start_round(1)
    lax.fori_loop(0, CHUNKS, chunk_step, 0)

    hidden_t = xhid[...].T
    for i in range(3):
        gs[0:WIDTH, i * WIDTH : (i + 1) * WIDTH] = dot(hidden_t, xd[i])
    gs[0:WIDTH, 3 * WIDTH :] = dot(xatt[...], xd[3], 0, 0)
    for i in range(4):
        gs[WIDTH : WIDTH + 1, i * WIDTH : (i + 1) * WIDTH] = jnp.sum(sums[i], 0, keepdims=True)
    for i in range(2):
        gs[WIDTH + 1 : WIDTH + 2, i * WIDTH : (i + 1) * WIDTH] = jnp.sum(
            sums[4 + i], 0, keepdims=True)
    for h, line in enumerate(table_grad(gsum[...], onehot, diag)):
        gs[WIDTH + 2 + h : WIDTH + 3 + h, 0:256] = line

    mine = pl.ds(pl.multiple_of(core * MID, 128), MID)
    other = pl.ds(pl.multiple_of((1 - core) * MID, 128), MID)
    partner = (my_r, my_c + 1 - 2 * core)
    c_out[...] = gs[:, other].astype(BF16)
    swap = remote(c_out, c_in, cs_sem.at[0], cr_sem.at[0], partner)
    swap.start()
    swap.wait_recv()
    plane_buf[...] = (gs[:, mine] + c_in[...].astype(F32)).astype(BF16).reshape(
        owners, rows_each, MID)

    def loop_group(me, count, step):
        def one(k, _):
            step(lax.rem(me + k, count))
            return 0

        lax.fori_loop(1, count, one, 0, unroll=LOOSE)

    def loop_plane(step):
        loop_group(my_p, n_plane, step)

    def loop_z(step):
        loop_group(my_z, n_z, step)

    def stage_of(buffer, count, send, recv):
        part = buffer.at[pl.ds(0, count)]
        return remote(part, part, send, recv, partner)

    def from_all_owners(step):
        @pl.when(my_p < owners)
        def _():
            step(owners - 1)

        @pl.when(my_p >= owners)
        def _():
            step(owners)

    def scatter(p):
        return remote(plane_buf.at[p], p_in.at[my_p], ps.at[0], pr.at[0], plane_peer(p))

    def along_z(z):
        return remote(z_out.at[0], z_in.at[my_z], zs.at[0], zr.at[0], z_peer(z))

    def spread(p):
        return remote(half_buf.at[my_p], half_buf.at[my_p], as_sem.at[0], ar_sem.at[0],
                      plane_peer(p))

    def send_scatter(p):
        @pl.when(p < owners)
        def _():
            scatter(p).start()

    pl.semaphore_wait(pair_known, 1)
    loop_plane(send_scatter)

    def output_step(g, _):
        lanes = pl.ds(pl.multiple_of(EDGE + g * CHUNK, 128), CHUNK)
        rows = pl.ds(pl.multiple_of(g * CHUNK_TOKENS, CHUNK_TOKENS), CHUNK_TOKENS)
        x, cot_f, d_hidden = xs[rows, :], cs[rows, :], dh[rows, :]
        center = x - jnp.mean(x, 1, keepdims=True)
        inv_std = lax.rsqrt(jnp.mean(center * center, 1, keepdims=True) + EPS)
        normed = center * inv_std
        out = x + dot(xatt[rows, :], wproj[...]) + proj_bias
        d_normed = d_hidden * gain
        d_tokens = cot_f + inv_std * (
            d_normed
            - jnp.mean(d_normed, 1, keepdims=True)
            - normed * jnp.mean(d_normed * normed, 1, keepdims=True))
        for i, (value, dst) in enumerate(((out, field), (d_tokens, cfield))):
            half = slice(i * WIN, i * WIN + WIN)
            first = value[:, :128]
            second = jnp.concatenate(
                [value[:, 128:], jnp.zeros((CHUNK_TOKENS, 256 - WIDTH), F32)], 1)
            strips = []
            for j in range(PER_CHUNK):
                r = slice(j * CELLS, (j + 1) * CELLS)
                strips.append(join_tokens(first[r], second[r]))
            whole = jnp.concatenate(strips, 1)
            dst[:, lanes] = whole
            orow[g, half, :] = pack_rows(whole).astype(BF16)
            ocol[half, :] = whole[:, CHUNK - EDGE :].astype(BF16)
        trail_row(g).start()
        return 0

    lax.fori_loop(0, CHUNKS, output_step, 0)
    for copy in trail:
        copy.start()

    def total_of(buffer, count):
        acc = buffer[0].astype(F32)
        for j in range(1, count):
            acc = acc + buffer[j].astype(F32)
        return acc

    if len(row_rounds) > 3:
        pl.semaphore_wait(row_known.at[3], 2)

    @pl.when(my_p < owners)
    def _():
        p_in[my_p] = plane_buf[my_p]
        stage_of(p_in, n_plane - 1, ps.at[0], pr.at[0]).wait_recv()
        z_out[0] = total_of(p_in, n_plane).astype(BF16)
        loop_z(lambda z: along_z(z).start())
        z_in[my_z] = z_out[0]

    for g in range(CHUNKS):
        trail_row(g).wait_recv()
    for copy in trail:
        copy.wait_recv()
    for i, (src, dst) in enumerate(((field, res), (cfield, gin))):
        half = slice(i * WIN, i * WIN + WIN)
        ends = jnp.where(
            upper((WIN, EDGE)), rdiag[half, :].astype(F32), rcol[half, :].astype(F32))
        dst[:, :EDGE] = ends.astype(BF16)
        for g in range(CHUNKS):
            start = EDGE + g * CHUNK
            size = min(CHUNK, LANES - start)
            whole = merge_rows(rrow[g, half, :].astype(F32), src[:, start : start + CHUNK])
            dst[:, start : start + size] = whole[:, :size].astype(BF16)

    @pl.when(my_p < owners)
    def _():
        stage_of(z_in, n_z - 1, zs.at[0], zr.at[0]).wait_recv()
        half_buf[my_p] = total_of(z_in, n_z).astype(BF16)
        loop_plane(lambda p: spread(p).start())

    from_all_owners(
        lambda count: stage_of(half_buf, count, as_sem.at[0], ar_sem.at[0]).wait_recv())
    back = remote(half_buf, last_in, cs_sem.at[1], cr_sem.at[1], partner)
    back.start()
    flat = (owners * rows_each, MID)
    total_out[:, mine] = half_buf[...].astype(F32).reshape(flat) * grad_scale
    back.wait_recv()
    total_out[:, other] = last_in[...].astype(F32).reshape(flat) * grad_scale

    for g in range(CHUNKS):
        lead_row(g).wait_send()
        trail_row(g).wait_send()
    for copy in lead + trail + (swap, back):
        copy.wait_send()

    from_all_owners(lambda count: stage_of(plane_buf, count, ps.at[0], pr.at[0]).wait_send())

    @pl.when(my_p < owners)
    def _():
        stage_of(z_in, n_z - 1, zs.at[0], zr.at[0]).wait_send()
        stage_of(p_in, n_plane - 1, as_sem.at[0], ar_sem.at[0]).wait_send()


def finish_kernel(res, gin, total, *refs):
    outs, (b0, b1, w0, w1, v0, v1, v2, t0, sems) = refs[:9], refs[9:]
    w0[...] = total[0:WIDTH, : 3 * WIDTH]
    w1[...] = total[0:WIDTH, 3 * WIDTH :]
    b0[...] = total[WIDTH : WIDTH + 1, : 3 * WIDTH].reshape(3 * WIDTH)
    v0[...] = total[WIDTH : WIDTH + 1, 3 * WIDTH :].reshape(WIDTH)
    v1[...] = total[WIDTH + 1 : WIDTH + 2, :WIDTH].reshape(WIDTH)
    v2[...] = total[WIDTH + 1 : WIDTH + 2, WIDTH : 2 * WIDTH].reshape(WIDTH)
    t0[...] = total[WIDTH + 2 : WIDTH + 2 + HEADS, :RELS]
    copies = [
        pltpu.make_async_copy(src, dst, sems.at[i])
        for i, (src, dst) in enumerate(zip((res, gin, w0, b0, w1, v0, v1, v2, t0), outs))
    ]
    for copy in copies:
        copy.start()
    for copy in copies:
        copy.wait()


def shards(image, cotangent, qkv_weight, qkv_bias, proj_weight, proj_bias, norm_gain, norm_bias,
           bias_table):
    n_row, n_col = lax.axis_size("row"), lax.axis_size("col")
    spp = -(-STRIPES // n_col)
    owners = -(-STRIPES // spp)
    rows_each = spp * 16
    factor = float(n_row * n_col * TOKENS_HERE) ** (-0.5)
    args = (image, cotangent, qkv_weight, qkv_bias, proj_weight, proj_bias, norm_gain, norm_bias,
            bias_table)
    tile = jax.ShapeDtypeStruct(image.shape, BF16)
    vmem = pl.BlockSpec(memory_space=pltpu.VMEM)
    hbm = pl.BlockSpec(memory_space=pltpu.HBM)
    dma = pltpu.SemaphoreType.DMA
    row_halo = pltpu.VMEM((CHUNKS, 16, HALF), BF16)
    col_halo = pltpu.VMEM((16, EDGE), BF16)
    half = (owners * rows_each, MID)
    halves = (owners, rows_each, MID)
    stripe = (rows_each, MID)
    parts = pl.pallas_call(
        functools.partial(block_kernel, n_row, n_col, spp, factor),
        out_shape=(tile, tile, jax.ShapeDtypeStruct((owners * rows_each, WIDE), F32)),
        in_specs=[hbm] * 9,
        out_specs=(vmem,) * 3,
        scratch_shapes=[pltpu.VMEM(a.shape, a.dtype) for a in args]
        + [row_halo, col_halo, row_halo, col_halo, col_halo] * 2
        + [
            pltpu.VMEM((WIN, LANES + EDGE), F32), pltpu.VMEM((WIN, LANES + EDGE), F32),
            pltpu.VMEM((2, WIN, EDGE), F32),
            pltpu.VMEM((3, WIDTH, WIDTH), BF16),
            pltpu.VMEM((TOKENS_HERE, WIDTH), F32),
            pltpu.VMEM((TOKENS_HERE, WIDTH), F32),
            pltpu.VMEM((TOKENS_HERE, WIDTH), F32),
            pltpu.VMEM((4, TOKENS_HERE, WIDTH), BF16),
            pltpu.VMEM((TOKENS_HERE, WIDTH), BF16),
            pltpu.VMEM((TOKENS_HERE, WIDTH), BF16),
            pltpu.VMEM((6, WIN, WIDTH), F32),
            pltpu.VMEM((CELLS, HEADS * CELLS), F32),
            pltpu.VMEM((2, CELLS, HEADS * CELLS), F32),
            pltpu.VMEM((WIN, 256, 128), BF16),
            pltpu.VMEM((8, 256), F32),
            pltpu.VMEM((HEADS, WIN, 128), F32),
            pltpu.VMEM((owners * rows_each, WIDE), F32),
            pltpu.VMEM(half, BF16), pltpu.VMEM(half, BF16),
            pltpu.VMEM(halves, BF16), pltpu.VMEM((n_col,) + stripe, BF16),
            pltpu.VMEM((1,) + stripe, BF16), pltpu.VMEM((n_row // 2,) + stripe, BF16),
            pltpu.VMEM(halves, BF16), pltpu.VMEM(halves, BF16),
            dma((9,)), dma((2 * CHUNKS + 4,)), dma((2 * CHUNKS + 4,)), dma((2,)), dma((2,)),
            dma((1,)), dma((1,)), dma((1,)), dma((1,)), dma((1,)), dma((1,)),
            pltpu.SemaphoreType.REGULAR((4,)), pltpu.SemaphoreType.REGULAR((4,)),
            pltpu.SemaphoreType.REGULAR,
        ],
        compiler_params=pltpu.CompilerParams(
            collective_id=1, has_side_effects=True, vmem_limit_bytes=60 * 1024 * 1024),
    )(*args)
    shapes = (image, cotangent, (WIDTH, 3 * WIDTH), (3 * WIDTH,), (WIDTH, WIDTH), (WIDTH,),
              (WIDTH,), (WIDTH,), (HEADS, RELS))
    outs = (tile, tile) + tuple(jax.ShapeDtypeStruct(s, F32) for s in shapes[2:])
    stage = [shapes[3], (1,), shapes[2], shapes[4], shapes[5], shapes[6], shapes[7], shapes[8]]
    return pl.pallas_call(
        finish_kernel,
        out_shape=outs,
        in_specs=[vmem] * 3,
        out_specs=(hbm,) * 9,
        scratch_shapes=[pltpu.VMEM(s, F32) for s in stage] + [dma((9,))],
        compiler_params=pltpu.CompilerParams(vmem_limit_bytes=60 * 1024 * 1024),
    )(*parts)


def solution(mesh):
    in_specs = (P("row", "col"), P("row", "col"), P(), P(), P(), P(), P(), P(), P())
    out_specs = (P("row", "col"), P("row", "col"), P(), P(), P(), P(), P(), P(), P())
    return jax.shard_map(shards, mesh=mesh, in_specs=in_specs, out_specs=out_specs, check_vma=False)
```

```python
import functools

import jax
import jax.numpy as jnp
from jax import lax
from jax.experimental import pallas as pl
from jax.experimental.pallas import tpu as pltpu
from jax.sharding import PartitionSpec as P

WIDTH = 192
HEADS = 6
HEAD_DIM = 32
WIN = 8
CELLS = WIN * WIN
SHIFT = 4
RELS = 225
EPS = 1e-05
NEG = -1e30
TILE_COLS = 64
LANES = TILE_COLS * WIDTH
EDGE = SHIFT * WIDTH
WINDOWS = TILE_COLS // WIN
SPAN = WIN * WIDTH
TOKENS_HERE = WINDOWS * CELLS
CHUNKS = 2
LOOSE = False
PER_CHUNK = WINDOWS // CHUNKS
CHUNK_TOKENS = PER_CHUNK * CELLS
CHUNK = PER_CHUNK * SPAN
HALF = CHUNK // 2
SCALE = HEAD_DIM**-0.5
GROUPS = ((0, 4), (4, 2))
STRIPES = 13
WIDE = 4 * WIDTH
MID = WIDE // 2

MESH = pl.DeviceIdType.MESH
F32 = jnp.float32
BF16 = jnp.bfloat16


def dot(a, b, ca=1, cb=0):
    return lax.dot_general(a, b, (((ca,), (cb,)), ((), ())), preferred_element_type=F32)


def iota(shape, dim):
    return lax.broadcasted_iota(jnp.int32, shape, dim)


def upper(shape):
    return iota(shape, 0) < SHIFT


def pack_rows(field):
    back = pltpu.roll(field[:, HALF:], SHIFT, 0)
    return jnp.where(upper((WIN, HALF)), field[:, :HALF], back)


def merge_rows(packed, field):
    low = jnp.where(upper((WIN, HALF)), packed, field[:, :HALF])
    high = jnp.where(upper((WIN, HALF)), pltpu.roll(packed, SHIFT, 0), field[:, HALF:])
    return jnp.concatenate([low, high], 1)


def split_tokens(strip):
    left = iota((WIN, 128), 1) < 64
    first, second = [], []
    for j in range(WIN // 2):
        v = [strip[:, (3 * j + i) * 128 : (3 * j + i + 1) * 128] for i in range(3)]
        r1, r2 = pltpu.roll(v[1], 64, 1), pltpu.roll(v[2], 64, 1)
        first += [v[0], jnp.where(left, r1, r2)]
        second += [v[1], r2]
    return jnp.concatenate(first, 0), jnp.concatenate(second, 0)


def join_tokens(first, second):
    left = iota((WIN, 128), 1) < 64
    out = []
    for j in range(WIN // 2):
        e = slice(16 * j, 16 * j + 8)
        o = slice(16 * j + 8, 16 * j + 16)
        swapped = pltpu.roll(first[o], 64, 1)
        out.append(first[e])
        out.append(jnp.where(left, second[e], swapped))
        out.append(jnp.where(left, swapped, pltpu.roll(second[o], 64, 1)))
    return jnp.concatenate(out, 1)


def build_bias(table_ref, onehot, padded, diag, bias, last_row, last_col):
    padded[...] = jnp.zeros((8, 256), F32)
    padded[0:HEADS, 0:RELS] = table_ref[...]
    table = padded[...]
    hi = table.astype(BF16)
    rest = table - hi.astype(F32)
    mid = rest.astype(BF16)
    low = (rest - mid.astype(F32)).astype(BF16)
    lane = iota((1, 128), 1)
    a_q = (lane + SHIFT) % WIN
    for a in range(WIN):
        target = (a_q - (a + SHIFT) % WIN + WIN - 1) * (2 * WIN - 1) + lane // WIN
        target = jnp.where(lane < 120, target, -1)
        hot = jnp.where(iota((256, 128), 0) == target, 1.0, 0.0).astype(BF16)
        onehot[a] = hot
        rows = dot(hi, hot) + dot(mid, hot) + dot(low, hot)
        for h in range(HEADS):
            diag[h, a : a + 1, :] = rows[h : h + 1, :]
    sub = iota((WIN, 128), 0)
    lanes = iota((WIN, 128), 1)
    row_cut = jnp.where((sub < SHIFT) != (lanes % WIN < SHIFT), NEG, 0.0) * last_row
    right = lanes % 64 // WIN >= SHIFT
    for b in range(WIN):
        col_cut = jnp.where(right != (b >= SHIFT), NEG, 0.0) * last_col
        for pair in range(HEADS // 2):
            shift = (WIN - 1 - b) * WIN
            even = pltpu.roll(diag[2 * pair], (128 - shift) % 128, 1)
            odd = pltpu.roll(diag[2 * pair + 1], (192 - shift) % 128, 1)
            block = jnp.where(lanes < 64, even, odd) + row_cut
            where = (slice(b * WIN, b * WIN + WIN), slice(pair * 128, pair * 128 + 128))
            bias[(0,) + where] = block
            bias[(1,) + where] = block + col_cut


def table_grad(total, onehot, diag):
    lanes = iota((WIN, 128), 1)
    for h in range(HEADS):
        mine = (lanes < 64) == (h % 2 == 0)
        acc = jnp.zeros((WIN, 128), F32)
        for b in range(WIN):
            block = total[b * WIN : b * WIN + WIN, h // 2 * 128 : h // 2 * 128 + 128]
            block = jnp.where(mine, block, 0.0)
            acc = acc + pltpu.roll(block, ((WIN - 1 - b) * WIN + h % 2 * 64) % 128, 1)
        diag[h] = acc
    flat = jnp.concatenate([diag[h] for h in range(HEADS)], 0)
    hi = flat.astype(BF16)
    low = (flat - hi.astype(F32)).astype(BF16)
    sub = iota((HEADS * WIN, 256), 0) % WIN
    acc = jnp.zeros((HEADS * WIN, 256), F32)
    for a in range(WIN):
        part = dot(hi, onehot[a], 1, 1) + dot(low, onehot[a], 1, 1)
        acc = acc + jnp.where(sub == a, part, 0.0)
    return [
        jnp.sum(acc[h * WIN : h * WIN + WIN], 0, keepdims=True) for h in range(HEADS)
    ]


def masked_heads(x, group):
    start, count = group
    lane = iota((CELLS, count * HEAD_DIM), 1) // HEAD_DIM
    wide = x[:, start * HEAD_DIM : (start + count) * HEAD_DIM]
    zero = jnp.zeros_like(wide)
    return jnp.concatenate([jnp.where(lane == h, wide, zero) for h in range(count)], 0)


def own_heads(x, count):
    lane = iota((CELLS, count * HEAD_DIM), 1) // HEAD_DIM
    out = x[(count - 1) * CELLS : count * CELLS]
    for h in range(count - 1):
        out = jnp.where(lane == h, x[h * CELLS : (h + 1) * CELLS], out)
    return out


def fold(x):
    return jnp.sum(x.reshape(-1, WIN, x.shape[1]), 0)


def window_step(q, k, v, da, bias, gsum):
    att, dq, dk, dv = [], [], [], []
    for start, count in GROUPS:
        ch = slice(start * HEAD_DIM, (start + count) * HEAD_DIM)
        lanes = slice(start * CELLS, (start + count) * CELLS)
        qm = masked_heads(q, (start, count))
        dam = masked_heads(da, (start, count))
        s = dot(k[:, ch], qm, 1, 1) * SCALE + bias[:, lanes]
        e = jnp.exp(s - jnp.max(s, 0, keepdims=True))
        p = e * (1.0 / jnp.sum(e, 0, keepdims=True))
        dp = dot(v[:, ch], dam, 1, 1)
        ds = p * (dp - jnp.sum(p * dp, 0, keepdims=True))
        gsum[:, lanes] += ds
        pb, dsb = p.astype(BF16), ds.astype(BF16)
        dv.append(dot(pb, dam))
        dk.append(dot(dsb, qm) * SCALE)
        att.append(own_heads(dot(pb, v[:, ch], 0, 0), count).astype(BF16))
        dq.append(own_heads(dot(dsb, k[:, ch], 0, 0), count) * SCALE)
    return [jnp.concatenate(parts, 1) for parts in (att, dq, dk, dv)]


def block_kernel(n_row, n_col, spp, grad_scale, *refs):
    (img_h, cot_h, wqkv_h, bqkv_h, wproj_h, bproj_h, gain_h, shift_h, table_h,
     res, gin, total_out,
     img, cot, wqkv, bqkv, wproj, bproj, gain_ref, shift_ref, table_ref,
     irow, icol, hrow, hcol, hdiag, orow, ocol, rrow, rcol, rdiag,
     field, cfield, corner, weights, xs, cs, dh, xd, xhid, xatt, sums, gsum,
     bias, onehot, padded, diag, gs, c_out, c_in, plane_buf, p_in, z_out, z_in, half_buf, last_in,
     ls, hs, hr, cs_sem, cr_sem, ps, pr, zs, zr, as_sem, ar_sem,
     row_known, col_known, pair_known) = refs
    my_r, my_c = lax.axis_index("row"), lax.axis_index("col")
    above, below = lax.rem(my_r + n_row - 1, n_row), lax.rem(my_r + 1, n_row)
    left, right = lax.rem(my_c + n_col - 1, n_col), lax.rem(my_c + 1, n_col)
    n_plane, n_z = n_col, n_row // 2
    core = lax.rem(my_c, 2)
    my_p = my_c // 2 * 2 + lax.rem(my_r, 2)
    my_z = my_r // 2
    owners = -(-STRIPES // spp)
    rows_each = spp * 16

    def plane_peer(p):
        return (my_z * 2 + lax.rem(p, 2), p // 2 * 2 + core)

    def z_peer(z):
        return (z * 2 + lax.rem(my_r, 2), my_c)

    local = [
        pltpu.make_async_copy(src, dst, ls.at[i])
        for i, (src, dst) in enumerate((
            (img_h, img), (cot_h, cot), (wqkv_h, wqkv), (bqkv_h, bqkv), (wproj_h, wproj),
            (bproj_h, bproj), (gain_h, gain_ref), (shift_h, shift_ref), (table_h, table_ref)))
    ]
    for copy in local:
        copy.start()
    barrier = pltpu.get_barrier_semaphore()

    def greet(device):
        pl.semaphore_signal(barrier, inc=1, device_id=device, device_id_type=MESH)

    for device in ((above, my_c), (below, my_c), (my_r, left), (my_r, right), (above, left),
                   (below, right)):
        greet(device)

    rounds = [(g, 2**g) for g in range(4)]
    row_rounds = [(g, d) for g, d in rounds if 4 * d <= n_row]
    col_rounds = [(g, d) for g, d in rounds if 4 * d <= n_col]

    def tell(sem, device):
        pl.semaphore_signal(sem, inc=1, device_id=device, device_id_type=MESH)

    def start_round(g):
        for k, d in row_rounds:
            @pl.when(g == k)
            def _():
                tell(row_known.at[k], (lax.rem(my_r + d, n_row), my_c))
                tell(row_known.at[k], (lax.rem(my_r + n_row - d, n_row), my_c))

        for k, d in col_rounds:
            @pl.when(g == k)
            def _():
                tell(col_known.at[k], (my_r, lax.rem(my_c + d, n_col)))
                tell(col_known.at[k], (my_r, lax.rem(my_c + n_col - d, n_col)))

        @pl.when(g == 3)
        def _():
            tell(pair_known, (my_r + 1 - 2 * lax.rem(my_r, 2), my_c))

    def end_round(g):
        for known, known_rounds in ((row_known, row_rounds), (col_known, col_rounds)):
            for k, _ in known_rounds:
                if k < 3:
                    @pl.when(g == k)
                    def _():
                        pl.semaphore_wait(known.at[k], 2)

    def remote(src, dst, send, recv, device):
        return pltpu.make_async_remote_copy(
            src_ref=src, dst_ref=dst, send_sem=send, recv_sem=recv, device_id=device,
            device_id_type=MESH)

    def halo(src, dst, i, device):
        return remote(src, dst, hs.at[i], hr.at[i], device)

    def lead_row(g):
        return halo(irow.at[g], hrow.at[g], g, (above, my_c))

    def trail_row(g):
        return halo(orow.at[g], rrow.at[g], CHUNKS + g, (below, my_c))

    n = 2 * CHUNKS
    lead = (halo(icol, hcol, n, (my_r, left)), halo(icol, hdiag, n + 1, (above, left)))
    trail = (halo(ocol, rcol, n + 2, (my_r, right)), halo(ocol, rdiag, n + 3, (below, right)))

    local[0].wait()
    local[1].wait()
    pl.semaphore_wait(barrier, 6)
    for g in range(CHUNKS):
        start = EDGE + g * CHUNK
        size = min(CHUNK, LANES - start)
        for i, (src, dst) in enumerate(((img, field), (cot, cfield))):
            half = slice(i * WIN, i * WIN + WIN)
            tile = src[:, start : start + size].astype(F32)
            if size < CHUNK:
                tile = jnp.concatenate([tile, src[:, :EDGE].astype(F32)], 1)
            dst[:, start : start + CHUNK] = tile
            irow[g, half, :] = pack_rows(tile).astype(BF16)
        lead_row(g).start()
    for i, src in enumerate((img, cot)):
        icol[i * WIN : i * WIN + WIN, :] = src[:, :EDGE]
    for copy in lead:
        copy.start()
    start_round(0)

    for copy in local[2:]:
        copy.wait()
    last_row = (my_r == n_row - 1).astype(F32)
    last_col = (my_c == n_col - 1).astype(F32)
    build_bias(table_ref, onehot, padded, diag, bias, last_row, last_col)
    gsum[...] = jnp.zeros_like(gsum)
    sums[...] = jnp.zeros_like(sums)
    corner[...] = jnp.zeros_like(corner)
    gs[WIDTH:, :] = jnp.zeros((owners * rows_each - WIDTH, WIDE), F32)
    for i in range(3):
        weights[i] = wqkv[:, i * WIDTH : (i + 1) * WIDTH]
    qkv_bias = bqkv[...].reshape(1, 3 * WIDTH)
    biases = [qkv_bias[:, i * WIDTH : (i + 1) * WIDTH] for i in range(3)]
    proj_bias = bproj[...].reshape(1, WIDTH)
    gain = gain_ref[...].reshape(1, WIDTH)
    shift = shift_ref[...].reshape(1, WIDTH)

    def chunk_step(g, _):
        final = g == CHUNKS - 1
        lanes = pl.ds(pl.multiple_of(EDGE + g * CHUNK, 128), CHUNK)
        rows = pl.ds(pl.multiple_of(g * CHUNK_TOKENS, CHUNK_TOKENS), CHUNK_TOKENS)
        lead_row(g).wait_recv()

        @pl.when(final)
        def _():
            for copy in lead:
                copy.wait_recv()
            for i in range(2):
                half = slice(i * WIN, i * WIN + WIN)
                corner[i] = jnp.where(
                    upper((WIN, EDGE)), hdiag[half, :].astype(F32), hcol[half, :].astype(F32))

        tokens = []
        for i, src in enumerate((field, cfield)):
            half = slice(i * WIN, i * WIN + WIN)
            whole = merge_rows(hrow[g, half, :].astype(F32), src[:, lanes])
            end = jnp.where(final, corner[i], whole[:, CHUNK - EDGE :])
            whole = jnp.concatenate([whole[:, : CHUNK - EDGE], end], 1)
            parts = [split_tokens(whole[:, j * SPAN : (j + 1) * SPAN]) for j in range(PER_CHUNK)]
            first = jnp.concatenate([part[0] for part in parts], 0)
            second = jnp.concatenate([part[1] for part in parts], 0)
            tokens.append(jnp.concatenate([first, second[:, : WIDTH - 128]], 1))
        x, cot_f = tokens
        center = x - jnp.mean(x, 1, keepdims=True)
        inv_std = lax.rsqrt(jnp.mean(center * center, 1, keepdims=True) + EPS)
        normed = center * inv_std
        hidden = (normed * gain + shift).astype(BF16)
        xhid[rows, :] = hidden
        q, k, v = [(dot(hidden, weights[i]) + biases[i]).astype(BF16) for i in range(3)]
        cot_b = cot_f.astype(BF16)
        da = dot(cot_b, wproj[...], 1, 1).astype(BF16)
        found = []
        for j in range(PER_CHUNK):
            r = slice(j * CELLS, (j + 1) * CELLS)
            if j == PER_CHUNK - 1:
                add = bias.at[final.astype(jnp.int32)]
            else:
                add = bias.at[0]
            found.append(window_step(q[r], k[r], v[r], da[r], add, gsum))
        att, dq, dk, dv = [jnp.concatenate([part[i] for part in found], 0) for i in range(4)]
        xatt[rows, :] = att
        xs[rows, :] = x
        cs[rows, :] = cot_f
        d_hidden = jnp.zeros((CHUNK_TOKENS, WIDTH), F32)
        for i, part in enumerate((dq, dk, dv)):
            part_b = part.astype(BF16)
            xd[i, rows, :] = part_b
            sums[i] += fold(part)
            d_hidden = d_hidden + dot(part_b, weights[i], 1, 1)
        xd[3, rows, :] = cot_b
        sums[3] += fold(cot_f)
        sums[4] += fold(d_hidden * normed)
        sums[5] += fold(d_hidden)
        dh[rows, :] = d_hidden
        end_round(g + 1)
        start_round(g + 2)
        return 0

    end_round(0)
    start_round(1)
    lax.fori_loop(0, CHUNKS, chunk_step, 0)

    hidden_t = xhid[...].T
    for i in range(3):
        gs[0:WIDTH, i * WIDTH : (i + 1) * WIDTH] = dot(hidden_t, xd[i])
    gs[0:WIDTH, 3 * WIDTH :] = dot(xatt[...], xd[3], 0, 0)
    for i in range(4):
        gs[WIDTH : WIDTH + 1, i * WIDTH : (i + 1) * WIDTH] = jnp.sum(sums[i], 0, keepdims=True)
    for i in range(2):
        gs[WIDTH + 1 : WIDTH + 2, i * WIDTH : (i + 1) * WIDTH] = jnp.sum(
            sums[4 + i], 0, keepdims=True)
    for h, line in enumerate(table_grad(gsum[...], onehot, diag)):
        gs[WIDTH + 2 + h : WIDTH + 3 + h, 0:256] = line

    mine = pl.ds(pl.multiple_of(core * MID, 128), MID)
    other = pl.ds(pl.multiple_of((1 - core) * MID, 128), MID)
    partner = (my_r, my_c + 1 - 2 * core)
    c_out[...] = gs[:, other].astype(BF16)
    swap = remote(c_out, c_in, cs_sem.at[0], cr_sem.at[0], partner)
    swap.start()
    swap.wait_recv()
    plane_buf[...] = (gs[:, mine] + c_in[...].astype(F32)).astype(BF16).reshape(
        owners, rows_each, MID)

    def loop_group(me, count, step):
        def one(k, _):
            step(lax.rem(me + k, count))
            return 0

        lax.fori_loop(1, count, one, 0, unroll=LOOSE)

    def loop_plane(step):
        loop_group(my_p, n_plane, step)

    def loop_z(step):
        loop_group(my_z, n_z, step)

    def stage_of(buffer, count, send, recv):
        part = buffer.at[pl.ds(0, count)]
        return remote(part, part, send, recv, partner)

    def from_all_owners(step):
        @pl.when(my_p < owners)
        def _():
            step(owners - 1)

        @pl.when(my_p >= owners)
        def _():
            step(owners)

    def scatter(p):
        return remote(plane_buf.at[p], p_in.at[my_p], ps.at[0], pr.at[0], plane_peer(p))

    def along_z(z):
        return remote(z_out.at[0], z_in.at[my_z], zs.at[0], zr.at[0], z_peer(z))

    def spread(p):
        return remote(half_buf.at[my_p], half_buf.at[my_p], as_sem.at[0], ar_sem.at[0],
                      plane_peer(p))

    def send_scatter(p):
        @pl.when(p < owners)
        def _():
            scatter(p).start()

    pl.semaphore_wait(pair_known, 1)
    loop_plane(send_scatter)

    def output_step(g, _):
        lanes = pl.ds(pl.multiple_of(EDGE + g * CHUNK, 128), CHUNK)
        rows = pl.ds(pl.multiple_of(g * CHUNK_TOKENS, CHUNK_TOKENS), CHUNK_TOKENS)
        x, cot_f, d_hidden = xs[rows, :], cs[rows, :], dh[rows, :]
        center = x - jnp.mean(x, 1, keepdims=True)
        inv_std = lax.rsqrt(jnp.mean(center * center, 1, keepdims=True) + EPS)
        normed = center * inv_std
        out = x + dot(xatt[rows, :], wproj[...]) + proj_bias
        d_normed = d_hidden * gain
        d_tokens = cot_f + inv_std * (
            d_normed
            - jnp.mean(d_normed, 1, keepdims=True)
            - normed * jnp.mean(d_normed * normed, 1, keepdims=True))
        for i, (value, dst) in enumerate(((out, field), (d_tokens, cfield))):
            half = slice(i * WIN, i * WIN + WIN)
            first = value[:, :128]
            second = jnp.concatenate(
                [value[:, 128:], jnp.zeros((CHUNK_TOKENS, 256 - WIDTH), F32)], 1)
            strips = []
            for j in range(PER_CHUNK):
                r = slice(j * CELLS, (j + 1) * CELLS)
                strips.append(join_tokens(first[r], second[r]))
            whole = jnp.concatenate(strips, 1)
            dst[:, lanes] = whole
            orow[g, half, :] = pack_rows(whole).astype(BF16)
            ocol[half, :] = whole[:, CHUNK - EDGE :].astype(BF16)
        trail_row(g).start()
        return 0


    def total_of(buffer, count):
        acc = buffer[0].astype(F32)
        for j in range(1, count):
            acc = acc + buffer[j].astype(F32)
        return acc

    if len(row_rounds) > 3:
        pl.semaphore_wait(row_known.at[3], 2)

    @pl.when(my_p < owners)
    def _():
        p_in[my_p] = plane_buf[my_p]
        stage_of(p_in, n_plane - 1, ps.at[0], pr.at[0]).wait_recv()
        z_out[0] = total_of(p_in, n_plane).astype(BF16)
        loop_z(lambda z: along_z(z).start())
        z_in[my_z] = z_out[0]

    lax.fori_loop(0, CHUNKS, output_step, 0)
    for copy in trail:
        copy.start()

    @pl.when(my_p < owners)
    def _():
        stage_of(z_in, n_z - 1, zs.at[0], zr.at[0]).wait_recv()
        half_buf[my_p] = total_of(z_in, n_z).astype(BF16)
        loop_plane(lambda p: spread(p).start())

    for g in range(CHUNKS):
        trail_row(g).wait_recv()
    for copy in trail:
        copy.wait_recv()
    for i, (src, dst) in enumerate(((field, res), (cfield, gin))):
        half = slice(i * WIN, i * WIN + WIN)
        ends = jnp.where(
            upper((WIN, EDGE)), rdiag[half, :].astype(F32), rcol[half, :].astype(F32))
        dst[:, :EDGE] = ends.astype(BF16)
        for g in range(CHUNKS):
            start = EDGE + g * CHUNK
            size = min(CHUNK, LANES - start)
            whole = merge_rows(rrow[g, half, :].astype(F32), src[:, start : start + CHUNK])
            dst[:, start : start + size] = whole[:, :size].astype(BF16)

    from_all_owners(
        lambda count: stage_of(half_buf, count, as_sem.at[0], ar_sem.at[0]).wait_recv())
    back = remote(half_buf, last_in, cs_sem.at[1], cr_sem.at[1], partner)
    back.start()
    flat = (owners * rows_each, MID)
    total_out[:, mine] = half_buf[...].astype(F32).reshape(flat) * grad_scale
    back.wait_recv()
    total_out[:, other] = last_in[...].astype(F32).reshape(flat) * grad_scale

    for g in range(CHUNKS):
        lead_row(g).wait_send()
        trail_row(g).wait_send()
    for copy in lead + trail + (swap, back):
        copy.wait_send()

    from_all_owners(lambda count: stage_of(plane_buf, count, ps.at[0], pr.at[0]).wait_send())

    @pl.when(my_p < owners)
    def _():
        stage_of(z_in, n_z - 1, zs.at[0], zr.at[0]).wait_send()
        stage_of(p_in, n_plane - 1, as_sem.at[0], ar_sem.at[0]).wait_send()


def finish_kernel(res, gin, total, *refs):
    outs, (b0, b1, w0, w1, v0, v1, v2, t0, sems) = refs[:9], refs[9:]
    staged = (res, gin, w0, b0, w1, v0, v1, v2, t0)
    copies = [
        pltpu.make_async_copy(src, dst, sems.at[i]) for i, (src, dst) in enumerate(zip(staged, outs))
    ]
    for copy in copies[:2]:
        copy.start()
    w0[...] = total[0:WIDTH, : 3 * WIDTH]
    copies[2].start()
    w1[...] = total[0:WIDTH, 3 * WIDTH :]
    copies[4].start()
    b0[...] = total[WIDTH : WIDTH + 1, : 3 * WIDTH].reshape(3 * WIDTH)
    v0[...] = total[WIDTH : WIDTH + 1, 3 * WIDTH :].reshape(WIDTH)
    v1[...] = total[WIDTH + 1 : WIDTH + 2, :WIDTH].reshape(WIDTH)
    v2[...] = total[WIDTH + 1 : WIDTH + 2, WIDTH : 2 * WIDTH].reshape(WIDTH)
    t0[...] = total[WIDTH + 2 : WIDTH + 2 + HEADS, :RELS]
    for i in (3, 5, 6, 7, 8):
        copies[i].start()
    for copy in copies:
        copy.wait()


def shards(image, cotangent, qkv_weight, qkv_bias, proj_weight, proj_bias, norm_gain, norm_bias,
           bias_table):
    n_row, n_col = lax.axis_size("row"), lax.axis_size("col")
    spp = -(-STRIPES // n_col)
    owners = -(-STRIPES // spp)
    rows_each = spp * 16
    factor = float(n_row * n_col * TOKENS_HERE) ** (-0.5)
    args = (image, cotangent, qkv_weight, qkv_bias, proj_weight, proj_bias, norm_gain, norm_bias,
            bias_table)
    tile = jax.ShapeDtypeStruct(image.shape, BF16)
    vmem = pl.BlockSpec(memory_space=pltpu.VMEM)
    hbm = pl.BlockSpec(memory_space=pltpu.HBM)
    dma = pltpu.SemaphoreType.DMA
    row_halo = pltpu.VMEM((CHUNKS, 16, HALF), BF16)
    col_halo = pltpu.VMEM((16, EDGE), BF16)
    half = (owners * rows_each, MID)
    halves = (owners, rows_each, MID)
    stripe = (rows_each, MID)
    parts = pl.pallas_call(
        functools.partial(block_kernel, n_row, n_col, spp, factor),
        out_shape=(tile, tile, jax.ShapeDtypeStruct((owners * rows_each, WIDE), F32)),
        in_specs=[hbm] * 9,
        out_specs=(vmem,) * 3,
        scratch_shapes=[pltpu.VMEM(a.shape, a.dtype) for a in args]
        + [row_halo, col_halo, row_halo, col_halo, col_halo] * 2
        + [
            pltpu.VMEM((WIN, LANES + EDGE), F32), pltpu.VMEM((WIN, LANES + EDGE), F32),
            pltpu.VMEM((2, WIN, EDGE), F32),
            pltpu.VMEM((3, WIDTH, WIDTH), BF16),
            pltpu.VMEM((TOKENS_HERE, WIDTH), F32),
            pltpu.VMEM((TOKENS_HERE, WIDTH), F32),
            pltpu.VMEM((TOKENS_HERE, WIDTH), F32),
            pltpu.VMEM((4, TOKENS_HERE, WIDTH), BF16),
            pltpu.VMEM((TOKENS_HERE, WIDTH), BF16),
            pltpu.VMEM((TOKENS_HERE, WIDTH), BF16),
            pltpu.VMEM((6, WIN, WIDTH), F32),
            pltpu.VMEM((CELLS, HEADS * CELLS), F32),
            pltpu.VMEM((2, CELLS, HEADS * CELLS), F32),
            pltpu.VMEM((WIN, 256, 128), BF16),
            pltpu.VMEM((8, 256), F32),
            pltpu.VMEM((HEADS, WIN, 128), F32),
            pltpu.VMEM((owners * rows_each, WIDE), F32),
            pltpu.VMEM(half, BF16), pltpu.VMEM(half, BF16),
            pltpu.VMEM(halves, BF16), pltpu.VMEM((n_col,) + stripe, BF16),
            pltpu.VMEM((1,) + stripe, BF16), pltpu.VMEM((n_row // 2,) + stripe, BF16),
            pltpu.VMEM(halves, BF16), pltpu.VMEM(halves, BF16),
            dma((9,)), dma((2 * CHUNKS + 4,)), dma((2 * CHUNKS + 4,)), dma((2,)), dma((2,)),
            dma((1,)), dma((1,)), dma((1,)), dma((1,)), dma((1,)), dma((1,)),
            pltpu.SemaphoreType.REGULAR((4,)), pltpu.SemaphoreType.REGULAR((4,)),
            pltpu.SemaphoreType.REGULAR,
        ],
        compiler_params=pltpu.CompilerParams(
            collective_id=1, has_side_effects=True, vmem_limit_bytes=60 * 1024 * 1024),
    )(*args)
    shapes = (image, cotangent, (WIDTH, 3 * WIDTH), (3 * WIDTH,), (WIDTH, WIDTH), (WIDTH,),
              (WIDTH,), (WIDTH,), (HEADS, RELS))
    outs = (tile, tile) + tuple(jax.ShapeDtypeStruct(s, F32) for s in shapes[2:])
    stage = [shapes[3], (1,), shapes[2], shapes[4], shapes[5], shapes[6], shapes[7], shapes[8]]
    return pl.pallas_call(
        finish_kernel,
        out_shape=outs,
        in_specs=[vmem] * 3,
        out_specs=(hbm,) * 9,
        scratch_shapes=[pltpu.VMEM(s, F32) for s in stage] + [dma((9,))],
        compiler_params=pltpu.CompilerParams(vmem_limit_bytes=60 * 1024 * 1024),
    )(*parts)


def solution(mesh):
    in_specs = (P("row", "col"), P("row", "col"), P(), P(), P(), P(), P(), P(), P())
    out_specs = (P("row", "col"), P("row", "col"), P(), P(), P(), P(), P(), P(), P())
    return jax.shard_map(shards, mesh=mesh, in_specs=in_specs, out_specs=out_specs, check_vma=False)
```

```python
import functools

import jax
import jax.numpy as jnp
from jax import lax
from jax.experimental import pallas as pl
from jax.experimental.pallas import tpu as pltpu
from jax.sharding import PartitionSpec as P

WIDTH = 192
HEADS = 6
HEAD_DIM = 32
WIN = 8
CELLS = WIN * WIN
SHIFT = 4
RELS = 225
EPS = 1e-05
NEG = -1e30
TILE_COLS = 64
LANES = TILE_COLS * WIDTH
EDGE = SHIFT * WIDTH
WINDOWS = TILE_COLS // WIN
SPAN = WIN * WIDTH
TOKENS_HERE = WINDOWS * CELLS
CHUNKS = 2
LOOSE = False
PER_CHUNK = WINDOWS // CHUNKS
CHUNK_TOKENS = PER_CHUNK * CELLS
CHUNK = PER_CHUNK * SPAN
HALF = CHUNK // 2
SCALE = HEAD_DIM**-0.5
GROUPS = ((0, 4), (4, 2))
STRIPES = 13
WIDE = 4 * WIDTH
MID = WIDE // 2
PARTS = MID // 128

MESH = pl.DeviceIdType.MESH
F32 = jnp.float32
BF16 = jnp.bfloat16


def dot(a, b, ca=1, cb=0):
    return lax.dot_general(a, b, (((ca,), (cb,)), ((), ())), preferred_element_type=F32)


def iota(shape, dim):
    return lax.broadcasted_iota(jnp.int32, shape, dim)


def upper(shape):
    return iota(shape, 0) < SHIFT


def pack_rows(field):
    back = pltpu.roll(field[:, HALF:], SHIFT, 0)
    return jnp.where(upper((WIN, HALF)), field[:, :HALF], back)


def merge_rows(packed, field):
    low = jnp.where(upper((WIN, HALF)), packed, field[:, :HALF])
    high = jnp.where(upper((WIN, HALF)), pltpu.roll(packed, SHIFT, 0), field[:, HALF:])
    return jnp.concatenate([low, high], 1)


def split_tokens(strip):
    left = iota((WIN, 128), 1) < 64
    first, second = [], []
    for j in range(WIN // 2):
        v = [strip[:, (3 * j + i) * 128 : (3 * j + i + 1) * 128] for i in range(3)]
        r1, r2 = pltpu.roll(v[1], 64, 1), pltpu.roll(v[2], 64, 1)
        first += [v[0], jnp.where(left, r1, r2)]
        second += [v[1], r2]
    return jnp.concatenate(first, 0), jnp.concatenate(second, 0)


def join_tokens(first, second):
    left = iota((WIN, 128), 1) < 64
    out = []
    for j in range(WIN // 2):
        e = slice(16 * j, 16 * j + 8)
        o = slice(16 * j + 8, 16 * j + 16)
        swapped = pltpu.roll(first[o], 64, 1)
        out.append(first[e])
        out.append(jnp.where(left, second[e], swapped))
        out.append(jnp.where(left, swapped, pltpu.roll(second[o], 64, 1)))
    return jnp.concatenate(out, 1)


def build_bias(table_ref, onehot, padded, diag, bias, last_row, last_col):
    padded[...] = jnp.zeros((8, 256), F32)
    padded[0:HEADS, 0:RELS] = table_ref[...]
    table = padded[...]
    hi = table.astype(BF16)
    rest = table - hi.astype(F32)
    mid = rest.astype(BF16)
    low = (rest - mid.astype(F32)).astype(BF16)
    lane = iota((1, 128), 1)
    a_q = (lane + SHIFT) % WIN
    for a in range(WIN):
        target = (a_q - (a + SHIFT) % WIN + WIN - 1) * (2 * WIN - 1) + lane // WIN
        target = jnp.where(lane < 120, target, -1)
        hot = jnp.where(iota((256, 128), 0) == target, 1.0, 0.0).astype(BF16)
        onehot[a] = hot
        rows = dot(hi, hot) + dot(mid, hot) + dot(low, hot)
        for h in range(HEADS):
            diag[h, a : a + 1, :] = rows[h : h + 1, :]
    sub = iota((WIN, 128), 0)
    lanes = iota((WIN, 128), 1)
    row_cut = jnp.where((sub < SHIFT) != (lanes % WIN < SHIFT), NEG, 0.0) * last_row
    right = lanes % 64 // WIN >= SHIFT
    for b in range(WIN):
        col_cut = jnp.where(right != (b >= SHIFT), NEG, 0.0) * last_col
        for pair in range(HEADS // 2):
            shift = (WIN - 1 - b) * WIN
            even = pltpu.roll(diag[2 * pair], (128 - shift) % 128, 1)
            odd = pltpu.roll(diag[2 * pair + 1], (192 - shift) % 128, 1)
            block = jnp.where(lanes < 64, even, odd) + row_cut
            where = (slice(b * WIN, b * WIN + WIN), slice(pair * 128, pair * 128 + 128))
            bias[(0,) + where] = block
            bias[(1,) + where] = block + col_cut


def table_grad(total, onehot, diag):
    lanes = iota((WIN, 128), 1)
    for h in range(HEADS):
        mine = (lanes < 64) == (h % 2 == 0)
        acc = jnp.zeros((WIN, 128), F32)
        for b in range(WIN):
            block = total[b * WIN : b * WIN + WIN, h // 2 * 128 : h // 2 * 128 + 128]
            block = jnp.where(mine, block, 0.0)
            acc = acc + pltpu.roll(block, ((WIN - 1 - b) * WIN + h % 2 * 64) % 128, 1)
        diag[h] = acc
    flat = jnp.concatenate([diag[h] for h in range(HEADS)], 0)
    hi = flat.astype(BF16)
    low = (flat - hi.astype(F32)).astype(BF16)
    sub = iota((HEADS * WIN, 256), 0) % WIN
    acc = jnp.zeros((HEADS * WIN, 256), F32)
    for a in range(WIN):
        part = dot(hi, onehot[a], 1, 1) + dot(low, onehot[a], 1, 1)
        acc = acc + jnp.where(sub == a, part, 0.0)
    return [
        jnp.sum(acc[h * WIN : h * WIN + WIN], 0, keepdims=True) for h in range(HEADS)
    ]


def masked_heads(x, group):
    start, count = group
    lane = iota((CELLS, count * HEAD_DIM), 1) // HEAD_DIM
    wide = x[:, start * HEAD_DIM : (start + count) * HEAD_DIM]
    zero = jnp.zeros_like(wide)
    return jnp.concatenate([jnp.where(lane == h, wide, zero) for h in range(count)], 0)


def own_heads(x, count):
    lane = iota((CELLS, count * HEAD_DIM), 1) // HEAD_DIM
    out = x[(count - 1) * CELLS : count * CELLS]
    for h in range(count - 1):
        out = jnp.where(lane == h, x[h * CELLS : (h + 1) * CELLS], out)
    return out


def fold(x):
    return jnp.sum(x.reshape(-1, WIN, x.shape[1]), 0)


def window_step(q, k, v, da, bias, gsum):
    att, dq, dk, dv = [], [], [], []
    for start, count in GROUPS:
        ch = slice(start * HEAD_DIM, (start + count) * HEAD_DIM)
        lanes = slice(start * CELLS, (start + count) * CELLS)
        qm = masked_heads(q, (start, count))
        dam = masked_heads(da, (start, count))
        s = dot(k[:, ch], qm, 1, 1) * SCALE + bias[:, lanes]
        e = jnp.exp(s - jnp.max(s, 0, keepdims=True))
        p = e * (1.0 / jnp.sum(e, 0, keepdims=True))
        dp = dot(v[:, ch], dam, 1, 1)
        ds = p * (dp - jnp.sum(p * dp, 0, keepdims=True))
        gsum[:, lanes] += ds
        pb, dsb = p.astype(BF16), ds.astype(BF16)
        dv.append(dot(pb, dam))
        dk.append(dot(dsb, qm) * SCALE)
        att.append(own_heads(dot(pb, v[:, ch], 0, 0), count).astype(BF16))
        dq.append(own_heads(dot(dsb, k[:, ch], 0, 0), count) * SCALE)
    return [jnp.concatenate(parts, 1) for parts in (att, dq, dk, dv)]


def block_kernel(n_row, n_col, spp, grad_scale, *refs):
    (img_h, cot_h, wqkv_h, bqkv_h, wproj_h, bproj_h, gain_h, shift_h, table_h,
     res, gin, total_out,
     img, cot, wqkv, bqkv, wproj, bproj, gain_ref, shift_ref, table_ref,
     irow, icol, hrow, hcol, hdiag, orow, ocol, rrow, rcol, rdiag,
     field, cfield, corner, weights, xs, cs, dh, xd, xhid, xatt, sums, gsum,
     bias, onehot, padded, diag, gs, c_out, c_in, plane_buf, p_in, z_out, z_in, half_buf, last_in,
     ls, hs, hr, cs_sem, cr_sem, ps, pr, zs, zr, as_sem, ar_sem,
     row_known, col_known, pair_known) = refs
    my_r, my_c = lax.axis_index("row"), lax.axis_index("col")
    above, below = lax.rem(my_r + n_row - 1, n_row), lax.rem(my_r + 1, n_row)
    left, right = lax.rem(my_c + n_col - 1, n_col), lax.rem(my_c + 1, n_col)
    n_plane, n_z = n_col, n_row // 2
    core = lax.rem(my_c, 2)
    my_p = my_c // 2 * 2 + lax.rem(my_r, 2)
    my_z = my_r // 2
    owners = -(-STRIPES // spp)
    rows_each = spp * 16

    def plane_peer(p):
        return (my_z * 2 + lax.rem(p, 2), p // 2 * 2 + core)

    def z_peer(z):
        return (z * 2 + lax.rem(my_r, 2), my_c)

    local = [
        pltpu.make_async_copy(src, dst, ls.at[i])
        for i, (src, dst) in enumerate((
            (img_h, img), (cot_h, cot), (wqkv_h, wqkv), (bqkv_h, bqkv), (wproj_h, wproj),
            (bproj_h, bproj), (gain_h, gain_ref), (shift_h, shift_ref), (table_h, table_ref)))
    ]
    for copy in local:
        copy.start()
    barrier = pltpu.get_barrier_semaphore()

    def greet(device):
        pl.semaphore_signal(barrier, inc=1, device_id=device, device_id_type=MESH)

    for device in ((above, my_c), (below, my_c), (my_r, left), (my_r, right), (above, left),
                   (below, right)):
        greet(device)

    rounds = [(g, 2**g) for g in range(4)]
    row_rounds = [(g, d) for g, d in rounds if 4 * d <= n_row]
    col_rounds = [(g, d) for g, d in rounds if 4 * d <= n_col]

    def tell(sem, device):
        pl.semaphore_signal(sem, inc=1, device_id=device, device_id_type=MESH)

    def start_round(g):
        for k, d in row_rounds:
            @pl.when(g == k)
            def _():
                tell(row_known.at[k], (lax.rem(my_r + d, n_row), my_c))
                tell(row_known.at[k], (lax.rem(my_r + n_row - d, n_row), my_c))

        for k, d in col_rounds:
            @pl.when(g == k)
            def _():
                tell(col_known.at[k], (my_r, lax.rem(my_c + d, n_col)))
                tell(col_known.at[k], (my_r, lax.rem(my_c + n_col - d, n_col)))

        @pl.when(g == 3)
        def _():
            tell(pair_known, (my_r + 1 - 2 * lax.rem(my_r, 2), my_c))

    def end_round(g):
        for known, known_rounds in ((row_known, row_rounds), (col_known, col_rounds)):
            for k, _ in known_rounds:
                if k < 3:
                    @pl.when(g == k)
                    def _():
                        pl.semaphore_wait(known.at[k], 2)

    def remote(src, dst, send, recv, device):
        return pltpu.make_async_remote_copy(
            src_ref=src, dst_ref=dst, send_sem=send, recv_sem=recv, device_id=device,
            device_id_type=MESH)

    def halo(src, dst, i, device):
        return remote(src, dst, hs.at[i], hr.at[i], device)

    def lead_row(g):
        return halo(irow.at[g], hrow.at[g], g, (above, my_c))

    def trail_row(g):
        return halo(orow.at[g], rrow.at[g], CHUNKS + g, (below, my_c))

    n = 2 * CHUNKS
    lead = (halo(icol, hcol, n, (my_r, left)), halo(icol, hdiag, n + 1, (above, left)))
    trail = (halo(ocol, rcol, n + 2, (my_r, right)), halo(ocol, rdiag, n + 3, (below, right)))

    local[0].wait()
    local[1].wait()
    pl.semaphore_wait(barrier, 6)
    for g in range(CHUNKS):
        start = EDGE + g * CHUNK
        size = min(CHUNK, LANES - start)
        for i, (src, dst) in enumerate(((img, field), (cot, cfield))):
            half = slice(i * WIN, i * WIN + WIN)
            tile = src[:, start : start + size].astype(F32)
            if size < CHUNK:
                tile = jnp.concatenate([tile, src[:, :EDGE].astype(F32)], 1)
            dst[:, start : start + CHUNK] = tile
            irow[g, half, :] = pack_rows(tile).astype(BF16)
        lead_row(g).start()
    for i, src in enumerate((img, cot)):
        icol[i * WIN : i * WIN + WIN, :] = src[:, :EDGE]
    for copy in lead:
        copy.start()
    start_round(0)

    for copy in local[2:]:
        copy.wait()
    last_row = (my_r == n_row - 1).astype(F32)
    last_col = (my_c == n_col - 1).astype(F32)
    build_bias(table_ref, onehot, padded, diag, bias, last_row, last_col)
    gsum[...] = jnp.zeros_like(gsum)
    sums[...] = jnp.zeros_like(sums)
    corner[...] = jnp.zeros_like(corner)
    gs[WIDTH:, :] = jnp.zeros((owners * rows_each - WIDTH, WIDE), F32)
    for i in range(3):
        weights[i] = wqkv[:, i * WIDTH : (i + 1) * WIDTH]
    qkv_bias = bqkv[...].reshape(1, 3 * WIDTH)
    biases = [qkv_bias[:, i * WIDTH : (i + 1) * WIDTH] for i in range(3)]
    proj_bias = bproj[...].reshape(1, WIDTH)
    gain = gain_ref[...].reshape(1, WIDTH)
    shift = shift_ref[...].reshape(1, WIDTH)

    def chunk_step(g, _):
        final = g == CHUNKS - 1
        lanes = pl.ds(pl.multiple_of(EDGE + g * CHUNK, 128), CHUNK)
        rows = pl.ds(pl.multiple_of(g * CHUNK_TOKENS, CHUNK_TOKENS), CHUNK_TOKENS)
        lead_row(g).wait_recv()

        @pl.when(final)
        def _():
            for copy in lead:
                copy.wait_recv()
            for i in range(2):
                half = slice(i * WIN, i * WIN + WIN)
                corner[i] = jnp.where(
                    upper((WIN, EDGE)), hdiag[half, :].astype(F32), hcol[half, :].astype(F32))

        tokens = []
        for i, src in enumerate((field, cfield)):
            half = slice(i * WIN, i * WIN + WIN)
            whole = merge_rows(hrow[g, half, :].astype(F32), src[:, lanes])
            end = jnp.where(final, corner[i], whole[:, CHUNK - EDGE :])
            whole = jnp.concatenate([whole[:, : CHUNK - EDGE], end], 1)
            parts = [split_tokens(whole[:, j * SPAN : (j + 1) * SPAN]) for j in range(PER_CHUNK)]
            first = jnp.concatenate([part[0] for part in parts], 0)
            second = jnp.concatenate([part[1] for part in parts], 0)
            tokens.append(jnp.concatenate([first, second[:, : WIDTH - 128]], 1))
        x, cot_f = tokens
        center = x - jnp.mean(x, 1, keepdims=True)
        inv_std = lax.rsqrt(jnp.mean(center * center, 1, keepdims=True) + EPS)
        normed = center * inv_std
        hidden = (normed * gain + shift).astype(BF16)
        xhid[rows, :] = hidden
        q, k, v = [(dot(hidden, weights[i]) + biases[i]).astype(BF16) for i in range(3)]
        cot_b = cot_f.astype(BF16)
        da = dot(cot_b, wproj[...], 1, 1).astype(BF16)
        found = []
        for j in range(PER_CHUNK):
            r = slice(j * CELLS, (j + 1) * CELLS)
            if j == PER_CHUNK - 1:
                add = bias.at[final.astype(jnp.int32)]
            else:
                add = bias.at[0]
            found.append(window_step(q[r], k[r], v[r], da[r], add, gsum))
        att, dq, dk, dv = [jnp.concatenate([part[i] for part in found], 0) for i in range(4)]
        xatt[rows, :] = att
        xs[rows, :] = x
        cs[rows, :] = cot_f
        d_hidden = jnp.zeros((CHUNK_TOKENS, WIDTH), F32)
        for i, part in enumerate((dq, dk, dv)):
            part_b = part.astype(BF16)
            xd[i, rows, :] = part_b
            sums[i] += fold(part)
            d_hidden = d_hidden + dot(part_b, weights[i], 1, 1)
        xd[3, rows, :] = cot_b
        sums[3] += fold(cot_f)
        sums[4] += fold(d_hidden * normed)
        sums[5] += fold(d_hidden)
        dh[rows, :] = d_hidden
        end_round(g + 1)
        start_round(g + 2)
        return 0

    end_round(0)
    start_round(1)
    lax.fori_loop(0, CHUNKS, chunk_step, 0)

    hidden_t = xhid[...].T
    for i in range(3):
        gs[0:WIDTH, i * WIDTH : (i + 1) * WIDTH] = dot(hidden_t, xd[i])
    gs[0:WIDTH, 3 * WIDTH :] = dot(xatt[...], xd[3], 0, 0)
    for i in range(4):
        gs[WIDTH : WIDTH + 1, i * WIDTH : (i + 1) * WIDTH] = jnp.sum(sums[i], 0, keepdims=True)
    for i in range(2):
        gs[WIDTH + 1 : WIDTH + 2, i * WIDTH : (i + 1) * WIDTH] = jnp.sum(
            sums[4 + i], 0, keepdims=True)
    for h, line in enumerate(table_grad(gsum[...], onehot, diag)):
        gs[WIDTH + 2 + h : WIDTH + 3 + h, 0:256] = line

    mine = pl.ds(pl.multiple_of(core * MID, 128), MID)
    other = pl.ds(pl.multiple_of((1 - core) * MID, 128), MID)
    partner = (my_r, my_c + 1 - 2 * core)
    c_out[...] = gs[:, other].astype(BF16)
    swap = remote(c_out, c_in, cs_sem.at[0], cr_sem.at[0], partner)
    swap.start()
    swap.wait_recv()
    halves = (gs[:, mine] + c_in[...].astype(F32)).astype(BF16)
    for t in range(PARTS):
        plane_buf[t] = halves[:, t * 128 : (t + 1) * 128].reshape(owners, rows_each, 128)

    def loop_group(me, count, step):
        def one(k, _):
            step(lax.rem(me + k, count))
            return 0

        lax.fori_loop(1, count, one, 0, unroll=LOOSE)

    def loop_plane(step):
        loop_group(my_p, n_plane, step)

    def loop_z(step):
        loop_group(my_z, n_z, step)

    def stage_of(buffer, t, count, send, recv):
        part = buffer.at[t, pl.ds(0, count)]
        return remote(part, part, send.at[t], recv.at[t], partner)

    def from_all_owners(step):
        @pl.when(my_p < owners)
        def _():
            step(owners - 1)

        @pl.when(my_p >= owners)
        def _():
            step(owners)

    def scatter(t, p):
        return remote(plane_buf.at[t, p], p_in.at[t, my_p], ps.at[t], pr.at[t], plane_peer(p))

    def along_z(t, z):
        return remote(z_out.at[t], z_in.at[t, my_z], zs.at[t], zr.at[t], z_peer(z))

    def spread(t, p):
        return remote(half_buf.at[t, my_p], half_buf.at[t, my_p], as_sem.at[t], ar_sem.at[t],
                      plane_peer(p))

    def back(t):
        return remote(half_buf.at[t], last_in.at[t], cs_sem.at[1 + t], cr_sem.at[1 + t], partner)

    def send_scatter(t):
        def one(p):
            @pl.when(p < owners)
            def _():
                scatter(t, p).start()

        loop_plane(one)

    pl.semaphore_wait(pair_known, 1)
    for t in range(PARTS):
        send_scatter(t)

    def output_step(g, _):
        lanes = pl.ds(pl.multiple_of(EDGE + g * CHUNK, 128), CHUNK)
        rows = pl.ds(pl.multiple_of(g * CHUNK_TOKENS, CHUNK_TOKENS), CHUNK_TOKENS)
        x, cot_f, d_hidden = xs[rows, :], cs[rows, :], dh[rows, :]
        center = x - jnp.mean(x, 1, keepdims=True)
        inv_std = lax.rsqrt(jnp.mean(center * center, 1, keepdims=True) + EPS)
        normed = center * inv_std
        out = x + dot(xatt[rows, :], wproj[...]) + proj_bias
        d_normed = d_hidden * gain
        d_tokens = cot_f + inv_std * (
            d_normed
            - jnp.mean(d_normed, 1, keepdims=True)
            - normed * jnp.mean(d_normed * normed, 1, keepdims=True))
        for i, (value, dst) in enumerate(((out, field), (d_tokens, cfield))):
            half = slice(i * WIN, i * WIN + WIN)
            first = value[:, :128]
            second = jnp.concatenate(
                [value[:, 128:], jnp.zeros((CHUNK_TOKENS, 256 - WIDTH), F32)], 1)
            strips = []
            for j in range(PER_CHUNK):
                r = slice(j * CELLS, (j + 1) * CELLS)
                strips.append(join_tokens(first[r], second[r]))
            whole = jnp.concatenate(strips, 1)
            dst[:, lanes] = whole
            orow[g, half, :] = pack_rows(whole).astype(BF16)
            ocol[half, :] = whole[:, CHUNK - EDGE :].astype(BF16)
        trail_row(g).start()
        return 0


    def total_of(buffer, t, count):
        acc = buffer[t, 0].astype(F32)
        for j in range(1, count):
            acc = acc + buffer[t, j].astype(F32)
        return acc.astype(BF16)

    if len(row_rounds) > 3:
        pl.semaphore_wait(row_known.at[3], 2)

    @pl.when(my_p < owners)
    def _():
        for t in range(PARTS):
            p_in[t, my_p] = plane_buf[t, my_p]
            stage_of(p_in, t, n_plane - 1, ps, pr).wait_recv()
            z_out[t] = total_of(p_in, t, n_plane)
            loop_z(lambda z: along_z(t, z).start())
            z_in[t, my_z] = z_out[t]

    lax.fori_loop(0, CHUNKS, output_step, 0)
    for copy in trail:
        copy.start()

    @pl.when(my_p < owners)
    def _():
        for t in range(PARTS):
            stage_of(z_in, t, n_z - 1, zs, zr).wait_recv()
            half_buf[t, my_p] = total_of(z_in, t, n_z)
            loop_plane(lambda p: spread(t, p).start())

    for g in range(CHUNKS):
        trail_row(g).wait_recv()
    for copy in trail:
        copy.wait_recv()
    for i, (src, dst) in enumerate(((field, res), (cfield, gin))):
        half = slice(i * WIN, i * WIN + WIN)
        ends = jnp.where(
            upper((WIN, EDGE)), rdiag[half, :].astype(F32), rcol[half, :].astype(F32))
        dst[:, :EDGE] = ends.astype(BF16)
        for g in range(CHUNKS):
            start = EDGE + g * CHUNK
            size = min(CHUNK, LANES - start)
            whole = merge_rows(rrow[g, half, :].astype(F32), src[:, start : start + CHUNK])
            dst[:, start : start + size] = whole[:, :size].astype(BF16)

    def lanes_of(first, t):
        return pl.ds(pl.multiple_of(first * MID + t * 128, 128), 128)

    flat = (owners * rows_each, 128)
    for t in range(PARTS):
        from_all_owners(lambda count: stage_of(half_buf, t, count, as_sem, ar_sem).wait_recv())
        back(t).start()
        total_out[:, lanes_of(core, t)] = half_buf[t].astype(F32).reshape(flat) * grad_scale
    for t in range(PARTS):
        back(t).wait_recv()
        total_out[:, lanes_of(1 - core, t)] = last_in[t].astype(F32).reshape(flat) * grad_scale

    for g in range(CHUNKS):
        lead_row(g).wait_send()
        trail_row(g).wait_send()
    for copy in lead + trail + (swap,):
        copy.wait_send()
    for t in range(PARTS):
        back(t).wait_send()
        from_all_owners(lambda count: stage_of(plane_buf, t, count, ps, pr).wait_send())

        @pl.when(my_p < owners)
        def _():
            stage_of(z_in, t, n_z - 1, zs, zr).wait_send()
            stage_of(p_in, t, n_plane - 1, as_sem, ar_sem).wait_send()


def finish_kernel(res, gin, total, *refs):
    outs, (b0, b1, w0, w1, v0, v1, v2, t0, sems) = refs[:9], refs[9:]
    staged = (res, gin, w0, b0, w1, v0, v1, v2, t0)
    copies = [
        pltpu.make_async_copy(src, dst, sems.at[i]) for i, (src, dst) in enumerate(zip(staged, outs))
    ]
    for copy in copies[:2]:
        copy.start()
    w0[...] = total[0:WIDTH, : 3 * WIDTH]
    copies[2].start()
    w1[...] = total[0:WIDTH, 3 * WIDTH :]
    copies[4].start()
    b0[...] = total[WIDTH : WIDTH + 1, : 3 * WIDTH].reshape(3 * WIDTH)
    v0[...] = total[WIDTH : WIDTH + 1, 3 * WIDTH :].reshape(WIDTH)
    v1[...] = total[WIDTH + 1 : WIDTH + 2, :WIDTH].reshape(WIDTH)
    v2[...] = total[WIDTH + 1 : WIDTH + 2, WIDTH : 2 * WIDTH].reshape(WIDTH)
    t0[...] = total[WIDTH + 2 : WIDTH + 2 + HEADS, :RELS]
    for i in (3, 5, 6, 7, 8):
        copies[i].start()
    for copy in copies:
        copy.wait()


def shards(image, cotangent, qkv_weight, qkv_bias, proj_weight, proj_bias, norm_gain, norm_bias,
           bias_table):
    n_row, n_col = lax.axis_size("row"), lax.axis_size("col")
    spp = -(-STRIPES // n_col)
    owners = -(-STRIPES // spp)
    rows_each = spp * 16
    factor = float(n_row * n_col * TOKENS_HERE) ** (-0.5)
    args = (image, cotangent, qkv_weight, qkv_bias, proj_weight, proj_bias, norm_gain, norm_bias,
            bias_table)
    tile = jax.ShapeDtypeStruct(image.shape, BF16)
    vmem = pl.BlockSpec(memory_space=pltpu.VMEM)
    hbm = pl.BlockSpec(memory_space=pltpu.HBM)
    dma = pltpu.SemaphoreType.DMA
    row_halo = pltpu.VMEM((CHUNKS, 16, HALF), BF16)
    col_halo = pltpu.VMEM((16, EDGE), BF16)
    half = (owners * rows_each, MID)
    stripe = (rows_each, 128)
    halves = (PARTS, owners) + stripe
    parts = pl.pallas_call(
        functools.partial(block_kernel, n_row, n_col, spp, factor),
        out_shape=(tile, tile, jax.ShapeDtypeStruct((owners * rows_each, WIDE), F32)),
        in_specs=[hbm] * 9,
        out_specs=(vmem,) * 3,
        scratch_shapes=[pltpu.VMEM(a.shape, a.dtype) for a in args]
        + [row_halo, col_halo, row_halo, col_halo, col_halo] * 2
        + [
            pltpu.VMEM((WIN, LANES + EDGE), F32), pltpu.VMEM((WIN, LANES + EDGE), F32),
            pltpu.VMEM((2, WIN, EDGE), F32),
            pltpu.VMEM((3, WIDTH, WIDTH), BF16),
            pltpu.VMEM((TOKENS_HERE, WIDTH), F32),
            pltpu.VMEM((TOKENS_HERE, WIDTH), F32),
            pltpu.VMEM((TOKENS_HERE, WIDTH), F32),
            pltpu.VMEM((4, TOKENS_HERE, WIDTH), BF16),
            pltpu.VMEM((TOKENS_HERE, WIDTH), BF16),
            pltpu.VMEM((TOKENS_HERE, WIDTH), BF16),
            pltpu.VMEM((6, WIN, WIDTH), F32),
            pltpu.VMEM((CELLS, HEADS * CELLS), F32),
            pltpu.VMEM((2, CELLS, HEADS * CELLS), F32),
            pltpu.VMEM((WIN, 256, 128), BF16),
            pltpu.VMEM((8, 256), F32),
            pltpu.VMEM((HEADS, WIN, 128), F32),
            pltpu.VMEM((owners * rows_each, WIDE), F32),
            pltpu.VMEM(half, BF16), pltpu.VMEM(half, BF16),
            pltpu.VMEM(halves, BF16), pltpu.VMEM((PARTS, n_col) + stripe, BF16),
            pltpu.VMEM((PARTS,) + stripe, BF16), pltpu.VMEM((PARTS, n_row // 2) + stripe, BF16),
            pltpu.VMEM(halves, BF16), pltpu.VMEM(halves, BF16),
            dma((9,)), dma((2 * CHUNKS + 4,)), dma((2 * CHUNKS + 4,)), dma((1 + PARTS,)),
            dma((1 + PARTS,)), dma((PARTS,)), dma((PARTS,)), dma((PARTS,)), dma((PARTS,)),
            dma((PARTS,)), dma((PARTS,)),
            pltpu.SemaphoreType.REGULAR((4,)), pltpu.SemaphoreType.REGULAR((4,)),
            pltpu.SemaphoreType.REGULAR,
        ],
        compiler_params=pltpu.CompilerParams(
            collective_id=1, has_side_effects=True, vmem_limit_bytes=60 * 1024 * 1024),
    )(*args)
    shapes = (image, cotangent, (WIDTH, 3 * WIDTH), (3 * WIDTH,), (WIDTH, WIDTH), (WIDTH,),
              (WIDTH,), (WIDTH,), (HEADS, RELS))
    outs = (tile, tile) + tuple(jax.ShapeDtypeStruct(s, F32) for s in shapes[2:])
    stage = [shapes[3], (1,), shapes[2], shapes[4], shapes[5], shapes[6], shapes[7], shapes[8]]
    return pl.pallas_call(
        finish_kernel,
        out_shape=outs,
        in_specs=[vmem] * 3,
        out_specs=(hbm,) * 9,
        scratch_shapes=[pltpu.VMEM(s, F32) for s in stage] + [dma((9,))],
        compiler_params=pltpu.CompilerParams(vmem_limit_bytes=60 * 1024 * 1024),
    )(*parts)


def solution(mesh):
    in_specs = (P("row", "col"), P("row", "col"), P(), P(), P(), P(), P(), P(), P())
    out_specs = (P("row", "col"), P("row", "col"), P(), P(), P(), P(), P(), P(), P())
    return jax.shard_map(shards, mesh=mesh, in_specs=in_specs, out_specs=out_specs, check_vma=False)
```

```python
import functools

import jax
import jax.numpy as jnp
from jax import lax
from jax.experimental import pallas as pl
from jax.experimental.pallas import tpu as pltpu
from jax.sharding import PartitionSpec as P

WIDTH = 192
HEADS = 6
HEAD_DIM = 32
WIN = 8
CELLS = WIN * WIN
SHIFT = 4
RELS = 225
EPS = 1e-05
NEG = -1e30
TILE_COLS = 64
LANES = TILE_COLS * WIDTH
EDGE = SHIFT * WIDTH
WINDOWS = TILE_COLS // WIN
SPAN = WIN * WIDTH
TOKENS_HERE = WINDOWS * CELLS
CHUNKS = 4
LOOSE = False
PER_CHUNK = WINDOWS // CHUNKS
CHUNK_TOKENS = PER_CHUNK * CELLS
CHUNK = PER_CHUNK * SPAN
HALF = CHUNK // 2
SCALE = HEAD_DIM**-0.5
GROUPS = ((0, 4), (4, 2))
STRIPES = 13
WIDE = 4 * WIDTH
MID = WIDE // 2
PARTS = MID // 128

MESH = pl.DeviceIdType.MESH
F32 = jnp.float32
BF16 = jnp.bfloat16


def dot(a, b, ca=1, cb=0):
    return lax.dot_general(a, b, (((ca,), (cb,)), ((), ())), preferred_element_type=F32)


def iota(shape, dim):
    return lax.broadcasted_iota(jnp.int32, shape, dim)


def upper(shape):
    return iota(shape, 0) < SHIFT


def pack_rows(field):
    back = pltpu.roll(field[:, HALF:], SHIFT, 0)
    return jnp.where(upper((WIN, HALF)), field[:, :HALF], back)


def merge_rows(packed, field):
    low = jnp.where(upper((WIN, HALF)), packed, field[:, :HALF])
    high = jnp.where(upper((WIN, HALF)), pltpu.roll(packed, SHIFT, 0), field[:, HALF:])
    return jnp.concatenate([low, high], 1)


def split_tokens(strip):
    left = iota((WIN, 128), 1) < 64
    first, second = [], []
    for j in range(WIN // 2):
        v = [strip[:, (3 * j + i) * 128 : (3 * j + i + 1) * 128] for i in range(3)]
        r1, r2 = pltpu.roll(v[1], 64, 1), pltpu.roll(v[2], 64, 1)
        first += [v[0], jnp.where(left, r1, r2)]
        second += [v[1], r2]
    return jnp.concatenate(first, 0), jnp.concatenate(second, 0)


def join_tokens(first, second):
    left = iota((WIN, 128), 1) < 64
    out = []
    for j in range(WIN // 2):
        e = slice(16 * j, 16 * j + 8)
        o = slice(16 * j + 8, 16 * j + 16)
        swapped = pltpu.roll(first[o], 64, 1)
        out.append(first[e])
        out.append(jnp.where(left, second[e], swapped))
        out.append(jnp.where(left, swapped, pltpu.roll(second[o], 64, 1)))
    return jnp.concatenate(out, 1)


def build_bias(table_ref, onehot, padded, diag, bias, last_row, last_col):
    padded[...] = jnp.zeros((8, 256), F32)
    padded[0:HEADS, 0:RELS] = table_ref[...]
    table = padded[...]
    hi = table.astype(BF16)
    rest = table - hi.astype(F32)
    mid = rest.astype(BF16)
    low = (rest - mid.astype(F32)).astype(BF16)
    lane = iota((1, 128), 1)
    a_q = (lane + SHIFT) % WIN
    for a in range(WIN):
        target = (a_q - (a + SHIFT) % WIN + WIN - 1) * (2 * WIN - 1) + lane // WIN
        target = jnp.where(lane < 120, target, -1)
        hot = jnp.where(iota((256, 128), 0) == target, 1.0, 0.0).astype(BF16)
        onehot[a] = hot
        rows = dot(hi, hot) + dot(mid, hot) + dot(low, hot)
        for h in range(HEADS):
            diag[h, a : a + 1, :] = rows[h : h + 1, :]
    sub = iota((WIN, 128), 0)
    lanes = iota((WIN, 128), 1)
    row_cut = jnp.where((sub < SHIFT) != (lanes % WIN < SHIFT), NEG, 0.0) * last_row
    right = lanes % 64 // WIN >= SHIFT
    for b in range(WIN):
        col_cut = jnp.where(right != (b >= SHIFT), NEG, 0.0) * last_col
        for pair in range(HEADS // 2):
            shift = (WIN - 1 - b) * WIN
            even = pltpu.roll(diag[2 * pair], (128 - shift) % 128, 1)
            odd = pltpu.roll(diag[2 * pair + 1], (192 - shift) % 128, 1)
            block = jnp.where(lanes < 64, even, odd) + row_cut
            where = (slice(b * WIN, b * WIN + WIN), slice(pair * 128, pair * 128 + 128))
            bias[(0,) + where] = block
            bias[(1,) + where] = block + col_cut


def table_grad(total, onehot, diag):
    lanes = iota((WIN, 128), 1)
    for h in range(HEADS):
        mine = (lanes < 64) == (h % 2 == 0)
        acc = jnp.zeros((WIN, 128), F32)
        for b in range(WIN):
            block = total[b * WIN : b * WIN + WIN, h // 2 * 128 : h // 2 * 128 + 128]
            block = jnp.where(mine, block, 0.0)
            acc = acc + pltpu.roll(block, ((WIN - 1 - b) * WIN + h % 2 * 64) % 128, 1)
        diag[h] = acc
    flat = jnp.concatenate([diag[h] for h in range(HEADS)], 0)
    hi = flat.astype(BF16)
    low = (flat - hi.astype(F32)).astype(BF16)
    sub = iota((HEADS * WIN, 256), 0) % WIN
    acc = jnp.zeros((HEADS * WIN, 256), F32)
    for a in range(WIN):
        part = dot(hi, onehot[a], 1, 1) + dot(low, onehot[a], 1, 1)
        acc = acc + jnp.where(sub == a, part, 0.0)
    return [
        jnp.sum(acc[h * WIN : h * WIN + WIN], 0, keepdims=True) for h in range(HEADS)
    ]


def masked_heads(x, group):
    start, count = group
    lane = iota((CELLS, count * HEAD_DIM), 1) // HEAD_DIM
    wide = x[:, start * HEAD_DIM : (start + count) * HEAD_DIM]
    zero = jnp.zeros_like(wide)
    return jnp.concatenate([jnp.where(lane == h, wide, zero) for h in range(count)], 0)


def own_heads(x, count):
    lane = iota((CELLS, count * HEAD_DIM), 1) // HEAD_DIM
    out = x[(count - 1) * CELLS : count * CELLS]
    for h in range(count - 1):
        out = jnp.where(lane == h, x[h * CELLS : (h + 1) * CELLS], out)
    return out


def fold(x):
    return jnp.sum(x.reshape(-1, WIN, x.shape[1]), 0)


def window_step(q, k, v, da, bias, gsum):
    att, dq, dk, dv = [], [], [], []
    for start, count in GROUPS:
        ch = slice(start * HEAD_DIM, (start + count) * HEAD_DIM)
        lanes = slice(start * CELLS, (start + count) * CELLS)
        qm = masked_heads(q, (start, count))
        dam = masked_heads(da, (start, count))
        s = dot(k[:, ch], qm, 1, 1) * SCALE + bias[:, lanes]
        e = jnp.exp(s - jnp.max(s, 0, keepdims=True))
        p = e * (1.0 / jnp.sum(e, 0, keepdims=True))
        dp = dot(v[:, ch], dam, 1, 1)
        ds = p * (dp - jnp.sum(p * dp, 0, keepdims=True))
        gsum[:, lanes] += ds
        pb, dsb = p.astype(BF16), ds.astype(BF16)
        dv.append(dot(pb, dam))
        dk.append(dot(dsb, qm) * SCALE)
        att.append(own_heads(dot(pb, v[:, ch], 0, 0), count).astype(BF16))
        dq.append(own_heads(dot(dsb, k[:, ch], 0, 0), count) * SCALE)
    return [jnp.concatenate(parts, 1) for parts in (att, dq, dk, dv)]


def block_kernel(n_row, n_col, spp, grad_scale, *refs):
    (img_h, cot_h, wqkv_h, bqkv_h, wproj_h, bproj_h, gain_h, shift_h, table_h,
     res, gin, total_out,
     img, cot, wqkv, bqkv, wproj, bproj, gain_ref, shift_ref, table_ref,
     irow, icol, hrow, hcol, hdiag, orow, ocol, rrow, rcol, rdiag,
     field, cfield, corner, weights, xs, cs, dh, xd, xhid, xatt, sums, gsum,
     bias, onehot, padded, diag, gs, c_out, c_in, plane_buf, p_in, z_out, z_in, half_buf, last_in,
     ls, hs, hr, cs_sem, cr_sem, ps, pr, zs, zr, as_sem, ar_sem,
     row_known, col_known, pair_known) = refs
    my_r, my_c = lax.axis_index("row"), lax.axis_index("col")
    above, below = lax.rem(my_r + n_row - 1, n_row), lax.rem(my_r + 1, n_row)
    left, right = lax.rem(my_c + n_col - 1, n_col), lax.rem(my_c + 1, n_col)
    n_plane, n_z = n_col, n_row // 2
    core = lax.rem(my_c, 2)
    my_p = my_c // 2 * 2 + lax.rem(my_r, 2)
    my_z = my_r // 2
    owners = -(-STRIPES // spp)
    rows_each = spp * 16

    def plane_peer(p):
        return (my_z * 2 + lax.rem(p, 2), p // 2 * 2 + core)

    def z_peer(z):
        return (z * 2 + lax.rem(my_r, 2), my_c)

    local = [
        pltpu.make_async_copy(src, dst, ls.at[i])
        for i, (src, dst) in enumerate((
            (img_h, img), (cot_h, cot), (wqkv_h, wqkv), (bqkv_h, bqkv), (wproj_h, wproj),
            (bproj_h, bproj), (gain_h, gain_ref), (shift_h, shift_ref), (table_h, table_ref)))
    ]
    for copy in local:
        copy.start()
    barrier = pltpu.get_barrier_semaphore()

    def greet(device):
        pl.semaphore_signal(barrier, inc=1, device_id=device, device_id_type=MESH)

    for device in ((above, my_c), (below, my_c), (my_r, left), (my_r, right), (above, left),
                   (below, right)):
        greet(device)

    rounds = [(g, 2**g) for g in range(4)]
    row_rounds = [(g, d) for g, d in rounds if 4 * d <= n_row]
    col_rounds = [(g, d) for g, d in rounds if 4 * d <= n_col]

    def tell(sem, device):
        pl.semaphore_signal(sem, inc=1, device_id=device, device_id_type=MESH)

    def start_round(g):
        for k, d in row_rounds:
            @pl.when(g == k)
            def _():
                tell(row_known.at[k], (lax.rem(my_r + d, n_row), my_c))
                tell(row_known.at[k], (lax.rem(my_r + n_row - d, n_row), my_c))

        for k, d in col_rounds:
            @pl.when(g == k)
            def _():
                tell(col_known.at[k], (my_r, lax.rem(my_c + d, n_col)))
                tell(col_known.at[k], (my_r, lax.rem(my_c + n_col - d, n_col)))

        @pl.when(g == 3)
        def _():
            tell(pair_known, (my_r + 1 - 2 * lax.rem(my_r, 2), my_c))

    def end_round(g):
        for known, known_rounds in ((row_known, row_rounds), (col_known, col_rounds)):
            for k, _ in known_rounds:
                if k < 3:
                    @pl.when(g == k)
                    def _():
                        pl.semaphore_wait(known.at[k], 2)

    def remote(src, dst, send, recv, device):
        return pltpu.make_async_remote_copy(
            src_ref=src, dst_ref=dst, send_sem=send, recv_sem=recv, device_id=device,
            device_id_type=MESH)

    def halo(src, dst, i, device):
        return remote(src, dst, hs.at[i], hr.at[i], device)

    def lead_row(g):
        return halo(irow.at[g], hrow.at[g], g, (above, my_c))

    def trail_row(g):
        return halo(orow.at[g], rrow.at[g], CHUNKS + g, (below, my_c))

    n = 2 * CHUNKS
    lead = (halo(icol, hcol, n, (my_r, left)), halo(icol, hdiag, n + 1, (above, left)))
    trail = (halo(ocol, rcol, n + 2, (my_r, right)), halo(ocol, rdiag, n + 3, (below, right)))

    local[0].wait()
    local[1].wait()
    pl.semaphore_wait(barrier, 6)
    for g in range(CHUNKS):
        start = EDGE + g * CHUNK
        size = min(CHUNK, LANES - start)
        for i, (src, dst) in enumerate(((img, field), (cot, cfield))):
            half = slice(i * WIN, i * WIN + WIN)
            tile = src[:, start : start + size].astype(F32)
            if size < CHUNK:
                tile = jnp.concatenate([tile, src[:, :EDGE].astype(F32)], 1)
            dst[:, start : start + CHUNK] = tile
            irow[g, half, :] = pack_rows(tile).astype(BF16)
        lead_row(g).start()
    for i, src in enumerate((img, cot)):
        icol[i * WIN : i * WIN + WIN, :] = src[:, :EDGE]
    for copy in lead:
        copy.start()
    start_round(0)

    for copy in local[2:]:
        copy.wait()
    last_row = (my_r == n_row - 1).astype(F32)
    last_col = (my_c == n_col - 1).astype(F32)
    build_bias(table_ref, onehot, padded, diag, bias, last_row, last_col)
    gsum[...] = jnp.zeros_like(gsum)
    sums[...] = jnp.zeros_like(sums)
    corner[...] = jnp.zeros_like(corner)
    gs[WIDTH:, :] = jnp.zeros((owners * rows_each - WIDTH, WIDE), F32)
    for i in range(3):
        weights[i] = wqkv[:, i * WIDTH : (i + 1) * WIDTH]
    qkv_bias = bqkv[...].reshape(1, 3 * WIDTH)
    biases = [qkv_bias[:, i * WIDTH : (i + 1) * WIDTH] for i in range(3)]
    proj_bias = bproj[...].reshape(1, WIDTH)
    gain = gain_ref[...].reshape(1, WIDTH)
    shift = shift_ref[...].reshape(1, WIDTH)

    def chunk_step(g, _):
        final = g == CHUNKS - 1
        lanes = pl.ds(pl.multiple_of(EDGE + g * CHUNK, 128), CHUNK)
        rows = pl.ds(pl.multiple_of(g * CHUNK_TOKENS, CHUNK_TOKENS), CHUNK_TOKENS)
        lead_row(g).wait_recv()

        @pl.when(final)
        def _():
            for copy in lead:
                copy.wait_recv()
            for i in range(2):
                half = slice(i * WIN, i * WIN + WIN)
                corner[i] = jnp.where(
                    upper((WIN, EDGE)), hdiag[half, :].astype(F32), hcol[half, :].astype(F32))

        tokens = []
        for i, src in enumerate((field, cfield)):
            half = slice(i * WIN, i * WIN + WIN)
            whole = merge_rows(hrow[g, half, :].astype(F32), src[:, lanes])
            end = jnp.where(final, corner[i], whole[:, CHUNK - EDGE :])
            whole = jnp.concatenate([whole[:, : CHUNK - EDGE], end], 1)
            parts = [split_tokens(whole[:, j * SPAN : (j + 1) * SPAN]) for j in range(PER_CHUNK)]
            first = jnp.concatenate([part[0] for part in parts], 0)
            second = jnp.concatenate([part[1] for part in parts], 0)
            tokens.append(jnp.concatenate([first, second[:, : WIDTH - 128]], 1))
        x, cot_f = tokens
        center = x - jnp.mean(x, 1, keepdims=True)
        inv_std = lax.rsqrt(jnp.mean(center * center, 1, keepdims=True) + EPS)
        normed = center * inv_std
        hidden = (normed * gain + shift).astype(BF16)
        xhid[rows, :] = hidden
        q, k, v = [(dot(hidden, weights[i]) + biases[i]).astype(BF16) for i in range(3)]
        cot_b = cot_f.astype(BF16)
        da = dot(cot_b, wproj[...], 1, 1).astype(BF16)
        found = []
        for j in range(PER_CHUNK):
            r = slice(j * CELLS, (j + 1) * CELLS)
            if j == PER_CHUNK - 1:
                add = bias.at[final.astype(jnp.int32)]
            else:
                add = bias.at[0]
            found.append(window_step(q[r], k[r], v[r], da[r], add, gsum))
        att, dq, dk, dv = [jnp.concatenate([part[i] for part in found], 0) for i in range(4)]
        xatt[rows, :] = att
        xs[rows, :] = x
        cs[rows, :] = cot_f
        d_hidden = jnp.zeros((CHUNK_TOKENS, WIDTH), F32)
        for i, part in enumerate((dq, dk, dv)):
            part_b = part.astype(BF16)
            xd[i, rows, :] = part_b
            sums[i] += fold(part)
            d_hidden = d_hidden + dot(part_b, weights[i], 1, 1)
        xd[3, rows, :] = cot_b
        sums[3] += fold(cot_f)
        sums[4] += fold(d_hidden * normed)
        sums[5] += fold(d_hidden)
        dh[rows, :] = d_hidden
        end_round(g + 1)
        start_round(g + 2)
        return 0

    end_round(0)
    start_round(1)
    lax.fori_loop(0, CHUNKS, chunk_step, 0)

    hidden_t = xhid[...].T
    for i in range(3):
        gs[0:WIDTH, i * WIDTH : (i + 1) * WIDTH] = dot(hidden_t, xd[i])
    gs[0:WIDTH, 3 * WIDTH :] = dot(xatt[...], xd[3], 0, 0)
    for i in range(4):
        gs[WIDTH : WIDTH + 1, i * WIDTH : (i + 1) * WIDTH] = jnp.sum(sums[i], 0, keepdims=True)
    for i in range(2):
        gs[WIDTH + 1 : WIDTH + 2, i * WIDTH : (i + 1) * WIDTH] = jnp.sum(
            sums[4 + i], 0, keepdims=True)
    for h, line in enumerate(table_grad(gsum[...], onehot, diag)):
        gs[WIDTH + 2 + h : WIDTH + 3 + h, 0:256] = line

    partner = (my_r, my_c + 1 - 2 * core)

    def lanes_of(first, t):
        return pl.ds(pl.multiple_of(first * MID + t * 128, 128), 128)

    swaps = [remote(c_out.at[t], c_in.at[t], cs_sem.at[PARTS + t], cr_sem.at[PARTS + t], partner)
             for t in range(PARTS)]
    for t in range(PARTS):
        c_out[t] = gs[:, lanes_of(1 - core, t)].astype(BF16)
        swaps[t].start()

    def loop_group(me, count, step):
        def one(k, _):
            step(lax.rem(me + k, count))
            return 0

        lax.fori_loop(1, count, one, 0, unroll=LOOSE)

    def loop_plane(step):
        loop_group(my_p, n_plane, step)

    def loop_z(step):
        loop_group(my_z, n_z, step)

    def stage_of(buffer, t, count, send, recv):
        part = buffer.at[t, pl.ds(0, count)]
        return remote(part, part, send.at[t], recv.at[t], partner)

    def from_all_owners(step):
        @pl.when(my_p < owners)
        def _():
            step(owners - 1)

        @pl.when(my_p >= owners)
        def _():
            step(owners)

    def scatter(t, p):
        return remote(plane_buf.at[t, p], p_in.at[t, my_p], ps.at[t], pr.at[t], plane_peer(p))

    def along_z(t, z):
        return remote(z_out.at[t], z_in.at[t, my_z], zs.at[t], zr.at[t], z_peer(z))

    def spread(t, p):
        return remote(half_buf.at[t, my_p], half_buf.at[t, my_p], as_sem.at[t], ar_sem.at[t],
                      plane_peer(p))

    def back(t):
        return remote(half_buf.at[t], last_in.at[t], cs_sem.at[t], cr_sem.at[t], partner)

    def send_scatter(t):
        def one(p):
            @pl.when(p < owners)
            def _():
                scatter(t, p).start()

        loop_plane(one)

    pl.semaphore_wait(pair_known, 1)
    for t in range(PARTS):
        swaps[t].wait_recv()
        part = (gs[:, lanes_of(core, t)] + c_in[t].astype(F32)).astype(BF16)
        plane_buf[t] = part.reshape(owners, rows_each, 128)
        send_scatter(t)

    def output_step(g, _):
        lanes = pl.ds(pl.multiple_of(EDGE + g * CHUNK, 128), CHUNK)
        rows = pl.ds(pl.multiple_of(g * CHUNK_TOKENS, CHUNK_TOKENS), CHUNK_TOKENS)
        x, cot_f, d_hidden = xs[rows, :], cs[rows, :], dh[rows, :]
        center = x - jnp.mean(x, 1, keepdims=True)
        inv_std = lax.rsqrt(jnp.mean(center * center, 1, keepdims=True) + EPS)
        normed = center * inv_std
        out = x + dot(xatt[rows, :], wproj[...]) + proj_bias
        d_normed = d_hidden * gain
        d_tokens = cot_f + inv_std * (
            d_normed
            - jnp.mean(d_normed, 1, keepdims=True)
            - normed * jnp.mean(d_normed * normed, 1, keepdims=True))
        for i, (value, dst) in enumerate(((out, field), (d_tokens, cfield))):
            half = slice(i * WIN, i * WIN + WIN)
            first = value[:, :128]
            second = jnp.concatenate(
                [value[:, 128:], jnp.zeros((CHUNK_TOKENS, 256 - WIDTH), F32)], 1)
            strips = []
            for j in range(PER_CHUNK):
                r = slice(j * CELLS, (j + 1) * CELLS)
                strips.append(join_tokens(first[r], second[r]))
            whole = jnp.concatenate(strips, 1)
            dst[:, lanes] = whole
            orow[g, half, :] = pack_rows(whole).astype(BF16)
            ocol[half, :] = whole[:, CHUNK - EDGE :].astype(BF16)
        trail_row(g).start()
        return 0


    def total_of(buffer, t, count):
        acc = buffer[t, 0].astype(F32)
        for j in range(1, count):
            acc = acc + buffer[t, j].astype(F32)
        return acc.astype(BF16)

    if len(row_rounds) > 3:
        pl.semaphore_wait(row_known.at[3], 2)

    @pl.when(my_p < owners)
    def _():
        for t in range(PARTS):
            p_in[t, my_p] = plane_buf[t, my_p]
            stage_of(p_in, t, n_plane - 1, ps, pr).wait_recv()
            z_out[t] = total_of(p_in, t, n_plane)
            loop_z(lambda z: along_z(t, z).start())
            z_in[t, my_z] = z_out[t]

    lax.fori_loop(0, CHUNKS, output_step, 0)
    for copy in trail:
        copy.start()

    @pl.when(my_p < owners)
    def _():
        for t in range(PARTS):
            stage_of(z_in, t, n_z - 1, zs, zr).wait_recv()
            half_buf[t, my_p] = total_of(z_in, t, n_z)
            loop_plane(lambda p: spread(t, p).start())

    for g in range(CHUNKS):
        trail_row(g).wait_recv()
    for copy in trail:
        copy.wait_recv()
    for i, (src, dst) in enumerate(((field, res), (cfield, gin))):
        half = slice(i * WIN, i * WIN + WIN)
        ends = jnp.where(
            upper((WIN, EDGE)), rdiag[half, :].astype(F32), rcol[half, :].astype(F32))
        dst[:, :EDGE] = ends.astype(BF16)
        for g in range(CHUNKS):
            start = EDGE + g * CHUNK
            size = min(CHUNK, LANES - start)
            whole = merge_rows(rrow[g, half, :].astype(F32), src[:, start : start + CHUNK])
            dst[:, start : start + size] = whole[:, :size].astype(BF16)

    flat = (owners * rows_each, 128)
    for t in range(PARTS):
        from_all_owners(lambda count: stage_of(half_buf, t, count, as_sem, ar_sem).wait_recv())
        back(t).start()
        total_out[:, lanes_of(core, t)] = half_buf[t].astype(F32).reshape(flat) * grad_scale
    for t in range(PARTS):
        back(t).wait_recv()
        total_out[:, lanes_of(1 - core, t)] = last_in[t].astype(F32).reshape(flat) * grad_scale

    for g in range(CHUNKS):
        lead_row(g).wait_send()
        trail_row(g).wait_send()
    for copy in lead + trail + tuple(swaps):
        copy.wait_send()
    for t in range(PARTS):
        back(t).wait_send()
        from_all_owners(lambda count: stage_of(plane_buf, t, count, ps, pr).wait_send())

        @pl.when(my_p < owners)
        def _():
            stage_of(z_in, t, n_z - 1, zs, zr).wait_send()
            stage_of(p_in, t, n_plane - 1, as_sem, ar_sem).wait_send()


def finish_kernel(res, gin, total, *refs):
    outs, (b0, b1, w0, w1, v0, v1, v2, t0, sems) = refs[:9], refs[9:]
    staged = (res, gin, w0, b0, w1, v0, v1, v2, t0)
    copies = [
        pltpu.make_async_copy(src, dst, sems.at[i]) for i, (src, dst) in enumerate(zip(staged, outs))
    ]
    for copy in copies[:2]:
        copy.start()
    w0[...] = total[0:WIDTH, : 3 * WIDTH]
    copies[2].start()
    w1[...] = total[0:WIDTH, 3 * WIDTH :]
    copies[4].start()
    b0[...] = total[WIDTH : WIDTH + 1, : 3 * WIDTH].reshape(3 * WIDTH)
    v0[...] = total[WIDTH : WIDTH + 1, 3 * WIDTH :].reshape(WIDTH)
    v1[...] = total[WIDTH + 1 : WIDTH + 2, :WIDTH].reshape(WIDTH)
    v2[...] = total[WIDTH + 1 : WIDTH + 2, WIDTH : 2 * WIDTH].reshape(WIDTH)
    t0[...] = total[WIDTH + 2 : WIDTH + 2 + HEADS, :RELS]
    for i in (3, 5, 6, 7, 8):
        copies[i].start()
    for copy in copies:
        copy.wait()


def shards(image, cotangent, qkv_weight, qkv_bias, proj_weight, proj_bias, norm_gain, norm_bias,
           bias_table):
    n_row, n_col = lax.axis_size("row"), lax.axis_size("col")
    spp = -(-STRIPES // n_col)
    owners = -(-STRIPES // spp)
    rows_each = spp * 16
    factor = float(n_row * n_col * TOKENS_HERE) ** (-0.5)
    args = (image, cotangent, qkv_weight, qkv_bias, proj_weight, proj_bias, norm_gain, norm_bias,
            bias_table)
    tile = jax.ShapeDtypeStruct(image.shape, BF16)
    vmem = pl.BlockSpec(memory_space=pltpu.VMEM)
    hbm = pl.BlockSpec(memory_space=pltpu.HBM)
    dma = pltpu.SemaphoreType.DMA
    row_halo = pltpu.VMEM((CHUNKS, 16, HALF), BF16)
    col_halo = pltpu.VMEM((16, EDGE), BF16)
    half = (PARTS, owners * rows_each, 128)
    stripe = (rows_each, 128)
    halves = (PARTS, owners) + stripe
    parts = pl.pallas_call(
        functools.partial(block_kernel, n_row, n_col, spp, factor),
        out_shape=(tile, tile, jax.ShapeDtypeStruct((owners * rows_each, WIDE), F32)),
        in_specs=[hbm] * 9,
        out_specs=(vmem,) * 3,
        scratch_shapes=[pltpu.VMEM(a.shape, a.dtype) for a in args]
        + [row_halo, col_halo, row_halo, col_halo, col_halo] * 2
        + [
            pltpu.VMEM((WIN, LANES + EDGE), F32), pltpu.VMEM((WIN, LANES + EDGE), F32),
            pltpu.VMEM((2, WIN, EDGE), F32),
            pltpu.VMEM((3, WIDTH, WIDTH), BF16),
            pltpu.VMEM((TOKENS_HERE, WIDTH), F32),
            pltpu.VMEM((TOKENS_HERE, WIDTH), F32),
            pltpu.VMEM((TOKENS_HERE, WIDTH), F32),
            pltpu.VMEM((4, TOKENS_HERE, WIDTH), BF16),
            pltpu.VMEM((TOKENS_HERE, WIDTH), BF16),
            pltpu.VMEM((TOKENS_HERE, WIDTH), BF16),
            pltpu.VMEM((6, WIN, WIDTH), F32),
            pltpu.VMEM((CELLS, HEADS * CELLS), F32),
            pltpu.VMEM((2, CELLS, HEADS * CELLS), F32),
            pltpu.VMEM((WIN, 256, 128), BF16),
            pltpu.VMEM((8, 256), F32),
            pltpu.VMEM((HEADS, WIN, 128), F32),
            pltpu.VMEM((owners * rows_each, WIDE), F32),
            pltpu.VMEM(half, BF16), pltpu.VMEM(half, BF16),
            pltpu.VMEM(halves, BF16), pltpu.VMEM((PARTS, n_col) + stripe, BF16),
            pltpu.VMEM((PARTS,) + stripe, BF16), pltpu.VMEM((PARTS, n_row // 2) + stripe, BF16),
            pltpu.VMEM(halves, BF16), pltpu.VMEM(halves, BF16),
            dma((9,)), dma((2 * CHUNKS + 4,)), dma((2 * CHUNKS + 4,)), dma((2 * PARTS,)),
            dma((2 * PARTS,)), dma((PARTS,)), dma((PARTS,)), dma((PARTS,)), dma((PARTS,)),
            dma((PARTS,)), dma((PARTS,)),
            pltpu.SemaphoreType.REGULAR((4,)), pltpu.SemaphoreType.REGULAR((4,)),
            pltpu.SemaphoreType.REGULAR,
        ],
        compiler_params=pltpu.CompilerParams(
            collective_id=1, has_side_effects=True, vmem_limit_bytes=60 * 1024 * 1024),
    )(*args)
    shapes = (image, cotangent, (WIDTH, 3 * WIDTH), (3 * WIDTH,), (WIDTH, WIDTH), (WIDTH,),
              (WIDTH,), (WIDTH,), (HEADS, RELS))
    outs = (tile, tile) + tuple(jax.ShapeDtypeStruct(s, F32) for s in shapes[2:])
    stage = [shapes[3], (1,), shapes[2], shapes[4], shapes[5], shapes[6], shapes[7], shapes[8]]
    return pl.pallas_call(
        finish_kernel,
        out_shape=outs,
        in_specs=[vmem] * 3,
        out_specs=(hbm,) * 9,
        scratch_shapes=[pltpu.VMEM(s, F32) for s in stage] + [dma((9,))],
        compiler_params=pltpu.CompilerParams(vmem_limit_bytes=60 * 1024 * 1024),
    )(*parts)


def solution(mesh):
    in_specs = (P("row", "col"), P("row", "col"), P(), P(), P(), P(), P(), P(), P())
    out_specs = (P("row", "col"), P("row", "col"), P(), P(), P(), P(), P(), P(), P())
    return jax.shard_map(shards, mesh=mesh, in_specs=in_specs, out_specs=out_specs, check_vma=False)
```
